128 devices in a mesh: space: 8 (over y_lo, z), vel: 16 (over y_hi, x, core).
Axes of the slice: x: 4, y: 4 (y_hi: 2, y_lo: 2; y = y_hi * 2 + y_lo), z: 4, core: 2. Of those that a mesh axis runs over, the one named last changes fastest.
Arguments:
- dist: float32 [128, 16, 16, 2048], P('space', None, None, 'vel'), may hold values from 0.05 to 2
- relax_rate: float32 [128, 16, 16], P('space'), may hold values from 0.2 to 0.9
- kinetic_cells: int32 [2, 32768], P(None, 'space'), may hold values from 0 to 4095, as said below
- kinetic_count: int32 [2, 8], replicated, may hold values from 1 to 4096, 16384 in all within a row
- map_a: bfloat16 [2048, 768], replicated, may hold values from -0.125 to 0.125
- map_b: bfloat16 [2048, 768], replicated, may hold values from -0.125 to 0.125
- map_c: bfloat16 [768, 2048], replicated, may hold values from -0.21875 to 0.21875
Outputs:
- dist_out: float32 [128, 16, 16, 2048], P('space', None, None, 'vel')
The draws below stay inside these ranges and needn't reach their ends.
Inputs may be any that keep to these rules, and one draw needn't show every extreme that they name: `kinetic_cells`: for each step, the 4096 entries of a slab's block are a permutation of that slab's local cell numbers. `kinetic_count`: each step's counts sum to 16384, and one slab is kinetic in all its cells.
All inputs are finite; a program needn't handle non-finite values.
Results may differ from the reference program's by a relative error of at most 0.0034.
Values may be sent and summed in bfloat16 or wider, within the bound.
No kernel may reach another device: no remote copies, remote signals or barrier semaphores. Data moves between devices by JAX's collectives and lax.ppermute only.
A program may use at most 128 MiB of HBM per device.

```python
import math
import jax
import jax.numpy as jnp
import numpy as np
from jax import lax

GX = 16
GY = 16
GZ = 8
RANK = 768
STEPS = 2
CX = 16
NY = 16
NZ = 16
NV = 2048
NX = 128
KMEAN = 2048
KTOT = 16384
N_SPACE = 8
N_VEL = 16


def draw_kinetic_cells(key, part):
    block_keys = jax.random.split(jax.random.fold_in(key, 17), STEPS * N_SPACE)
    chosen = jax.vmap(lambda one_key: jax.random.permutation(one_key, CX * NY * NZ))(block_keys)
    return chosen.reshape(STEPS, N_SPACE * CX * NY * NZ).astype(jnp.int32)


def levels(key, dims, cuts, least, top_value):
    def one(dim, blocks):
        heights = jax.random.uniform(jax.random.fold_in(jax.random.fold_in(key, 6), dim), (blocks,), jnp.float32, least / len(cuts), top_value / len(cuts))
        return jnp.repeat(jnp.exp(heights), dims[dim] // blocks).reshape((-1,) + (1,) * (len(dims) - dim - 1))

    factor_of = one(*cuts[0])
    for cut in cuts[1:]:
        factor_of = factor_of * one(*cut)
    return factor_of


def profile(number_of, total, most, lean):
    loads = [(1 << 20) // math.isqrt(grade ** lean) + 1 for grade in range(2, number_of + 1)]
    spare, given = total - most - (number_of - 1), [1] * (number_of - 1)
    while spare > 0:
        free = [i for i in range(number_of - 1) if given[i] < most]
        pool, left = sum([loads[i] for i in free]), spare
        for i in free:
            more = min(most - given[i], max(1, left * loads[i] // pool), spare)
            given[i] = given[i] + more
            spare = spare - more
    return np.array([most] + given)


def uneven(rng, number_of, total, bound, slope):
    if number_of == 2:
        one = jax.random.randint(rng, (), max(1, total - bound), min(bound, total - 1) + 1)
        return jnp.stack([one, total - one])
    sizes = jnp.asarray(profile(number_of, total, bound, slope), jnp.int32)
    pairs = (number_of - 1) // 2
    donor, sink = sizes[1:1 + 2 * pairs:2], sizes[2:2 + 2 * pairs:2]
    slack = jnp.minimum(donor - 1, bound - sink)
    moved = jax.random.randint(jax.random.fold_in(rng, 1), (pairs,), 0, 1 << 20) % (slack + 1)
    sizes = sizes.at[1:1 + 2 * pairs:2].set(donor - moved).at[2:2 + 2 * pairs:2].set(sink + moved)
    return sizes[jax.random.permutation(jax.random.fold_in(rng, 2), number_of)]


def centred(key, dims, scale, limit, held_as=jnp.bfloat16):
    result = jax.random.normal(key, dims, jnp.float32) * scale
    return jnp.minimum(jnp.maximum(result, -limit), limit).astype(held_as)


def setup_inputs(seed: int = 0) -> dict:
    key_list = jax.random.split(jax.random.key(seed), 8)
    dist = jnp.clip(jnp.exp(math.log(2.0) - 3.6888794 * jax.random.uniform(key_list[0], (NX, NY, NZ, NV), jnp.float32) ** levels(key_list[0], (NX, NY, NZ, NV), ((0, 8), (3, 16)), -0.2, 0.2)), 0.05, 2.0)
    relax_rate = jnp.clip(0.2 + 0.7 * jax.random.uniform(key_list[1], (NX, NY, NZ), jnp.float32) ** levels(key_list[1], (NX, NY, NZ), ((0, 8),), -0.2, 0.2), 0.2, 0.9)
    kinetic_cells = draw_kinetic_cells(jax.random.fold_in(key_list[7], 71), 0)
    kinetic_count = jax.vmap(lambda own: uneven(own, N_SPACE, KTOT, CX * NY * NZ, 2))(jax.random.split(key_list[3], STEPS)).reshape((STEPS, N_SPACE)).astype(jnp.int32)
    map_a = centred(key_list[4], (NV, RANK), NV ** -0.5, 0.125)
    map_b = centred(key_list[5], (NV, RANK), NV ** -0.5, 0.125)
    map_c = centred(key_list[6], (RANK, NV), RANK ** -0.5, 0.21875)
    return dict(dist=dist, relax_rate=relax_rate, kinetic_cells=kinetic_cells, kinetic_count=kinetic_count, map_a=map_a, map_b=map_b, map_c=map_c)


COURANT = 0.1
SPACING = 0.5
COLLIDE = 0.5


def velocity_tables():
    grid_index = jnp.arange(GX * GY * GZ, dtype=jnp.int32)
    along_x = ((grid_index // (GY * GZ)).astype(jnp.float32) - 0.5 * (GX - 1)) * SPACING
    along_y = (((grid_index // GZ) % GY).astype(jnp.float32) - 0.5 * (GY - 1)) * SPACING
    along_z = ((grid_index % GZ).astype(jnp.float32) - 0.5 * (GZ - 1)) * SPACING
    speed_sq = along_x * along_x + along_y * along_y + along_z * along_z
    weights = jnp.exp(-0.5 * speed_sq)
    weights = weights / jnp.sum(weights)
    moment_basis = jnp.stack([jnp.ones_like(along_x), along_x, along_y, along_z, speed_sq])
    consts = (jnp.sum(weights * along_x * along_x), jnp.sum(weights * along_y * along_y),
              jnp.sum(weights * along_z * along_z), jnp.sum(weights * speed_sq),
              jnp.sum(weights * speed_sq * speed_sq))
    return moment_basis, moment_basis * weights[None, :], consts


def coefficients(moments, consts):
    thermal = (moments[4] - consts[3] * moments[0]) / (consts[4] - consts[3] * consts[3])
    return jnp.stack([moments[0] - consts[3] * thermal, moments[1] / consts[0],
                      moments[2] / consts[1], moments[3] / consts[2], thermal])


def limited_slope(first_diff, second_diff):
    return 0.5 * (jnp.sign(first_diff) + jnp.sign(second_diff)) * jnp.minimum(jnp.abs(first_diff), jnp.abs(second_diff))


def face_flux(padded, velocity, direction):
    extent = padded.shape[direction] - 4
    def window(array, offset, amount):
        return lax.slice_in_dim(array, offset, offset + amount, axis=direction)
    diffs = window(padded, 1, extent + 3) - window(padded, 0, extent + 3)
    left_state = window(padded, 1, extent + 1) + 0.5 * limited_slope(window(diffs, 0, extent + 1), window(diffs, 1, extent + 1))
    right_state = window(padded, 2, extent + 1) - 0.5 * limited_slope(window(diffs, 1, extent + 1), window(diffs, 2, extent + 1))
    fluxes = jnp.maximum(velocity, 0.0) * left_state + jnp.minimum(velocity, 0.0) * right_state
    return window(fluxes, 1, extent) - window(fluxes, 0, extent)


def periodic_pad(current, direction):
    extent = current.shape[direction]
    return jnp.concatenate([lax.slice_in_dim(current, extent - 2, extent, axis=direction), current,
                            lax.slice_in_dim(current, 0, 2, axis=direction)], axis=direction)


def transport(padded, current, speed_x, speed_y, speed_z):
    change = face_flux(padded, speed_x, 0) + face_flux(periodic_pad(current, 1), speed_y, 1)
    change = change + face_flux(periodic_pad(current, 2), speed_z, 2)
    return current - COURANT * change


def collide(row_block, map_a, map_b, map_c):
    first_map = jnp.dot(row_block, map_a, preferred_element_type=jnp.float32)
    second_map = jnp.dot(row_block, map_b, preferred_element_type=jnp.float32)
    hidden = (first_map * second_map).astype(jnp.bfloat16)
    return jnp.dot(hidden, map_c, preferred_element_type=jnp.float32).astype(jnp.bfloat16)


def reference(dist, relax_rate, kinetic_cells, kinetic_count, map_a, map_b, map_c):
    vel_width = NV // N_VEL
    moment_basis, weighted, consts = velocity_tables()
    cell_total = NX * NY * NZ
    slab_cells = cell_total // N_SPACE
    current = jnp.moveaxis(dist.reshape(NX, NY, NZ, N_VEL, vel_width), 3, 0)
    speeds = moment_basis[1:4].reshape(3, N_VEL, vel_width)
    grouped_basis = moment_basis.reshape(5, N_VEL, vel_width)
    grouped_weighted = weighted.reshape(5, N_VEL, vel_width)
    relax_rows = relax_rate.reshape(1, cell_total, 1)
    for step_index in range(STEPS):
        advected = lax.map(lambda member: transport(periodic_pad(member[0], 0), member[0], member[1], member[2], member[3]),
                           (current, speeds[0], speeds[1], speeds[2]))
        flat_rows = advected.reshape(N_VEL, cell_total, vel_width)
        moments = jnp.einsum("mgv,gcv->mc", grouped_basis, flat_rows, precision=lax.Precision.HIGHEST)
        coeffs = coefficients(moments, consts)
        equilibrium = jnp.einsum("mc,mgv->gcv", coeffs, grouped_weighted, precision=lax.Precision.HIGHEST)
        relaxed = flat_rows + relax_rows * (equilibrium - flat_rows)
        slab_counts = kinetic_count[step_index].astype(jnp.int32)
        slab_ends = jnp.cumsum(slab_counts).astype(jnp.int32)
        slab_starts = slab_ends - slab_counts
        global_slot = jnp.arange(KTOT, dtype=jnp.int32)
        owner_slab = jnp.sum((slab_ends[None, :] <= global_slot[:, None]).astype(jnp.int32), axis=1).astype(jnp.int32)
        position = global_slot - slab_starts[owner_slab]
        local_cell = kinetic_cells[step_index][owner_slab * slab_cells + position]
        global_rows = (owner_slab * slab_cells + local_cell).astype(jnp.int32)
        kin_rows = jnp.moveaxis(flat_rows[:, global_rows, :], 0, 1).reshape(KTOT, NV)
        collided = lax.map(lambda row_block: collide(row_block, map_a, map_b, map_c),
                           kin_rows.astype(jnp.bfloat16).reshape(KTOT // KMEAN, KMEAN, NV)).reshape(KTOT, NV)
        kinetic = kin_rows + COLLIDE * collided.astype(jnp.float32)
        kinetic_grouped = jnp.moveaxis(kinetic.reshape(KTOT, N_VEL, vel_width), 1, 0)
        updated = relaxed.at[:, global_rows, :].set(kinetic_grouped)
        current = updated.reshape(N_VEL, NX, NY, NZ, vel_width)
    return jnp.moveaxis(current, 0, 3).reshape(NX, NY, NZ, NV)
```

```python
import jax
import jax.numpy as jnp
import numpy as np
from jax import lax
from jax.experimental import pallas as pl
from jax.experimental.pallas import tpu as pltpu
from jax.sharding import PartitionSpec as P

GX = 16
GY = 16
GZ = 8
NV = GX * GY * GZ
RANK = 768
COURANT = 0.1
SPACING = 0.5
COLLIDE = 0.5

CX = 16
NY = 16
NZ = 16
LAYER = NY * NZ
WIDTH = 128
GROUPS = NV // WIDTH
OFFSET = 3.0 / 16.0
BX = 4
BY = 4
LINE = BX * NZ
LIMIT = 12 << 20


def tables():
    k = np.arange(NV)
    vx = ((k // (GY * GZ)) - 0.5 * (GX - 1)) * SPACING
    vy = ((k // GZ % GY) - 0.5 * (GY - 1)) * SPACING
    vz = ((k % GZ) - 0.5 * (GZ - 1)) * SPACING
    s = vx * vx + vy * vy + vz * vz
    w = np.exp(-0.5 * s)
    w = w / w.sum()
    sx, sy, sz = (w * vx * vx).sum(), (w * vy * vy).sum(), (w * vz * vz).sum()
    m2, m4 = (w * s).sum(), (w * s * s).sum()
    basis = np.stack([np.ones(NV), vx, vy, vz, s - OFFSET])
    q = np.zeros((5, 5))
    scale = 1.0 / (m4 - m2 * m2)
    thermal = np.zeros(5)
    thermal[0] = (OFFSET - m2) * scale
    thermal[4] = scale
    q[:, 4] = thermal
    q[:, 0] = (OFFSET - m2) * thermal
    q[0, 0] += 1.0
    q[1, 1], q[2, 2], q[3, 3] = 1.0 / sx, 1.0 / sy, 1.0 / sz
    project = np.zeros((NV, 128))
    project[:, :5] = basis.T
    mix = np.zeros((128, 128))
    expand = np.zeros((128, NV))
    for part in range(3):
        mix[:5, 8 * part : 8 * part + 5] = q
        expand[8 * part : 8 * part + 5] = basis
    return (
        project.astype(jnp.bfloat16),
        mix.astype(np.float32),
        expand.astype(jnp.bfloat16),
        w.reshape(1, NV).astype(np.float32),
        (COURANT * np.stack([vy[:WIDTH], vz[:WIDTH]])).astype(np.float32),
    )


def minmod_half(a, b):
    return 0.5 * (jnp.maximum(jnp.minimum(a, b), 0.0) + jnp.minimum(jnp.maximum(a, b), 0.0))


def call(kernel, name, operands, outs, spaces=None, scratch=(), flops=0, limit=8 << 20):
    vmem = pl.BlockSpec(memory_space=pltpu.VMEM)
    smem = pl.BlockSpec(memory_space=pltpu.SMEM)
    scalars = spaces or 0
    moved = sum(o.size * o.dtype.itemsize for o in operands) + sum(
        o.size * o.dtype.itemsize for o in outs
    )
    return pl.pallas_call(
        kernel,
        out_shape=tuple(outs),
        in_specs=[smem] * scalars + [vmem] * (len(operands) - scalars),
        out_specs=tuple(vmem for _ in outs),
        scratch_shapes=list(scratch),
        compiler_params=pltpu.CompilerParams(vmem_limit_bytes=limit),
        cost_estimate=pl.CostEstimate(flops=flops, bytes_accessed=moved, transcendentals=0),
        name=name,
    )(*operands)


def flux_change_z(f, uz, z_up):
    dz = pltpu.roll(f, NZ - 1, 0) - f
    slope = minmod_half(pltpu.roll(dz, 1, 0), dz)
    down = pltpu.roll(f - slope, NZ - 1, 0)
    flux = jnp.where(z_up, f + slope, down)
    return uz * (flux - pltpu.roll(flux, 1, 0))


def edges(before, here, after):
    slope = minmod_half(here - before, after - here)
    return here + slope, here - slope


def upwind_face(before, here, after):
    return here + minmod_half(here - before, after - here)


def first_yz_kernel(f_ref, u_ref, part_ref):
    uy = jnp.broadcast_to(u_ref[0:1], (NZ, WIDTH))
    uz = jnp.broadcast_to(u_ref[1:2], (NZ, WIDTH))
    y_up = uy > 0.0
    z_up = uz > 0.0

    def layer(x, carry):
        def at(y):
            return f_ref[x, y % NY]

        up, _ = edges(at(-2), at(-1), at(0))
        next_up, next_down = edges(at(-1), at(0), at(1))
        flux_before = jnp.where(y_up, up, next_down)
        for y in range(NY):
            up = next_up
            next_up, next_down = edges(at(y), at(y + 1), at(y + 2))
            flux = jnp.where(y_up, up, next_down)
            here = at(y)
            part_ref[x, y] = here - uy * (flux - flux_before) - flux_change_z(here, uz, z_up)
            flux_before = flux
        return carry

    lax.fori_loop(0, CX, layer, 0)


def first_x_kernel(sign_ref, speed_ref, f_ref, part_ref, behind_ref, ahead_ref, rows_ref):
    s = sign_ref[0]
    ux = speed_ref[0]
    forward = s > 0

    def line(y, carry):
        quarter = y // BY
        high = quarter // 2
        core = (quarter + high) % 2
        target = high * (GROUPS // 2) + core
        inner = (y % BY) * NZ

        def at(k):
            if k == -2:
                return behind_ref[jnp.where(forward, 0, 1), y].astype(jnp.float32)
            if k == -1:
                return behind_ref[jnp.where(forward, 1, 0), y].astype(jnp.float32)
            if k == CX:
                return ahead_ref[0, y].astype(jnp.float32)
            return f_ref[jnp.where(forward, k, CX - 1 - k), y]

        face_before = upwind_face(at(-2), at(-1), at(0))
        for k in range(CX):
            x = jnp.where(forward, k, CX - 1 - k)
            face = upwind_face(at(k - 1), at(k), at(k + 1))
            result = part_ref[x, y] - ux * (face - face_before)
            face_before = face
            start = pl.multiple_of((x % BX) * LINE + inner, NZ)
            rows_ref[target + (x // BX) * 2, pl.ds(start, NZ), :] = result.astype(jnp.bfloat16)
        return carry

    lax.fori_loop(0, NY, line, 0)


def collision_terms(
    rows, a_ref, b_ref, c_ref, project_ref, mix_ref, expand_ref, w_ref, hidden_ref
):
    moments = jnp.dot(rows, project_ref[...], preferred_element_type=jnp.float32)
    coeffs = jnp.dot(
        moments, mix_ref[...], precision=lax.Precision.HIGHEST, preferred_element_type=jnp.float32
    )
    lane = lax.broadcasted_iota(jnp.int32, coeffs.shape, 1)
    high = coeffs.astype(jnp.bfloat16).astype(jnp.float32)
    rest = coeffs - high
    middle = rest.astype(jnp.bfloat16).astype(jnp.float32)
    split = jnp.where(lane < 8, high, jnp.where(lane < 16, middle, rest - middle))
    split = split.astype(jnp.bfloat16)
    for n in range(RANK // 256):
        cols = slice(256 * n, 256 * (n + 1))
        first = jnp.dot(rows, a_ref[:, cols], preferred_element_type=jnp.float32)
        second = jnp.dot(rows, b_ref[:, cols], preferred_element_type=jnp.float32)
        hidden_ref[:, cols] = (first * second).astype(jnp.bfloat16)
    hidden = hidden_ref[...]
    for n in range(NV // 256):
        cols = slice(256 * n, 256 * (n + 1))
        collision = jnp.dot(hidden, c_ref[:, cols], preferred_element_type=jnp.float32)
        collision = collision.astype(jnp.bfloat16).astype(jnp.float32)
        poly = jnp.dot(split, expand_ref[:, cols], preferred_element_type=jnp.float32)
        equilibrium = poly * w_ref[:, cols]
        for half in range(2):
            part = slice(WIDTH * half, WIDTH * (half + 1))
            yield 2 * n + half, collision[:, part], equilibrium[:, part]


def first_collide_kernel(
    rows_ref, a_ref, b_ref, c_ref, project_ref, mix_ref, expand_ref, w_ref, rate_ref, mask_ref,
    f_ref, x_up_ref, x_down_ref, y_up_ref, y_down_ref, hidden_ref,
):
    rows = jnp.concatenate([rows_ref[g] for g in range(GROUPS)], axis=1)
    rate = jnp.broadcast_to(rate_ref[...], (LAYER, WIDTH))
    kinetic = jnp.broadcast_to(mask_ref[...], (LAYER, WIDTH)) > 0.0
    half = GROUPS // 2
    for g, collision, equilibrium in collision_terms(
        rows, a_ref, b_ref, c_ref, project_ref, mix_ref, expand_ref, w_ref, hidden_ref
    ):
        moved = rows_ref[g].astype(jnp.float32)
        change = jnp.where(kinetic, COLLIDE * collision, rate * (equilibrium - moved))
        result = moved + change
        f_ref[g] = result
        sent = result.astype(jnp.bfloat16)
        x_up_ref[g] = sent[3 * LINE : 4 * LINE]
        x_down_ref[g] = sent[0:LINE]
        if g >= half:
            x_up_ref[g + half] = sent[2 * LINE : 3 * LINE]
        else:
            x_down_ref[g + GROUPS] = sent[LINE : 2 * LINE]
        for x in range(BX):
            here = slice(NZ * x, NZ * (x + 1))
            y_down_ref[g, here] = sent[LINE * x : LINE * x + NZ]
            y_up_ref[g, here] = sent[LINE * x + 3 * NZ : LINE * x + 4 * NZ]
    low_lane = lax.broadcasted_iota(jnp.int32, (NZ, WIDTH), 1) < WIDTH // 2
    for g in range(half):
        for x in range(BX):
            here = slice(NZ * x, NZ * (x + 1))
            second = slice(LINE * x + NZ, LINE * x + 2 * NZ)
            third = slice(LINE * x + 2 * NZ, LINE * x + 3 * NZ)
            y_up_ref[GROUPS + g, here] = jnp.where(
                low_lane,
                pltpu.roll(f_ref[g, third], WIDTH // 2, 1),
                f_ref[g + half, third],
            ).astype(jnp.bfloat16)
            y_down_ref[GROUPS + g, here] = jnp.where(
                low_lane,
                f_ref[g, second],
                pltpu.roll(f_ref[g + half, second], WIDTH // 2, 1),
            ).astype(jnp.bfloat16)


def second_z_kernel(f_ref, u_ref, part_ref):
    uz = jnp.broadcast_to(u_ref[1:2], (NZ, WIDTH))
    z_up = uz > 0.0

    def group(g, carry):
        for c in range(BX * BY):
            here = slice(NZ * c, NZ * (c + 1))
            f = f_ref[g, here]
            part_ref[g, here] = f - flux_change_z(f, uz, z_up)
        return carry

    lax.fori_loop(0, GROUPS, group, 0)


def second_xy_kernel(
    f_ref, part_ref, x_below_ref, x_above_ref, y_below_ref, y_above_ref, u_ref,
    moved_ref,
):
    uy = jnp.broadcast_to(u_ref[0:1], (NZ, WIDTH))
    y_up = uy > 0.0
    half = GROUPS // 2

    def wide(ref, g, i):
        return ref[g, NZ * i : NZ * (i + 1)].astype(jnp.float32)

    def group(pair, upward):
        g = pair + half if upward else pair
        extra = pair + GROUPS
        ux = (g.astype(jnp.float32) - 0.5 * (GX - 1)) * (SPACING * COURANT)
        ux = ux if upward else -ux
        for y in range(BY):
            behind, ahead = (x_below_ref, x_above_ref) if upward else (x_above_ref, x_below_ref)

            def at_x(k):
                if k == -2:
                    return wide(behind, extra, y)
                if k == -1:
                    return wide(behind, g, y)
                if k == BX:
                    return wide(ahead, g, y)
                x = k if upward else BX - 1 - k
                return f_ref[g, LINE * x + NZ * y : LINE * x + NZ * (y + 1)]

            face_before = upwind_face(at_x(-2), at_x(-1), at_x(0))
            for k in range(BX):
                x = k if upward else BX - 1 - k
                face = upwind_face(at_x(k - 1), at_x(k), at_x(k + 1))
                here = slice(LINE * x + NZ * y, LINE * x + NZ * (y + 1))
                moved_ref[g, here] = part_ref[g, here] - ux * (face - face_before)
                face_before = face
        for x in range(BX):

            def at_y(y):
                if y == -2:
                    below = wide(y_below_ref, extra, x)
                    return below if upward else pltpu.roll(below, WIDTH // 2, 1)
                if y == -1:
                    return wide(y_below_ref, g, x)
                if y == BY:
                    return wide(y_above_ref, g, x)
                if y == BY + 1:
                    above = wide(y_above_ref, extra, x)
                    return pltpu.roll(above, WIDTH // 2, 1) if upward else above
                return f_ref[g, LINE * x + NZ * y : LINE * x + NZ * (y + 1)]

            up, _ = edges(at_y(-2), at_y(-1), at_y(0))
            next_up, next_down = edges(at_y(-1), at_y(0), at_y(1))
            flux_before = jnp.where(y_up, up, next_down)
            for y in range(BY):
                up = next_up
                next_up, next_down = edges(at_y(y), at_y(y + 1), at_y(y + 2))
                flux = jnp.where(y_up, up, next_down)
                here = slice(LINE * x + NZ * y, LINE * x + NZ * (y + 1))
                moved_ref[g, here] = moved_ref[g, here] - uy * (flux - flux_before)
                flux_before = flux

    def downwards(pair, carry):
        group(pair, False)
        return carry

    def upwards(pair, carry):
        group(pair, True)
        return carry

    lax.fori_loop(0, half, downwards, 0)
    lax.fori_loop(0, half, upwards, 0)


def second_collide_kernel(
    moved_ref, a_ref, b_ref, c_ref, project_ref, mix_ref, expand_ref, w_ref, rate_ref, mask_ref,
    out_ref, hidden_ref,
):
    rows = jnp.concatenate([moved_ref[g].astype(jnp.bfloat16) for g in range(GROUPS)], axis=1)
    rate = jnp.broadcast_to(rate_ref[...], (LAYER, WIDTH))
    kinetic = jnp.broadcast_to(mask_ref[...], (LAYER, WIDTH)) > 0.0
    for g, collision, equilibrium in collision_terms(
        rows, a_ref, b_ref, c_ref, project_ref, mix_ref, expand_ref, w_ref, hidden_ref
    ):
        moved = moved_ref[g]
        change = jnp.where(kinetic, COLLIDE * collision, rate * (equilibrium - moved))
        out_ref[g] = (moved + change).astype(jnp.bfloat16)


def place_kernel(in_ref, out_ref):
    for high in range(2):
        for core in range(2):
            quarter = 2 * high + (core ^ high)
            for x in range(BX):
                for y in range(BY):
                    c = LINE * x + NZ * y
                    out_ref[x, BY * quarter + y] = in_ref[high, 0, core, c : c + NZ].astype(
                        jnp.float32
                    )


def place(pieces):
    pieces = pieces.reshape(2, GROUPS // 4, 2, LAYER, WIDTH)
    return pl.pallas_call(
        place_kernel,
        grid=(GROUPS // 4,),
        out_shape=jax.ShapeDtypeStruct((CX, NY, NZ, WIDTH), jnp.float32),
        in_specs=[pl.BlockSpec((2, 1, 2, LAYER, WIDTH), lambda i: (0, i, 0, 0, 0))],
        out_specs=pl.BlockSpec((BX, NY, NZ, WIDTH), lambda i: (i, 0, 0, 0)),
        compiler_params=pltpu.CompilerParams(vmem_limit_bytes=8 << 20),
        cost_estimate=pl.CostEstimate(flops=0, bytes_accessed=3 << 20, transcendentals=0),
        name="place",
    )(pieces)


def device_of(space, high, x, core):
    return (space * 2 + high) * 8 + x * 2 + core


def steps_of(slabs):
    upwind, downwind, x_up, y_up = [], [], [], []
    for space in range(slabs):
        for high in range(2):
            for x in range(4):
                for core in range(2):
                    me = device_of(space, high, x, core)
                    after = device_of((space + 1) % slabs, high, x, core)
                    before = device_of((space - 1) % slabs, high, x, core)
                    upwind.append((me, after if high else before))
                    downwind.append((me, before if high else after))
                    next_slab = (space + (x == 3)) % slabs
                    x_up.append((me, device_of(next_slab, high, (x + 1) % 4, core)))
                    quarter = (2 * high + (core ^ high) + 1) % 4
                    y_up.append(
                        (me, device_of(space, quarter // 2, x, (quarter % 2) ^ (quarter // 2)))
                    )
    back = lambda pairs: [(target, source) for source, target in pairs]
    return upwind, downwind, x_up, back(x_up), y_up, back(y_up)


def body(dist, relax_rate, kinetic_cells, kinetic_count, map_a, map_b, map_c):
    rank_vel = lax.axis_index("vel")
    rank_space = lax.axis_index("space")
    both = ("space", "vel")
    upwind, downwind, x_up, x_down, y_up, y_down = steps_of(lax.axis_size("space"))
    project, mix, expand, w, u = tables()
    consts = (jnp.asarray(project), jnp.asarray(mix), jnp.asarray(expand), jnp.asarray(w))
    maps = (map_a, map_b, map_c)
    u = jnp.asarray(u)
    vx = (rank_vel.astype(jnp.float32) - 0.5 * (GX - 1)) * SPACING
    speed = (COURANT * jnp.abs(vx)).reshape(1)
    forward = rank_vel >= GROUPS // 2
    sign = jnp.where(forward, 1, -1).astype(jnp.int32).reshape(1)

    behind = lax.dynamic_slice_in_dim(dist, jnp.where(forward, CX - 2, 0), 2, 0)
    ahead = lax.dynamic_slice_in_dim(dist, jnp.where(forward, 0, CX - 1), 1, 0)
    behind = lax.ppermute(behind, both, upwind)
    ahead = lax.ppermute(ahead, both, downwind)

    high, x_quarter, core = rank_vel // 8, rank_vel // 2 % 4, rank_vel % 2
    y_quarter = 2 * high + (core + high) % 2
    rate = lax.dynamic_slice(relax_rate, (BX * x_quarter, BY * y_quarter, 0), (BX, BY, NZ))
    rate = rate.reshape(LAYER, 1)
    own = lax.dynamic_index_in_dim(kinetic_count, rank_space, 1, False)
    live = jnp.arange(CX * LAYER, dtype=jnp.int32)[None, :] < own[:, None]
    listed = jnp.where(live, kinetic_cells, -1)
    slot = jnp.arange(LAYER, dtype=jnp.int32)
    cell = (BX * x_quarter + slot // LINE) * LAYER + (BY * y_quarter * NZ + slot % LINE)
    masks = jnp.any(listed[:, None, :] == cell[None, :, None], axis=2, keepdims=True)
    masks = masks.astype(jnp.float32)

    state = jax.ShapeDtypeStruct((CX, NY, NZ, WIDTH), jnp.float32)
    wide = jax.ShapeDtypeStruct((GROUPS, LAYER, WIDTH), jnp.float32)
    narrow = jax.ShapeDtypeStruct((GROUPS, LAYER, WIDTH), jnp.bfloat16)
    halo = jax.ShapeDtypeStruct((GROUPS + GROUPS // 2, LINE, WIDTH), jnp.bfloat16)
    hidden = (pltpu.VMEM((LAYER, RANK), jnp.bfloat16),)

    (part,) = call(first_yz_kernel, "first_yz", (dist, u), (state,), flops=12_000_000)
    (rows,) = call(
        first_x_kernel, "first_x", (sign, speed, dist, part, behind, ahead), (narrow,), 2,
        flops=6_000_000,
    )
    gathered = lax.all_to_all(rows, "vel", split_axis=0, concat_axis=0, tiled=True)
    f, up_x, down_x, up_y, down_y = call(
        first_collide_kernel, "first_collide", (gathered,) + maps + consts + (rate, masks[0]),
        (wide, halo, halo, halo, halo), scratch=hidden, flops=2_500_000_000, limit=LIMIT,
    )
    x_below = lax.ppermute(up_x, both, x_up)
    x_above = lax.ppermute(down_x, both, x_down)
    y_below = lax.ppermute(up_y, both, y_up)
    y_above = lax.ppermute(down_y, both, y_down)
    (part,) = call(second_z_kernel, "second_z", (f, u), (wide,), flops=6_000_000)
    (moved,) = call(
        second_xy_kernel, "second_xy", (f, part, x_below, x_above, y_below, y_above, u), (wide,),
        flops=12_000_000,
    )
    (result,) = call(
        second_collide_kernel, "second_collide", (moved,) + maps + consts + (rate, masks[1]),
        (narrow,), scratch=hidden, flops=2_500_000_000, limit=LIMIT,
    )
    return place(lax.all_to_all(result, "vel", split_axis=0, concat_axis=0, tiled=True))


def solution(mesh):
    return jax.shard_map(
        body,
        mesh=mesh,
        in_specs=(
            P("space", None, None, "vel"),
            P("space", None, None),
            P(None, "space"),
            P(),
            P(),
            P(),
            P(),
        ),
        out_specs=P("space", None, None, "vel"),
        check_vma=False,
    )
```

```python
import jax
import jax.numpy as jnp
import numpy as np
from jax import lax
from jax.experimental import pallas as pl
from jax.experimental.pallas import tpu as pltpu
from jax.sharding import PartitionSpec as P

GX = 16
GY = 16
GZ = 8
NV = GX * GY * GZ
RANK = 768
COURANT = 0.1
SPACING = 0.5
COLLIDE = 0.5

CX = 16
NY = 16
NZ = 16
LAYER = NY * NZ
WIDTH = 128
GROUPS = NV // WIDTH
OFFSET = 3.0 / 16.0
BX = 4
BY = 4
LINE = BX * NZ


def tables():
    k = np.arange(NV)
    vx = ((k // (GY * GZ)) - 0.5 * (GX - 1)) * SPACING
    vy = ((k // GZ % GY) - 0.5 * (GY - 1)) * SPACING
    vz = ((k % GZ) - 0.5 * (GZ - 1)) * SPACING
    s = vx * vx + vy * vy + vz * vz
    w = np.exp(-0.5 * s)
    w = w / w.sum()
    sx, sy, sz = (w * vx * vx).sum(), (w * vy * vy).sum(), (w * vz * vz).sum()
    m2, m4 = (w * s).sum(), (w * s * s).sum()
    basis = np.stack([np.ones(NV), vx, vy, vz, s - OFFSET])
    q = np.zeros((5, 5))
    scale = 1.0 / (m4 - m2 * m2)
    thermal = np.zeros(5)
    thermal[0] = (OFFSET - m2) * scale
    thermal[4] = scale
    q[:, 4] = thermal
    q[:, 0] = (OFFSET - m2) * thermal
    q[0, 0] += 1.0
    q[1, 1], q[2, 2], q[3, 3] = 1.0 / sx, 1.0 / sy, 1.0 / sz
    project = np.zeros((NV, 128))
    project[:, :5] = basis.T
    mix = np.zeros((128, 128))
    expand = np.zeros((128, NV))
    for part in range(3):
        mix[:5, 8 * part : 8 * part + 5] = q
        expand[8 * part : 8 * part + 5] = basis
    return (
        project.astype(jnp.bfloat16),
        mix.astype(np.float32),
        expand.astype(jnp.bfloat16),
        w.reshape(1, NV).astype(np.float32),
    )


def minmod_half(a, b):
    return 0.5 * (jnp.maximum(jnp.minimum(a, b), 0.0) + jnp.minimum(jnp.maximum(a, b), 0.0))


ALL_VMEM = 62 << 20
X_VMEM = 8 << 20
HBM = pltpu.HBM
VMEM = pltpu.VMEM
SMEM = pltpu.SMEM
DMA = pltpu.SemaphoreType.DMA


def call(kernel, name, operands, outs, scratch=(), flops=0, limit=8 << 20):
    shapes = [jax.ShapeDtypeStruct(shape, dtype) for shape, dtype, _ in outs]
    arrays = [o for o, _ in operands]
    moved = sum(o.size * o.dtype.itemsize for o in arrays + shapes)
    return pl.pallas_call(
        kernel,
        out_shape=tuple(shapes),
        in_specs=[pl.BlockSpec(memory_space=space) for _, space in operands],
        out_specs=tuple(pl.BlockSpec(memory_space=space) for _, _, space in outs),
        scratch_shapes=list(scratch),
        compiler_params=pltpu.CompilerParams(vmem_limit_bytes=limit),
        cost_estimate=pl.CostEstimate(flops=flops, bytes_accessed=moved, transcendentals=0),
        name=name,
    )(*arrays)


def speeds_yz():
    lane = lax.broadcasted_iota(jnp.int32, (NZ, WIDTH), 1)
    along_y = (lane >> 3).astype(jnp.float32) - 0.5 * (GY - 1)
    along_z = (lane & (GZ - 1)).astype(jnp.float32) - 0.5 * (GZ - 1)
    return along_y * (SPACING * COURANT), along_z * (SPACING * COURANT)


def flux_change_z(f, uz, z_up):
    dz = pltpu.roll(f, NZ - 1, 0) - f
    slope = minmod_half(pltpu.roll(dz, 1, 0), dz)
    down = pltpu.roll(f - slope, NZ - 1, 0)
    flux = jnp.where(z_up, f + slope, down)
    return uz * (flux - pltpu.roll(flux, 1, 0))


def edges(before, here, after):
    slope = minmod_half(here - before, after - here)
    return here + slope, here - slope


def upwind_face(before, here, after):
    return here + minmod_half(here - before, after - here)


def first_halo_kernel(sign_ref, dist_ref, behind_ref, ahead_ref, layers_ref, sems):
    forward = sign_ref[0] > 0
    copies = [
        pltpu.make_async_copy(
            dist_ref.at[pl.ds(jnp.where(forward, CX - 2, 0), 2)], layers_ref.at[0:2], sems.at[0]
        ),
        pltpu.make_async_copy(
            dist_ref.at[pl.ds(jnp.where(forward, 0, CX - 1), 1)], layers_ref.at[2:3], sems.at[1]
        ),
    ]
    for copy in copies:
        copy.start()
    copies[0].wait()
    behind_ref[...] = layers_ref[0:2].astype(jnp.bfloat16)
    copies[1].wait()
    ahead_ref[...] = layers_ref[2:3].astype(jnp.bfloat16)


def first_yz_kernel(dist_ref, f_ref, part_ref, sems):
    uy, uz = speeds_yz()
    y_up = uy > 0.0
    z_up = uz > 0.0

    def fetch(i):
        return pltpu.make_async_copy(
            dist_ref.at[pl.ds(2 * i, 2)], f_ref.at[pl.ds(2 * i, 2)], sems.at[i]
        )

    for i in range(CX // 2):
        fetch(i).start()

    def layer(x):
        def at(y):
            return f_ref[x, y % NY]

        up, _ = edges(at(-2), at(-1), at(0))
        next_up, next_down = edges(at(-1), at(0), at(1))
        flux_before = jnp.where(y_up, up, next_down)
        for y in range(NY):
            up = next_up
            next_up, next_down = edges(at(y), at(y + 1), at(y + 2))
            flux = jnp.where(y_up, up, next_down)
            here = at(y)
            part_ref[x, y] = here - uy * (flux - flux_before) - flux_change_z(here, uz, z_up)
            flux_before = flux

    def two_layers(i, carry):
        fetch(i).wait()
        layer(2 * i)
        layer(2 * i + 1)
        return carry

    lax.fori_loop(0, CX // 2, two_layers, 0)


def first_x_kernel(
    sign_ref, speed_ref, f_ref, part_ref, behind_ref, ahead_ref, out_ref, rows_ref, sems
):
    s = sign_ref[0]
    ux = speed_ref[0]
    forward = s > 0

    def put(target):
        return pltpu.make_async_copy(rows_ref.at[target], out_ref.at[target], sems.at[target])

    def line(quarter, y):
        inner = y * NZ
        y = quarter * BY + y

        def at(k):
            if k == -2:
                return behind_ref[jnp.where(forward, 0, 1), y].astype(jnp.float32)
            if k == -1:
                return behind_ref[jnp.where(forward, 1, 0), y].astype(jnp.float32)
            if k == CX:
                return ahead_ref[0, y].astype(jnp.float32)
            return f_ref[jnp.where(forward, k, CX - 1 - k), y]

        face_before = upwind_face(at(-2), at(-1), at(0))
        for k in range(CX):
            x = jnp.where(forward, k, CX - 1 - k)
            face = upwind_face(at(k - 1), at(k), at(k + 1))
            result = part_ref[x, y] - ux * (face - face_before)
            face_before = face
            start = pl.multiple_of((x % BX) * LINE + inner, NZ)
            high = x // (2 * BX)
            core = (x // BX + high) % 2
            target = high * (GROUPS // 2) + quarter * 2 + core
            rows_ref[target, pl.ds(start, NZ), :] = result.astype(jnp.bfloat16)

    def lines(quarter, carry):
        def one(y, inside):
            line(quarter, y)
            return inside

        lax.fori_loop(0, BY, one, 0)
        for high in range(2):
            for core in range(2):
                put(high * (GROUPS // 2) + quarter * 2 + core).start()
        return carry

    lax.fori_loop(0, NY // BY, lines, 0)
    for target in range(GROUPS):
        put(target).wait()


def collision_terms(
    rows, a_ref, b_ref, c_ref, project_ref, mix_ref, expand_ref, w_ref, hidden_ref, arrive
):
    arrive(0)
    moments = jnp.dot(rows, project_ref[...], preferred_element_type=jnp.float32)
    coeffs = jnp.dot(
        moments, mix_ref[...], precision=lax.Precision.HIGHEST, preferred_element_type=jnp.float32
    )
    lane = lax.broadcasted_iota(jnp.int32, coeffs.shape, 1)
    high = coeffs.astype(jnp.bfloat16).astype(jnp.float32)
    rest = coeffs - high
    middle = rest.astype(jnp.bfloat16).astype(jnp.float32)
    split = jnp.where(lane < 8, high, jnp.where(lane < 16, middle, rest - middle))
    split = split.astype(jnp.bfloat16)
    for n in range(RANK // 256):
        cols = slice(256 * n, 256 * (n + 1))
        arrive(1 + n)
        first = jnp.dot(rows, a_ref[:, cols], preferred_element_type=jnp.float32)
        second = jnp.dot(rows, b_ref[:, cols], preferred_element_type=jnp.float32)
        hidden_ref[:, cols] = (first * second).astype(jnp.bfloat16)
    hidden = hidden_ref[...]
    for n in range(NV // 256):
        cols = slice(256 * n, 256 * (n + 1))
        if n % 2 == 0:
            arrive(4 + n // 2)
        collision = jnp.dot(hidden, c_ref[:, cols], preferred_element_type=jnp.float32)
        collision = collision.astype(jnp.bfloat16).astype(jnp.float32)
        poly = jnp.dot(split, expand_ref[:, cols], preferred_element_type=jnp.float32)
        equilibrium = poly * w_ref[:, cols]
        for half in range(2):
            part = slice(WIDTH * half, WIDTH * (half + 1))
            yield 2 * n + half, collision[:, part], equilibrium[:, part]


def first_collide_kernel(
    rows_hbm, a_hbm, b_hbm, c_hbm, project_hbm, mix_hbm, expand_hbm, w_ref, rate_ref, mask_ref,
    f_out, x_up_out, x_down_out, y_up_out, y_down_out,
    rows_ref, a_ref, b_ref, c_ref, project_ref, mix_ref, expand_ref, hidden_ref,
    f_ref, x_up_ref, x_down_ref, y_up_ref, y_down_ref, in_sems, out_sems,
):
    pieces = [[(rows_hbm, rows_ref), (project_hbm, project_ref), (mix_hbm, mix_ref)]]
    for n in range(RANK // 256):
        cols = slice(256 * n, 256 * (n + 1))
        pieces.append([(a_hbm.at[:, cols], a_ref.at[:, cols]), (b_hbm.at[:, cols], b_ref.at[:, cols])])
    pieces.append([(expand_hbm, expand_ref)])
    for n in range(4):
        cols = slice(512 * n, 512 * (n + 1))
        if n:
            pieces.append([])
        pieces[-1].append((c_hbm.at[:, cols], c_ref.at[:, cols]))
    fetches, count = [], 0
    for piece in pieces:
        fetches.append([])
        for source, target in piece:
            fetches[-1].append(pltpu.make_async_copy(source, target, in_sems.at[count]))
            fetches[-1][-1].start()
            count += 1

    def arrive(i):
        for fetch in fetches[i]:
            fetch.wait()

    stores = []

    def send(source, target, first, last):
        stores.append(
            pltpu.make_async_copy(
                source.at[first:last], target.at[first:last], out_sems.at[len(stores)]
            )
        )
        stores[-1].start()

    for fetch in fetches[0]:
        fetch.wait()
    rows = jnp.concatenate([rows_ref[g] for g in range(GROUPS)], axis=1)
    rate = jnp.broadcast_to(rate_ref[...], (LAYER, WIDTH))
    kinetic = jnp.broadcast_to(mask_ref[...], (LAYER, WIDTH)) > 0.0
    half = GROUPS // 2
    low_lane = lax.broadcasted_iota(jnp.int32, (NZ, WIDTH), 1) < WIDTH // 2
    for g, collision, equilibrium in collision_terms(
        rows, a_ref, b_ref, c_ref, project_ref, mix_ref, expand_ref, w_ref, hidden_ref,
        lambda i: arrive(i) if i else None,
    ):
        moved = rows_ref[g].astype(jnp.float32)
        change = jnp.where(kinetic, COLLIDE * collision, rate * (equilibrium - moved))
        result = moved + change
        f_ref[g] = result
        sent = result.astype(jnp.bfloat16)
        x_up_ref[g] = sent[3 * LINE : 4 * LINE]
        x_down_ref[g] = sent[0:LINE]
        if g >= half:
            x_up_ref[g + half] = sent[2 * LINE : 3 * LINE]
        else:
            x_down_ref[g + GROUPS] = sent[LINE : 2 * LINE]
        for x in range(BX):
            here = slice(NZ * x, NZ * (x + 1))
            y_down_ref[g, here] = sent[LINE * x : LINE * x + NZ]
            y_up_ref[g, here] = sent[LINE * x + 3 * NZ : LINE * x + 4 * NZ]
            if g >= half:
                low = g - half
                second = slice(LINE * x + NZ, LINE * x + 2 * NZ)
                third = slice(LINE * x + 2 * NZ, LINE * x + 3 * NZ)
                y_up_ref[GROUPS + low, here] = jnp.where(
                    low_lane, pltpu.roll(f_ref[low, third], WIDTH // 2, 1), result[third]
                ).astype(jnp.bfloat16)
                y_down_ref[GROUPS + low, here] = jnp.where(
                    low_lane, f_ref[low, second], pltpu.roll(result[second], WIDTH // 2, 1)
                ).astype(jnp.bfloat16)
        if g % 4 == 3:
            first = g - 3
            send(f_ref, f_out, first, g + 1)
            for source, target in (
                (y_up_ref, y_up_out), (y_down_ref, y_down_out),
                (x_up_ref, x_up_out), (x_down_ref, x_down_out),
            ):
                send(source, target, first, g + 1)
            if g >= half:
                send(y_up_ref, y_up_out, first + half, g + 1 + half)
                send(y_down_ref, y_down_out, first + half, g + 1 + half)
                send(x_up_ref, x_up_out, first + half, g + 1 + half)
            else:
                send(x_down_ref, x_down_out, first + GROUPS, g + 1 + GROUPS)
    for store in stores:
        store.wait()


def second_z_kernel(f_hbm, f_ref, part_ref, sems):
    _, uz = speeds_yz()
    z_up = uz > 0.0

    def fetch(i):
        return pltpu.make_async_copy(
            f_hbm.at[pl.ds(2 * i, 2)], f_ref.at[pl.ds(2 * i, 2)], sems.at[i]
        )

    for i in range(GROUPS // 2):
        fetch(i).start()

    def two_groups(i, carry):
        fetch(i).wait()
        for g in (2 * i, 2 * i + 1):
            for c in range(BX * BY):
                here = slice(NZ * c, NZ * (c + 1))
                f = f_ref[g, here]
                part_ref[g, here] = f - flux_change_z(f, uz, z_up)
        return carry

    lax.fori_loop(0, GROUPS // 2, two_groups, 0)


def second_xy_kernel(
    f_ref, part_ref, x_below_ref, x_above_ref, y_below_ref, y_above_ref, moved_ref
):
    uy, _ = speeds_yz()
    y_up = uy > 0.0
    half = GROUPS // 2

    def wide(ref, g, i):
        return ref[g, NZ * i : NZ * (i + 1)].astype(jnp.float32)

    def group(pair, upward):
        g = pair + half if upward else pair
        extra = pair + GROUPS
        ux = (g.astype(jnp.float32) - 0.5 * (GX - 1)) * (SPACING * COURANT)
        ux = ux if upward else -ux
        for y in range(BY):
            behind, ahead = (x_below_ref, x_above_ref) if upward else (x_above_ref, x_below_ref)

            def at_x(k):
                if k == -2:
                    return wide(behind, extra, y)
                if k == -1:
                    return wide(behind, g, y)
                if k == BX:
                    return wide(ahead, g, y)
                x = k if upward else BX - 1 - k
                return f_ref[g, LINE * x + NZ * y : LINE * x + NZ * (y + 1)]

            face_before = upwind_face(at_x(-2), at_x(-1), at_x(0))
            for k in range(BX):
                x = k if upward else BX - 1 - k
                face = upwind_face(at_x(k - 1), at_x(k), at_x(k + 1))
                here = slice(LINE * x + NZ * y, LINE * x + NZ * (y + 1))
                moved_ref[g, here] = part_ref[g, here] - ux * (face - face_before)
                face_before = face
        for x in range(BX):

            def at_y(y):
                if y == -2:
                    below = wide(y_below_ref, extra, x)
                    return below if upward else pltpu.roll(below, WIDTH // 2, 1)
                if y == -1:
                    return wide(y_below_ref, g, x)
                if y == BY:
                    return wide(y_above_ref, g, x)
                if y == BY + 1:
                    above = wide(y_above_ref, extra, x)
                    return pltpu.roll(above, WIDTH // 2, 1) if upward else above
                return f_ref[g, LINE * x + NZ * y : LINE * x + NZ * (y + 1)]

            up, _ = edges(at_y(-2), at_y(-1), at_y(0))
            next_up, next_down = edges(at_y(-1), at_y(0), at_y(1))
            flux_before = jnp.where(y_up, up, next_down)
            for y in range(BY):
                up = next_up
                next_up, next_down = edges(at_y(y), at_y(y + 1), at_y(y + 2))
                flux = jnp.where(y_up, up, next_down)
                here = slice(LINE * x + NZ * y, LINE * x + NZ * (y + 1))
                moved_ref[g, here] = moved_ref[g, here] - uy * (flux - flux_before)
                flux_before = flux

    def downwards(pair, carry):
        group(pair, False)
        return carry

    def upwards(pair, carry):
        group(pair, True)
        return carry

    lax.fori_loop(0, half, downwards, 0)
    lax.fori_loop(0, half, upwards, 0)


def second_collide_kernel(
    moved_ref, a_ref, b_ref, c_ref, project_ref, mix_ref, expand_ref, w_ref, rate_ref, mask_ref,
    out_ref, hidden_ref,
):
    rows = jnp.concatenate([moved_ref[g].astype(jnp.bfloat16) for g in range(GROUPS)], axis=1)
    rate = jnp.broadcast_to(rate_ref[...], (LAYER, WIDTH))
    kinetic = jnp.broadcast_to(mask_ref[...], (LAYER, WIDTH)) > 0.0
    for g, collision, equilibrium in collision_terms(
        rows, a_ref, b_ref, c_ref, project_ref, mix_ref, expand_ref, w_ref, hidden_ref,
        lambda i: None,
    ):
        moved = moved_ref[g]
        change = jnp.where(kinetic, COLLIDE * collision, rate * (equilibrium - moved))
        out_ref[g] = (moved + change).astype(jnp.bfloat16)


def place_kernel(in_ref, out_hbm, out_ref, sems):
    stores = []
    for quarter in range(4):
        high = quarter // 2
        core = (quarter % 2) ^ high
        for x in range(BX):
            for y_quarter in range(4):
                for y in range(BY):
                    c = LINE * x + NZ * y
                    out_ref[BX * quarter + x, BY * y_quarter + y] = in_ref[
                        high * (GROUPS // 2) + y_quarter * 2 + core, c : c + NZ
                    ].astype(jnp.float32)
        part = slice(BX * quarter, BX * (quarter + 1))
        stores.append(pltpu.make_async_copy(out_ref.at[part], out_hbm.at[part], sems.at[quarter]))
        stores[-1].start()
    for store in stores:
        store.wait()


def device_of(space, high, x, core):
    return (space * 2 + high) * 8 + x * 2 + core


def steps_of(slabs):
    upwind, downwind, x_up, y_up = [], [], [], []
    for space in range(slabs):
        for high in range(2):
            for x in range(4):
                for core in range(2):
                    me = device_of(space, high, x, core)
                    after = device_of((space + 1) % slabs, high, x, core)
                    before = device_of((space - 1) % slabs, high, x, core)
                    upwind.append((me, after if high else before))
                    downwind.append((me, before if high else after))
                    quarter = 2 * high + (core ^ high)
                    next_slab = (space + (quarter == 3)) % slabs
                    quarter = (quarter + 1) % 4
                    x_up.append(
                        (me, device_of(next_slab, quarter // 2, x, (quarter % 2) ^ (quarter // 2)))
                    )
                    y_up.append((me, device_of(space, high, (x + 1) % 4, core)))
    back = lambda pairs: [(target, source) for source, target in pairs]
    return upwind, downwind, x_up, back(x_up), y_up, back(y_up)


def body(dist, relax_rate, kinetic_cells, kinetic_count, map_a, map_b, map_c):
    rank_vel = lax.axis_index("vel")
    rank_space = lax.axis_index("space")
    both = ("space", "vel")
    upwind, downwind, x_up, x_down, y_up, y_down = steps_of(lax.axis_size("space"))
    project, mix, expand, w = tables()
    consts = (jnp.asarray(project), jnp.asarray(mix), jnp.asarray(expand), jnp.asarray(w))
    vx = (rank_vel.astype(jnp.float32) - 0.5 * (GX - 1)) * SPACING
    speed = (COURANT * jnp.abs(vx)).reshape(1)
    forward = rank_vel >= GROUPS // 2
    sign = jnp.where(forward, 1, -1).astype(jnp.int32).reshape(1)

    layers = (NY, NZ, WIDTH)
    behind, ahead = call(
        first_halo_kernel, "first_halo", ((sign, SMEM), (dist, HBM)),
        (((2,) + layers, jnp.bfloat16, VMEM), ((1,) + layers, jnp.bfloat16, VMEM)),
        scratch=(VMEM((3,) + layers, jnp.float32), DMA((2,))), limit=ALL_VMEM,
    )
    behind = lax.ppermute(behind, both, upwind)
    ahead = lax.ppermute(ahead, both, downwind)

    high, y_quarter, core = rank_vel // 8, rank_vel // 2 % 4, rank_vel % 2
    x_quarter = 2 * high + (core + high) % 2
    rate = lax.dynamic_slice(relax_rate, (BX * x_quarter, BY * y_quarter, 0), (BX, BY, NZ))
    rate = rate.reshape(LAYER, 1)
    own = lax.dynamic_index_in_dim(kinetic_count, rank_space, 1, False)
    live = jnp.arange(CX * LAYER, dtype=jnp.int32)[None, :] < own[:, None]
    listed = jnp.where(live, kinetic_cells, -1)
    slot = jnp.arange(LAYER, dtype=jnp.int32)
    cell = (BX * x_quarter + slot // LINE) * LAYER + (BY * y_quarter * NZ + slot % LINE)
    masks = jnp.any(listed[:, None, :] == cell[None, :, None], axis=2, keepdims=True)
    masks = masks.astype(jnp.float32)

    state = ((CX,) + layers, jnp.float32, VMEM)
    wide = (GROUPS, LAYER, WIDTH)
    halo = (GROUPS + GROUPS // 2, LINE, WIDTH)
    half = jnp.bfloat16
    hidden = VMEM((LAYER, RANK), half)

    f, part = call(
        first_yz_kernel, "first_yz", ((dist, HBM),), (state, state),
        scratch=(DMA((CX // 2,)),), flops=12_000_000,
    )
    (rows,) = call(
        first_x_kernel, "first_x",
        ((sign, SMEM), (speed, SMEM), (f, VMEM), (part, VMEM), (behind, VMEM), (ahead, VMEM)),
        ((wide, half, HBM),), scratch=(VMEM(wide, half), DMA((GROUPS,))), flops=6_000_000, limit=X_VMEM,
    )
    gathered = lax.all_to_all(rows, "vel", split_axis=0, concat_axis=0, tiled=True)
    held = (map_a, map_b, map_c) + consts[:3]
    f, up_x, down_x, up_y, down_y = call(
        first_collide_kernel, "first_collide",
        ((gathered, HBM),) + tuple((o, HBM) for o in held)
        + ((consts[3], VMEM), (rate, VMEM), (masks[0], VMEM)),
        ((wide, jnp.float32, HBM),) + ((halo, half, HBM),) * 4,
        scratch=(VMEM(wide, half),) + tuple(VMEM(o.shape, o.dtype) for o in held)
        + (hidden, VMEM(wide, jnp.float32)) + (VMEM(halo, half),) * 4 + (DMA((16,)), DMA((32,))),
        flops=2_500_000_000, limit=ALL_VMEM,
    )
    y_below = lax.ppermute(up_y, both, y_up)
    y_above = lax.ppermute(down_y, both, y_down)
    x_below = lax.ppermute(up_x, both, x_up)
    x_above = lax.ppermute(down_x, both, x_down)
    f, part = call(
        second_z_kernel, "second_z", ((f, HBM),), ((wide, jnp.float32, VMEM),) * 2,
        scratch=(DMA((GROUPS // 2,)),), flops=6_000_000,
    )
    (moved,) = call(
        second_xy_kernel, "second_xy",
        tuple((o, VMEM) for o in (f, part, x_below, x_above, y_below, y_above)),
        ((wide, jnp.float32, VMEM),), flops=12_000_000,
    )
    (result,) = call(
        second_collide_kernel, "second_collide",
        ((moved, VMEM),) + tuple((o, VMEM) for o in held + (consts[3], rate, masks[1])),
        ((wide, half, VMEM),), scratch=(hidden,), flops=2_500_000_000, limit=12 << 20,
    )
    pieces = lax.all_to_all(result, "vel", split_axis=0, concat_axis=0, tiled=True)
    (out,) = call(
        place_kernel, "place", ((pieces, VMEM),), (((CX,) + layers, jnp.float32, HBM),),
        scratch=(VMEM((CX,) + layers, jnp.float32), DMA((4,))),
    )
    return out


def solution(mesh):
    return jax.shard_map(
        body,
        mesh=mesh,
        in_specs=(
            P("space", None, None, "vel"),
            P("space", None, None),
            P(None, "space"),
            P(),
            P(),
            P(),
            P(),
        ),
        out_specs=P("space", None, None, "vel"),
        check_vma=False,
    )
```

```python
import jax
import jax.numpy as jnp
import numpy as np
from jax import lax
from jax.experimental import pallas as pl
from jax.experimental.pallas import tpu as pltpu
from jax.sharding import PartitionSpec as P

GX = 16
GY = 16
GZ = 8
NV = GX * GY * GZ
RANK = 768
COURANT = 0.1
SPACING = 0.5
COLLIDE = 0.5

CX = 16
NY = 16
NZ = 16
LAYER = NY * NZ
WIDTH = 128
GROUPS = NV // WIDTH
OFFSET = 3.0 / 16.0
BX = 4
BY = 4
LINE = BX * NZ


def tables():
    k = np.arange(NV)
    vx = ((k // (GY * GZ)) - 0.5 * (GX - 1)) * SPACING
    vy = ((k // GZ % GY) - 0.5 * (GY - 1)) * SPACING
    vz = ((k % GZ) - 0.5 * (GZ - 1)) * SPACING
    s = vx * vx + vy * vy + vz * vz
    w = np.exp(-0.5 * s)
    w = w / w.sum()
    sx, sy, sz = (w * vx * vx).sum(), (w * vy * vy).sum(), (w * vz * vz).sum()
    m2, m4 = (w * s).sum(), (w * s * s).sum()
    basis = np.stack([np.ones(NV), vx, vy, vz, s - OFFSET])
    q = np.zeros((5, 5))
    scale = 1.0 / (m4 - m2 * m2)
    thermal = np.zeros(5)
    thermal[0] = (OFFSET - m2) * scale
    thermal[4] = scale
    q[:, 4] = thermal
    q[:, 0] = (OFFSET - m2) * thermal
    q[0, 0] += 1.0
    q[1, 1], q[2, 2], q[3, 3] = 1.0 / sx, 1.0 / sy, 1.0 / sz
    project = np.zeros((NV, 128))
    project[:, :5] = basis.T
    mix = np.zeros((128, 128))
    expand = np.zeros((128, NV))
    for part in range(3):
        mix[:5, 8 * part : 8 * part + 5] = q
        expand[8 * part : 8 * part + 5] = basis
    return (
        project.astype(jnp.bfloat16),
        mix.astype(np.float32),
        expand.astype(jnp.bfloat16),
        w.reshape(1, NV).astype(np.float32),
    )


def minmod_half(a, b):
    return 0.5 * (jnp.maximum(jnp.minimum(a, b), 0.0) + jnp.minimum(jnp.maximum(a, b), 0.0))


ALL_VMEM = 62 << 20
HBM = pltpu.HBM
VMEM = pltpu.VMEM
SMEM = pltpu.SMEM
DMA = pltpu.SemaphoreType.DMA


def call(kernel, name, operands, outs, scratch=(), flops=0, limit=8 << 20):
    shapes = [jax.ShapeDtypeStruct(shape, dtype) for shape, dtype, _ in outs]
    arrays = [o for o, _ in operands]
    moved = sum(o.size * o.dtype.itemsize for o in arrays + shapes)
    return pl.pallas_call(
        kernel,
        out_shape=tuple(shapes),
        in_specs=[pl.BlockSpec(memory_space=space) for _, space in operands],
        out_specs=tuple(pl.BlockSpec(memory_space=space) for _, _, space in outs),
        scratch_shapes=list(scratch),
        compiler_params=pltpu.CompilerParams(vmem_limit_bytes=limit),
        cost_estimate=pl.CostEstimate(flops=flops, bytes_accessed=moved, transcendentals=0),
        name=name,
    )(*arrays)


def speeds_yz():
    lane = lax.broadcasted_iota(jnp.int32, (NZ, WIDTH), 1)
    along_y = (lane >> 3).astype(jnp.float32) - 0.5 * (GY - 1)
    along_z = (lane & (GZ - 1)).astype(jnp.float32) - 0.5 * (GZ - 1)
    return along_y * (SPACING * COURANT), along_z * (SPACING * COURANT)


def flux_change_z(f, uz, z_up):
    dz = pltpu.roll(f, NZ - 1, 0) - f
    slope = minmod_half(pltpu.roll(dz, 1, 0), dz)
    down = pltpu.roll(f - slope, NZ - 1, 0)
    flux = jnp.where(z_up, f + slope, down)
    return uz * (flux - pltpu.roll(flux, 1, 0))


def edges(before, here, after):
    slope = minmod_half(here - before, after - here)
    return here + slope, here - slope


def upwind_face(before, here, after):
    return here + minmod_half(here - before, after - here)


def first_halo_kernel(sign_ref, dist_ref, behind_ref, ahead_ref, layers_ref, sems):
    forward = sign_ref[0] > 0
    copies = [
        pltpu.make_async_copy(
            dist_ref.at[pl.ds(jnp.where(forward, CX - 2, 0), 2)], layers_ref.at[0:2], sems.at[0]
        ),
        pltpu.make_async_copy(
            dist_ref.at[pl.ds(jnp.where(forward, 0, CX - 1), 1)], layers_ref.at[2:3], sems.at[1]
        ),
    ]
    for copy in copies:
        copy.start()
    copies[0].wait()
    behind_ref[...] = layers_ref[0:2].astype(jnp.bfloat16)
    copies[1].wait()
    ahead_ref[...] = layers_ref[2:3].astype(jnp.bfloat16)


def first_yz_kernel(dist_ref, f_ref, part_ref, sems):
    uy, uz = speeds_yz()
    y_up = uy > 0.0
    z_up = uz > 0.0

    def fetch(i):
        return pltpu.make_async_copy(
            dist_ref.at[pl.ds(2 * i, 2)], f_ref.at[pl.ds(2 * i, 2)], sems.at[i]
        )

    for i in range(CX // 2):
        fetch(i).start()

    def layer(x):
        def at(y):
            return f_ref[x, y % NY]

        up, _ = edges(at(-2), at(-1), at(0))
        next_up, next_down = edges(at(-1), at(0), at(1))
        flux_before = jnp.where(y_up, up, next_down)
        for y in range(NY):
            up = next_up
            next_up, next_down = edges(at(y), at(y + 1), at(y + 2))
            flux = jnp.where(y_up, up, next_down)
            here = at(y)
            part_ref[x, y] = here - uy * (flux - flux_before) - flux_change_z(here, uz, z_up)
            flux_before = flux

    def two_layers(i, carry):
        fetch(i).wait()
        layer(2 * i)
        layer(2 * i + 1)
        return carry

    lax.fori_loop(0, CX // 2, two_layers, 0)


def first_x_kernel(
    sign_ref, speed_ref, f_ref, part_ref, behind_ref, ahead_ref, out_ref, rows_ref, sems
):
    s = sign_ref[0]
    ux = speed_ref[0]
    forward = s > 0
    layers = [jnp.where(forward, k, CX - 1 - k) for k in range(CX)]
    starts = [(x % BX) * LINE for x in layers[:BX]]
    owners = []
    for k in range(4):
        quarter = jnp.where(forward, k, 3 - k)
        high = quarter // 2
        owners.append(high * (GROUPS // 2) + (quarter + high) % 2)

    def put(target):
        return pltpu.make_async_copy(rows_ref.at[target], out_ref.at[target], sems.at[target])

    def line(quarter, y):
        inner = y * NZ
        y = quarter * BY + y

        def at(k):
            if k == -2:
                return behind_ref[jnp.where(forward, 0, 1), y].astype(jnp.float32)
            if k == -1:
                return behind_ref[jnp.where(forward, 1, 0), y].astype(jnp.float32)
            if k == CX:
                return ahead_ref[0, y].astype(jnp.float32)
            return f_ref[layers[k], y]

        face_before = upwind_face(at(-2), at(-1), at(0))
        for k in range(CX):
            face = upwind_face(at(k - 1), at(k), at(k + 1))
            result = part_ref[layers[k], y] - ux * (face - face_before)
            face_before = face
            start = pl.multiple_of(starts[k % BX] + inner, NZ)
            target = owners[k // BX] + quarter * 2
            rows_ref[target, pl.ds(start, NZ), :] = result.astype(jnp.bfloat16)

    def lines(quarter, carry):
        def one(y, inside):
            line(quarter, y)
            return inside

        lax.fori_loop(0, BY, one, 0)
        for high in range(2):
            for core in range(2):
                put(high * (GROUPS // 2) + quarter * 2 + core).start()
        return carry

    lax.fori_loop(0, NY // BY, lines, 0)
    for target in range(GROUPS):
        put(target).wait()


def split_coefficients(moments, mix_ref):
    coeffs = jnp.dot(
        moments, mix_ref[...], precision=lax.Precision.HIGHEST, preferred_element_type=jnp.float32
    )
    lane = lax.broadcasted_iota(jnp.int32, coeffs.shape, 1)
    high = coeffs.astype(jnp.bfloat16).astype(jnp.float32)
    rest = coeffs - high
    middle = rest.astype(jnp.bfloat16).astype(jnp.float32)
    split = jnp.where(lane < 8, high, jnp.where(lane < 16, middle, rest - middle))
    return split.astype(jnp.bfloat16)


def outcome(hidden, split, c_ref, expand_ref, w_ref, arrive=None):
    for n in range(NV // 256):
        cols = slice(256 * n, 256 * (n + 1))
        if arrive is not None and n % 2 == 0:
            arrive[n // 2].wait()
        poly = jnp.dot(split, expand_ref[:, cols], preferred_element_type=jnp.float32)
        equilibrium = poly * w_ref[:, cols]
        collision = jnp.dot(hidden, c_ref[:, cols], preferred_element_type=jnp.float32)
        collision = collision.astype(jnp.bfloat16).astype(jnp.float32)
        for half in range(2):
            part = slice(WIDTH * half, WIDTH * (half + 1))
            yield 2 * n + half, collision[:, part], equilibrium[:, part]


def first_collide_kernel(
    rows_hbm, a_hbm, b_hbm, c_hbm, project_hbm, mix_hbm, expand_hbm, w_ref, rate_ref, mask_ref,
    f_out, x_up_out, x_down_out, y_up_out, y_down_out,
    rows_ref, a_ref, b_ref, c_ref, project_ref, mix_ref, expand_ref, hidden_ref,
    first_ref, second_ref, f_ref, x_up_ref, x_down_ref, y_up_ref, y_down_ref, in_sems, out_sems,
):
    count = 0

    def fetch(source, target, piece=None):
        nonlocal count
        if piece is not None:
            source, target = source.at[piece], target.at[piece]
        copy = pltpu.make_async_copy(source, target, in_sems.at[count])
        copy.start()
        count += 1
        return copy

    chunks = []
    for k in range(4):
        groups, depth = slice(4 * k, 4 * (k + 1)), slice(512 * k, 512 * (k + 1))
        chunks.append(
            [
                fetch(rows_hbm, rows_ref, groups), fetch(a_hbm, a_ref, depth),
                fetch(b_hbm, b_ref, depth), fetch(project_hbm, project_ref, depth),
            ]
        )
    tables = [fetch(mix_hbm, mix_ref), fetch(expand_hbm, expand_ref)]
    c_parts = [
        fetch(c_hbm, c_ref, (slice(None), slice(512 * k, 512 * (k + 1)))) for k in range(4)
    ]
    moments = jnp.zeros((LAYER, WIDTH), jnp.float32)
    for k in range(4):
        depth = slice(512 * k, 512 * (k + 1))
        for copy in chunks[k]:
            copy.wait()
        rows = jnp.concatenate([rows_ref[g] for g in range(4 * k, 4 * (k + 1))], axis=1)
        moments += jnp.dot(rows, project_ref[depth], preferred_element_type=jnp.float32)
        for n in range(RANK // 256):
            cols = slice(256 * n, 256 * (n + 1))
            first = jnp.dot(rows, a_ref[depth, cols], preferred_element_type=jnp.float32)
            second = jnp.dot(rows, b_ref[depth, cols], preferred_element_type=jnp.float32)
            if k:
                first += first_ref[:, cols]
                second += second_ref[:, cols]
            if k < 3:
                first_ref[:, cols] = first
                second_ref[:, cols] = second
            else:
                hidden_ref[:, cols] = (first * second).astype(jnp.bfloat16)
    for copy in tables:
        copy.wait()
    split = split_coefficients(moments, mix_ref)

    stores = []

    def send(source, target, first, last):
        stores.append(
            pltpu.make_async_copy(
                source.at[first:last], target.at[first:last], out_sems.at[len(stores)]
            )
        )
        stores[-1].start()

    rate = jnp.broadcast_to(rate_ref[...], (LAYER, WIDTH))
    kinetic = jnp.broadcast_to(mask_ref[...], (LAYER, WIDTH)) > 0.0
    half = GROUPS // 2
    low_lane = lax.broadcasted_iota(jnp.int32, (NZ, WIDTH), 1) < WIDTH // 2
    for g, collision, equilibrium in outcome(
        hidden_ref[...], split, c_ref, expand_ref, w_ref, c_parts
    ):
        moved = rows_ref[g].astype(jnp.float32)
        change = jnp.where(kinetic, COLLIDE * collision, rate * (equilibrium - moved))
        result = moved + change
        f_ref[g] = result
        sent = result.astype(jnp.bfloat16)
        x_up_ref[g] = sent[3 * LINE : 4 * LINE]
        x_down_ref[g] = sent[0:LINE]
        if g >= half:
            x_up_ref[g + half] = sent[2 * LINE : 3 * LINE]
        else:
            x_down_ref[g + GROUPS] = sent[LINE : 2 * LINE]
        for x in range(BX):
            here = slice(NZ * x, NZ * (x + 1))
            y_down_ref[g, here] = sent[LINE * x : LINE * x + NZ]
            y_up_ref[g, here] = sent[LINE * x + 3 * NZ : LINE * x + 4 * NZ]
            if g >= half:
                low = g - half
                second = slice(LINE * x + NZ, LINE * x + 2 * NZ)
                third = slice(LINE * x + 2 * NZ, LINE * x + 3 * NZ)
                y_up_ref[GROUPS + low, here] = jnp.where(
                    low_lane, pltpu.roll(f_ref[low, third], WIDTH // 2, 1), result[third]
                ).astype(jnp.bfloat16)
                y_down_ref[GROUPS + low, here] = jnp.where(
                    low_lane, f_ref[low, second], pltpu.roll(result[second], WIDTH // 2, 1)
                ).astype(jnp.bfloat16)
        if g % 4 == 3:
            first = g - 3
            send(f_ref, f_out, first, g + 1)
            for source, target in (
                (y_up_ref, y_up_out), (y_down_ref, y_down_out),
                (x_up_ref, x_up_out), (x_down_ref, x_down_out),
            ):
                send(source, target, first, g + 1)
            if g >= half:
                send(y_up_ref, y_up_out, first + half, g + 1 + half)
                send(y_down_ref, y_down_out, first + half, g + 1 + half)
                send(x_up_ref, x_up_out, first + half, g + 1 + half)
            else:
                send(x_down_ref, x_down_out, first + GROUPS, g + 1 + GROUPS)
    for store in stores:
        store.wait()


def second_z_kernel(f_hbm, f_ref, part_ref, sems):
    _, uz = speeds_yz()
    z_up = uz > 0.0

    def fetch(i):
        return pltpu.make_async_copy(
            f_hbm.at[pl.ds(2 * i, 2)], f_ref.at[pl.ds(2 * i, 2)], sems.at[i]
        )

    for i in range(GROUPS // 2):
        fetch(i).start()

    def two_groups(i, carry):
        fetch(i).wait()
        for g in (2 * i, 2 * i + 1):
            for c in range(BX * BY):
                here = slice(NZ * c, NZ * (c + 1))
                f = f_ref[g, here]
                part_ref[g, here] = f - flux_change_z(f, uz, z_up)
        return carry

    lax.fori_loop(0, GROUPS // 2, two_groups, 0)


def second_xy_kernel(
    f_ref, part_ref, x_below_ref, x_above_ref, y_below_ref, y_above_ref, moved_ref
):
    uy, _ = speeds_yz()
    y_up = uy > 0.0
    half = GROUPS // 2

    def wide(ref, g, i):
        return ref[g, NZ * i : NZ * (i + 1)].astype(jnp.float32)

    def group(pair, upward):
        g = pair + half if upward else pair
        extra = pair + GROUPS
        ux = (g.astype(jnp.float32) - 0.5 * (GX - 1)) * (SPACING * COURANT)
        ux = ux if upward else -ux
        for y in range(BY):
            behind, ahead = (x_below_ref, x_above_ref) if upward else (x_above_ref, x_below_ref)

            def at_x(k):
                if k == -2:
                    return wide(behind, extra, y)
                if k == -1:
                    return wide(behind, g, y)
                if k == BX:
                    return wide(ahead, g, y)
                x = k if upward else BX - 1 - k
                return f_ref[g, LINE * x + NZ * y : LINE * x + NZ * (y + 1)]

            face_before = upwind_face(at_x(-2), at_x(-1), at_x(0))
            for k in range(BX):
                x = k if upward else BX - 1 - k
                face = upwind_face(at_x(k - 1), at_x(k), at_x(k + 1))
                here = slice(LINE * x + NZ * y, LINE * x + NZ * (y + 1))
                moved_ref[g, here] = part_ref[g, here] - ux * (face - face_before)
                face_before = face
        for x in range(BX):

            def at_y(y):
                if y == -2:
                    below = wide(y_below_ref, extra, x)
                    return below if upward else pltpu.roll(below, WIDTH // 2, 1)
                if y == -1:
                    return wide(y_below_ref, g, x)
                if y == BY:
                    return wide(y_above_ref, g, x)
                if y == BY + 1:
                    above = wide(y_above_ref, extra, x)
                    return pltpu.roll(above, WIDTH // 2, 1) if upward else above
                return f_ref[g, LINE * x + NZ * y : LINE * x + NZ * (y + 1)]

            up, _ = edges(at_y(-2), at_y(-1), at_y(0))
            next_up, next_down = edges(at_y(-1), at_y(0), at_y(1))
            flux_before = jnp.where(y_up, up, next_down)
            for y in range(BY):
                up = next_up
                next_up, next_down = edges(at_y(y), at_y(y + 1), at_y(y + 2))
                flux = jnp.where(y_up, up, next_down)
                here = slice(LINE * x + NZ * y, LINE * x + NZ * (y + 1))
                moved_ref[g, here] = moved_ref[g, here] - uy * (flux - flux_before)
                flux_before = flux

    def downwards(pair, carry):
        group(pair, False)
        return carry

    def upwards(pair, carry):
        group(pair, True)
        return carry

    lax.fori_loop(0, half, downwards, 0)
    lax.fori_loop(0, half, upwards, 0)


def second_collide_kernel(
    moved_ref, a_ref, b_ref, c_ref, project_ref, mix_ref, expand_ref, w_ref, rate_ref, mask_ref,
    out_ref, hidden_ref,
):
    rows = jnp.concatenate([moved_ref[g].astype(jnp.bfloat16) for g in range(GROUPS)], axis=1)
    rate = jnp.broadcast_to(rate_ref[...], (LAYER, WIDTH))
    kinetic = jnp.broadcast_to(mask_ref[...], (LAYER, WIDTH)) > 0.0
    moments = jnp.dot(rows, project_ref[...], preferred_element_type=jnp.float32)
    split = split_coefficients(moments, mix_ref)
    for n in range(RANK // 256):
        cols = slice(256 * n, 256 * (n + 1))
        first = jnp.dot(rows, a_ref[:, cols], preferred_element_type=jnp.float32)
        second = jnp.dot(rows, b_ref[:, cols], preferred_element_type=jnp.float32)
        hidden_ref[:, cols] = (first * second).astype(jnp.bfloat16)
    for g, collision, equilibrium in outcome(hidden_ref[...], split, c_ref, expand_ref, w_ref):
        moved = moved_ref[g]
        change = jnp.where(kinetic, COLLIDE * collision, rate * (equilibrium - moved))
        out_ref[g] = (moved + change).astype(jnp.bfloat16)


def place_kernel(in_ref, out_hbm, out_ref, sems):
    stores = []
    for quarter in range(4):
        high = quarter // 2
        core = (quarter % 2) ^ high
        for x in range(BX):
            for y_quarter in range(4):
                for y in range(BY):
                    c = LINE * x + NZ * y
                    out_ref[BX * quarter + x, BY * y_quarter + y] = in_ref[
                        high * (GROUPS // 2) + y_quarter * 2 + core, c : c + NZ
                    ].astype(jnp.float32)
        part = slice(BX * quarter, BX * (quarter + 1))
        stores.append(pltpu.make_async_copy(out_ref.at[part], out_hbm.at[part], sems.at[quarter]))
        stores[-1].start()
    for store in stores:
        store.wait()


def device_of(space, high, x, core):
    return (space * 2 + high) * 8 + x * 2 + core


def steps_of(slabs):
    upwind, downwind, x_up, y_up = [], [], [], []
    for space in range(slabs):
        for high in range(2):
            for x in range(4):
                for core in range(2):
                    me = device_of(space, high, x, core)
                    after = device_of((space + 1) % slabs, high, x, core)
                    before = device_of((space - 1) % slabs, high, x, core)
                    upwind.append((me, after if high else before))
                    downwind.append((me, before if high else after))
                    quarter = 2 * high + (core ^ high)
                    next_slab = (space + (quarter == 3)) % slabs
                    quarter = (quarter + 1) % 4
                    x_up.append(
                        (me, device_of(next_slab, quarter // 2, x, (quarter % 2) ^ (quarter // 2)))
                    )
                    y_up.append((me, device_of(space, high, (x + 1) % 4, core)))
    back = lambda pairs: [(target, source) for source, target in pairs]
    return upwind, downwind, x_up, back(x_up), y_up, back(y_up)


def body(dist, relax_rate, kinetic_cells, kinetic_count, map_a, map_b, map_c):
    rank_vel = lax.axis_index("vel")
    rank_space = lax.axis_index("space")
    both = ("space", "vel")
    upwind, downwind, x_up, x_down, y_up, y_down = steps_of(lax.axis_size("space"))
    project, mix, expand, w = tables()
    consts = (jnp.asarray(project), jnp.asarray(mix), jnp.asarray(expand), jnp.asarray(w))
    vx = (rank_vel.astype(jnp.float32) - 0.5 * (GX - 1)) * SPACING
    speed = (COURANT * jnp.abs(vx)).reshape(1)
    forward = rank_vel >= GROUPS // 2
    sign = jnp.where(forward, 1, -1).astype(jnp.int32).reshape(1)

    layers = (NY, NZ, WIDTH)
    behind, ahead = call(
        first_halo_kernel, "first_halo", ((sign, SMEM), (dist, HBM)),
        (((2,) + layers, jnp.bfloat16, VMEM), ((1,) + layers, jnp.bfloat16, VMEM)),
        scratch=(VMEM((3,) + layers, jnp.float32), DMA((2,))), limit=ALL_VMEM,
    )
    behind = lax.ppermute(behind, both, upwind)
    ahead = lax.ppermute(ahead, both, downwind)

    high, y_quarter, core = rank_vel // 8, rank_vel // 2 % 4, rank_vel % 2
    x_quarter = 2 * high + (core + high) % 2
    rate = lax.dynamic_slice(relax_rate, (BX * x_quarter, BY * y_quarter, 0), (BX, BY, NZ))
    rate = rate.reshape(LAYER, 1)
    own = lax.dynamic_index_in_dim(kinetic_count, rank_space, 1, False)
    live = jnp.arange(CX * LAYER, dtype=jnp.int32)[None, :] < own[:, None]
    listed = jnp.where(live, kinetic_cells, -1)
    slot = jnp.arange(LAYER, dtype=jnp.int32)
    cell = (BX * x_quarter + slot // LINE) * LAYER + (BY * y_quarter * NZ + slot % LINE)
    masks = jnp.any(listed[:, None, :] == cell[None, :, None], axis=2, keepdims=True)
    masks = masks.astype(jnp.float32)

    state = ((CX,) + layers, jnp.float32, VMEM)
    wide = (GROUPS, LAYER, WIDTH)
    halo = (GROUPS + GROUPS // 2, LINE, WIDTH)
    half = jnp.bfloat16
    hidden = VMEM((LAYER, RANK), half)

    f, part = call(
        first_yz_kernel, "first_yz", ((dist, HBM),), (state, state),
        scratch=(DMA((CX // 2,)),), flops=12_000_000,
    )
    (rows,) = call(
        first_x_kernel, "first_x",
        ((sign, SMEM), (speed, SMEM), (f, VMEM), (part, VMEM), (behind, VMEM), (ahead, VMEM)),
        ((wide, half, HBM),), scratch=(VMEM(wide, half), DMA((GROUPS,))), flops=6_000_000,
    )
    gathered = lax.all_to_all(rows, "vel", split_axis=0, concat_axis=0, tiled=True)
    held = (map_a, map_b, map_c) + consts[:3]
    f, up_x, down_x, up_y, down_y = call(
        first_collide_kernel, "first_collide",
        tuple((o, HBM) for o in (gathered,) + held)
        + tuple((o, VMEM) for o in (consts[3], rate, masks[0])),
        ((wide, jnp.float32, HBM),) + ((halo, half, HBM),) * 4,
        scratch=(VMEM(wide, half),) + tuple(VMEM(o.shape, o.dtype) for o in held)
        + (hidden, VMEM((LAYER, RANK), jnp.float32), VMEM((LAYER, RANK), jnp.float32))
        + (VMEM(wide, jnp.float32),) + (VMEM(halo, half),) * 4 + (DMA((22,)), DMA((32,))),
        flops=2_500_000_000, limit=ALL_VMEM,
    )
    y_below = lax.ppermute(up_y, both, y_up)
    y_above = lax.ppermute(down_y, both, y_down)
    x_below = lax.ppermute(up_x, both, x_up)
    x_above = lax.ppermute(down_x, both, x_down)
    f, part = call(
        second_z_kernel, "second_z", ((f, HBM),), ((wide, jnp.float32, VMEM),) * 2,
        scratch=(DMA((GROUPS // 2,)),), flops=6_000_000,
    )
    (moved,) = call(
        second_xy_kernel, "second_xy",
        tuple((o, VMEM) for o in (f, part, x_below, x_above, y_below, y_above)),
        ((wide, jnp.float32, VMEM),), flops=12_000_000,
    )
    (result,) = call(
        second_collide_kernel, "second_collide",
        ((moved, VMEM),) + tuple((o, VMEM) for o in held + (consts[3], rate, masks[1])),
        ((wide, half, VMEM),), scratch=(hidden,), flops=2_500_000_000, limit=12 << 20,
    )
    pieces = lax.all_to_all(result, "vel", split_axis=0, concat_axis=0, tiled=True)
    (out,) = call(
        place_kernel, "place", ((pieces, VMEM),), (((CX,) + layers, jnp.float32, HBM),),
        scratch=(VMEM((CX,) + layers, jnp.float32), DMA((4,))),
    )
    return out


def solution(mesh):
    return jax.shard_map(
        body,
        mesh=mesh,
        in_specs=(
            P("space", None, None, "vel"),
            P("space", None, None),
            P(None, "space"),
            P(),
            P(),
            P(),
            P(),
        ),
        out_specs=P("space", None, None, "vel"),
        check_vma=False,
    )
```

```python
import jax
import jax.numpy as jnp
import numpy as np
from jax import lax
from jax.experimental import pallas as pl
from jax.experimental.pallas import tpu as pltpu
from jax.sharding import PartitionSpec as P

GX = 16
GY = 16
GZ = 8
NV = GX * GY * GZ
RANK = 768
COURANT = 0.1
SPACING = 0.5
COLLIDE = 0.5

CX = 16
NY = 16
NZ = 16
LAYER = NY * NZ
WIDTH = 128
GROUPS = NV // WIDTH
OFFSET = 3.0 / 16.0
BX = 4
BY = 4
LINE = BX * NZ


def tables():
    k = np.arange(NV)
    vx = ((k // (GY * GZ)) - 0.5 * (GX - 1)) * SPACING
    vy = ((k // GZ % GY) - 0.5 * (GY - 1)) * SPACING
    vz = ((k % GZ) - 0.5 * (GZ - 1)) * SPACING
    s = vx * vx + vy * vy + vz * vz
    w = np.exp(-0.5 * s)
    w = w / w.sum()
    sx, sy, sz = (w * vx * vx).sum(), (w * vy * vy).sum(), (w * vz * vz).sum()
    m2, m4 = (w * s).sum(), (w * s * s).sum()
    basis = np.stack([np.ones(NV), vx, vy, vz, s - OFFSET])
    q = np.zeros((5, 5))
    scale = 1.0 / (m4 - m2 * m2)
    thermal = np.zeros(5)
    thermal[0] = (OFFSET - m2) * scale
    thermal[4] = scale
    q[:, 4] = thermal
    q[:, 0] = (OFFSET - m2) * thermal
    q[0, 0] += 1.0
    q[1, 1], q[2, 2], q[3, 3] = 1.0 / sx, 1.0 / sy, 1.0 / sz
    project = np.zeros((NV, 128))
    project[:, :5] = basis.T
    mix = np.zeros((128, 128))
    expand = np.zeros((128, NV))
    for part in range(3):
        mix[:5, 8 * part : 8 * part + 5] = q
        expand[8 * part : 8 * part + 5] = basis
    return (
        project.astype(jnp.bfloat16),
        mix.astype(np.float32),
        expand.astype(jnp.bfloat16),
        w.reshape(1, NV).astype(np.float32),
    )


def minmod_half(a, b):
    return 0.5 * (jnp.maximum(jnp.minimum(a, b), 0.0) + jnp.minimum(jnp.maximum(a, b), 0.0))


C_VMEM = 12 << 20
HBM = pltpu.HBM
VMEM = pltpu.VMEM
SMEM = pltpu.SMEM
DMA = pltpu.SemaphoreType.DMA


def call(kernel, name, operands, outs, scratch=(), flops=0, limit=8 << 20):
    shapes = [jax.ShapeDtypeStruct(shape, dtype) for shape, dtype, _ in outs]
    arrays = [o for o, _ in operands]
    moved = sum(o.size * o.dtype.itemsize for o in arrays + shapes)
    return pl.pallas_call(
        kernel,
        out_shape=tuple(shapes),
        in_specs=[pl.BlockSpec(memory_space=space) for _, space in operands],
        out_specs=tuple(pl.BlockSpec(memory_space=space) for _, _, space in outs),
        scratch_shapes=list(scratch),
        compiler_params=pltpu.CompilerParams(vmem_limit_bytes=limit),
        cost_estimate=pl.CostEstimate(flops=flops, bytes_accessed=moved, transcendentals=0),
        name=name,
    )(*arrays)


def speeds_yz():
    lane = lax.broadcasted_iota(jnp.int32, (NZ, WIDTH), 1)
    along_y = (lane >> 3).astype(jnp.float32) - 0.5 * (GY - 1)
    along_z = (lane & (GZ - 1)).astype(jnp.float32) - 0.5 * (GZ - 1)
    return along_y * (SPACING * COURANT), along_z * (SPACING * COURANT)


def flux_change_z(f, uz, z_up):
    dz = pltpu.roll(f, NZ - 1, 0) - f
    slope = minmod_half(pltpu.roll(dz, 1, 0), dz)
    down = pltpu.roll(f - slope, NZ - 1, 0)
    flux = jnp.where(z_up, f + slope, down)
    return uz * (flux - pltpu.roll(flux, 1, 0))


def edges(before, here, after):
    slope = minmod_half(here - before, after - here)
    return here + slope, here - slope


def upwind_face(before, here, after):
    return here + minmod_half(here - before, after - here)


def first_halo_kernel(vel_ref, space_ref, dist_ref, behind_ref, ahead_ref):
    forward = vel_ref[0] >= GROUPS // 2
    start = jnp.where(forward, CX - 2, 0)
    for i in range(2):
        behind_ref[i] = dist_ref[start + i].astype(jnp.bfloat16)
    ahead_ref[0] = dist_ref[jnp.where(forward, 0, CX - 1)].astype(jnp.bfloat16)


def first_yz_kernel(f_ref, part_ref):
    uy, uz = speeds_yz()
    y_up = uy > 0.0
    z_up = uz > 0.0

    def layer(x, carry):
        def at(y):
            return f_ref[x, y % NY]

        up, _ = edges(at(-2), at(-1), at(0))
        next_up, next_down = edges(at(-1), at(0), at(1))
        flux_before = jnp.where(y_up, up, next_down)
        for y in range(NY):
            up = next_up
            next_up, next_down = edges(at(y), at(y + 1), at(y + 2))
            flux = jnp.where(y_up, up, next_down)
            here = at(y)
            part_ref[x, y] = here - uy * (flux - flux_before) - flux_change_z(here, uz, z_up)
            flux_before = flux
        return carry

    lax.fori_loop(0, CX, layer, 0)


def first_x_kernel(vel_ref, f_ref, part_ref, behind_ref, ahead_ref, rows_ref):
    rank = vel_ref[0]
    forward = rank >= GROUPS // 2
    ux = jnp.abs(rank.astype(jnp.float32) - 0.5 * (GX - 1)) * (SPACING * COURANT)
    layers = [jnp.where(forward, k, CX - 1 - k) for k in range(CX)]
    starts = [(x % BX) * LINE for x in layers[:BX]]
    owners = []
    for k in range(4):
        quarter = jnp.where(forward, k, 3 - k)
        high = quarter // 2
        owners.append(high * (GROUPS // 2) + (quarter + high) % 2)

    def line(quarter, y):
        inner = y * NZ
        y = quarter * BY + y

        def at(k):
            if k == -2:
                return behind_ref[jnp.where(forward, 0, 1), y].astype(jnp.float32)
            if k == -1:
                return behind_ref[jnp.where(forward, 1, 0), y].astype(jnp.float32)
            if k == CX:
                return ahead_ref[0, y].astype(jnp.float32)
            return f_ref[layers[k], y]

        face_before = upwind_face(at(-2), at(-1), at(0))
        for k in range(CX):
            face = upwind_face(at(k - 1), at(k), at(k + 1))
            result = part_ref[layers[k], y] - ux * (face - face_before)
            face_before = face
            start = pl.multiple_of(starts[k % BX] + inner, NZ)
            target = owners[k // BX] + quarter * 2
            rows_ref[target, pl.ds(start, NZ), :] = result.astype(jnp.bfloat16)

    def lines(quarter, carry):
        def one(y, inside):
            line(quarter, y)
            return inside

        lax.fori_loop(0, BY, one, 0)
        return carry

    lax.fori_loop(0, NY // BY, lines, 0)


def cell_facts(step, vel_ref, space_ref, count_ref, cells_ref, rate_ref):
    rank = vel_ref[0]
    high, y_quarter, core = rank // 8, rank // 2 % 4, rank % 2
    x_quarter = 2 * high + (core + high) % 2
    count = count_ref[step, space_ref[0]]
    shape = (LAYER, WIDTH)
    slot = lax.broadcasted_iota(jnp.int32, shape, 0)
    cell = (
        (BX * x_quarter + (slot >> 6)) * LAYER + BY * NZ * y_quarter + (slot & (LINE - 1))
    )
    lane = lax.broadcasted_iota(jnp.int32, (1, WIDTH), 1)
    found = jnp.zeros(shape, jnp.float32)
    for i in range(CX * LAYER // WIDTH):
        part = cells_ref[step : step + 1, WIDTH * i : WIDTH * (i + 1)]
        part = jnp.where(lane + WIDTH * i < count, part, -1)
        found = jnp.where(cell == part, 1.0, found)
    kinetic = jnp.broadcast_to(jnp.max(found, axis=1, keepdims=True), shape) > 0.0
    diagonal = lax.broadcasted_iota(jnp.int32, (NZ, NZ), 0) == lax.broadcasted_iota(
        jnp.int32, (NZ, NZ), 1
    )
    columns = []
    for x in range(BX):
        for y in range(BY):
            line = rate_ref[BX * x_quarter + x, pl.ds(BY * y_quarter + y, 1), :]
            column = jnp.sum(jnp.where(diagonal, line, 0.0), axis=1, keepdims=True)
            columns.append(jnp.broadcast_to(column, (NZ, WIDTH)))
    return kinetic, jnp.concatenate(columns, axis=0)


def collide(rows, a_ref, b_ref, c_ref, project_ref, mix_ref, expand_ref, w_ref, hidden_ref):
    moments = jnp.dot(rows, project_ref[...], preferred_element_type=jnp.float32)
    coeffs = jnp.dot(
        moments, mix_ref[...], precision=lax.Precision.HIGHEST, preferred_element_type=jnp.float32
    )
    lane = lax.broadcasted_iota(jnp.int32, coeffs.shape, 1)
    high = coeffs.astype(jnp.bfloat16).astype(jnp.float32)
    rest = coeffs - high
    middle = rest.astype(jnp.bfloat16).astype(jnp.float32)
    split = jnp.where(lane < 8, high, jnp.where(lane < 16, middle, rest - middle))
    split = split.astype(jnp.bfloat16)
    for n in range(RANK // 256):
        cols = slice(256 * n, 256 * (n + 1))
        first = jnp.dot(rows, a_ref[:, cols], preferred_element_type=jnp.float32)
        second = jnp.dot(rows, b_ref[:, cols], preferred_element_type=jnp.float32)
        hidden_ref[:, cols] = (first * second).astype(jnp.bfloat16)
    hidden = hidden_ref[...]
    for n in range(NV // 256):
        cols = slice(256 * n, 256 * (n + 1))
        collision = jnp.dot(hidden, c_ref[:, cols], preferred_element_type=jnp.float32)
        collision = collision.astype(jnp.bfloat16).astype(jnp.float32)
        poly = jnp.dot(split, expand_ref[:, cols], preferred_element_type=jnp.float32)
        equilibrium = poly * w_ref[:, cols]
        for half in range(2):
            part = slice(WIDTH * half, WIDTH * (half + 1))
            yield 2 * n + half, collision[:, part], equilibrium[:, part]


def first_collide_kernel(
    vel_ref, space_ref, count_ref, rows_ref, a_ref, b_ref, c_ref, project_ref, mix_ref,
    expand_ref, w_ref, cells_ref, rate_ref,
    f_ref, x_up_ref, x_down_ref, y_up_ref, y_down_ref, hidden_ref,
):
    rows = jnp.concatenate([rows_ref[g] for g in range(GROUPS)], axis=1)
    kinetic, rate = cell_facts(0, vel_ref, space_ref, count_ref, cells_ref, rate_ref)
    half = GROUPS // 2
    low_lane = lax.broadcasted_iota(jnp.int32, (NZ, WIDTH), 1) < WIDTH // 2
    for g, collision, equilibrium in collide(
        rows, a_ref, b_ref, c_ref, project_ref, mix_ref, expand_ref, w_ref, hidden_ref
    ):
        moved = rows_ref[g].astype(jnp.float32)
        change = jnp.where(kinetic, COLLIDE * collision, rate * (equilibrium - moved))
        result = moved + change
        f_ref[g] = result
        sent = result.astype(jnp.bfloat16)
        x_up_ref[g] = sent[3 * LINE : 4 * LINE]
        x_down_ref[g] = sent[0:LINE]
        if g >= half:
            x_up_ref[g + half] = sent[2 * LINE : 3 * LINE]
        else:
            x_down_ref[g + GROUPS] = sent[LINE : 2 * LINE]
        for x in range(BX):
            here = slice(NZ * x, NZ * (x + 1))
            y_down_ref[g, here] = sent[LINE * x : LINE * x + NZ]
            y_up_ref[g, here] = sent[LINE * x + 3 * NZ : LINE * x + 4 * NZ]
            if g >= half:
                low = g - half
                second = slice(LINE * x + NZ, LINE * x + 2 * NZ)
                third = slice(LINE * x + 2 * NZ, LINE * x + 3 * NZ)
                y_up_ref[GROUPS + low, here] = jnp.where(
                    low_lane, pltpu.roll(f_ref[low, third], WIDTH // 2, 1), result[third]
                ).astype(jnp.bfloat16)
                y_down_ref[GROUPS + low, here] = jnp.where(
                    low_lane, f_ref[low, second], pltpu.roll(result[second], WIDTH // 2, 1)
                ).astype(jnp.bfloat16)


def second_z_kernel(f_ref, part_ref):
    _, uz = speeds_yz()
    z_up = uz > 0.0

    def group(g, carry):
        for c in range(BX * BY):
            here = slice(NZ * c, NZ * (c + 1))
            f = f_ref[g, here]
            part_ref[g, here] = f - flux_change_z(f, uz, z_up)
        return carry

    lax.fori_loop(0, GROUPS, group, 0)


def second_xy_kernel(
    f_ref, part_ref, x_below_ref, x_above_ref, y_below_ref, y_above_ref, moved_ref
):
    uy, _ = speeds_yz()
    y_up = uy > 0.0
    half = GROUPS // 2

    def wide(ref, g, i):
        return ref[g, NZ * i : NZ * (i + 1)].astype(jnp.float32)

    def group(pair, upward):
        g = pair + half if upward else pair
        extra = pair + GROUPS
        ux = (g.astype(jnp.float32) - 0.5 * (GX - 1)) * (SPACING * COURANT)
        ux = ux if upward else -ux
        for y in range(BY):
            behind, ahead = (x_below_ref, x_above_ref) if upward else (x_above_ref, x_below_ref)

            def at_x(k):
                if k == -2:
                    return wide(behind, extra, y)
                if k == -1:
                    return wide(behind, g, y)
                if k == BX:
                    return wide(ahead, g, y)
                x = k if upward else BX - 1 - k
                return f_ref[g, LINE * x + NZ * y : LINE * x + NZ * (y + 1)]

            face_before = upwind_face(at_x(-2), at_x(-1), at_x(0))
            for k in range(BX):
                x = k if upward else BX - 1 - k
                face = upwind_face(at_x(k - 1), at_x(k), at_x(k + 1))
                here = slice(LINE * x + NZ * y, LINE * x + NZ * (y + 1))
                moved_ref[g, here] = part_ref[g, here] - ux * (face - face_before)
                face_before = face
        for x in range(BX):

            def at_y(y):
                if y == -2:
                    below = wide(y_below_ref, extra, x)
                    return below if upward else pltpu.roll(below, WIDTH // 2, 1)
                if y == -1:
                    return wide(y_below_ref, g, x)
                if y == BY:
                    return wide(y_above_ref, g, x)
                if y == BY + 1:
                    above = wide(y_above_ref, extra, x)
                    return pltpu.roll(above, WIDTH // 2, 1) if upward else above
                return f_ref[g, LINE * x + NZ * y : LINE * x + NZ * (y + 1)]

            up, _ = edges(at_y(-2), at_y(-1), at_y(0))
            next_up, next_down = edges(at_y(-1), at_y(0), at_y(1))
            flux_before = jnp.where(y_up, up, next_down)
            for y in range(BY):
                up = next_up
                next_up, next_down = edges(at_y(y), at_y(y + 1), at_y(y + 2))
                flux = jnp.where(y_up, up, next_down)
                here = slice(LINE * x + NZ * y, LINE * x + NZ * (y + 1))
                moved_ref[g, here] = moved_ref[g, here] - uy * (flux - flux_before)
                flux_before = flux

    def downwards(pair, carry):
        group(pair, False)
        return carry

    def upwards(pair, carry):
        group(pair, True)
        return carry

    lax.fori_loop(0, half, downwards, 0)
    lax.fori_loop(0, half, upwards, 0)


def second_collide_kernel(
    vel_ref, space_ref, count_ref, moved_ref, a_ref, b_ref, c_ref, project_ref, mix_ref,
    expand_ref, w_ref, cells_ref, rate_ref, out_ref, hidden_ref,
):
    rows = jnp.concatenate([moved_ref[g].astype(jnp.bfloat16) for g in range(GROUPS)], axis=1)
    kinetic, rate = cell_facts(1, vel_ref, space_ref, count_ref, cells_ref, rate_ref)
    for g, collision, equilibrium in collide(
        rows, a_ref, b_ref, c_ref, project_ref, mix_ref, expand_ref, w_ref, hidden_ref
    ):
        moved = moved_ref[g]
        change = jnp.where(kinetic, COLLIDE * collision, rate * (equilibrium - moved))
        out_ref[g] = (moved + change).astype(jnp.bfloat16)


def place_kernel(in_ref, out_hbm, out_ref, sems):
    stores = []
    for quarter in range(4):
        high = quarter // 2
        core = (quarter % 2) ^ high
        for x in range(BX):
            for y_quarter in range(4):
                for y in range(BY):
                    c = LINE * x + NZ * y
                    out_ref[BX * quarter + x, BY * y_quarter + y] = in_ref[
                        high * (GROUPS // 2) + y_quarter * 2 + core, c : c + NZ
                    ].astype(jnp.float32)
        part = slice(BX * quarter, BX * (quarter + 1))
        stores.append(pltpu.make_async_copy(out_ref.at[part], out_hbm.at[part], sems.at[quarter]))
        stores[-1].start()
    for store in stores:
        store.wait()


def device_of(space, high, x, core):
    return (space * 2 + high) * 8 + x * 2 + core


def steps_of(slabs):
    upwind, downwind, x_up, y_up = [], [], [], []
    for space in range(slabs):
        for high in range(2):
            for x in range(4):
                for core in range(2):
                    me = device_of(space, high, x, core)
                    after = device_of((space + 1) % slabs, high, x, core)
                    before = device_of((space - 1) % slabs, high, x, core)
                    upwind.append((me, after if high else before))
                    downwind.append((me, before if high else after))
                    quarter = 2 * high + (core ^ high)
                    next_slab = (space + (quarter == 3)) % slabs
                    quarter = (quarter + 1) % 4
                    x_up.append(
                        (me, device_of(next_slab, quarter // 2, x, (quarter % 2) ^ (quarter // 2)))
                    )
                    y_up.append((me, device_of(space, high, (x + 1) % 4, core)))
    back = lambda pairs: [(target, source) for source, target in pairs]
    return upwind, downwind, x_up, back(x_up), y_up, back(y_up)


def body(dist, relax_rate, kinetic_cells, kinetic_count, map_a, map_b, map_c):
    vel = (lax.axis_index("vel").astype(jnp.int32).reshape(1), SMEM)
    space = (lax.axis_index("space").astype(jnp.int32).reshape(1), SMEM)
    both = ("space", "vel")
    upwind, downwind, x_up, x_down, y_up, y_down = steps_of(lax.axis_size("space"))
    project, mix, expand, w = tables()
    consts = (jnp.asarray(project), jnp.asarray(mix), jnp.asarray(expand), jnp.asarray(w))
    layers = (NY, NZ, WIDTH)
    behind, ahead = call(
        first_halo_kernel, "first_halo", (vel, space, (dist, VMEM)),
        (((2,) + layers, jnp.bfloat16, VMEM), ((1,) + layers, jnp.bfloat16, VMEM)),
    )
    behind = lax.ppermute(behind, both, upwind)
    ahead = lax.ppermute(ahead, both, downwind)

    state = ((CX,) + layers, jnp.float32, VMEM)
    wide = (GROUPS, LAYER, WIDTH)
    halo = (GROUPS + GROUPS // 2, LINE, WIDTH)
    half = jnp.bfloat16
    hidden = VMEM((LAYER, RANK), half)

    (part,) = call(first_yz_kernel, "first_yz", ((dist, VMEM),), (state,), flops=12_000_000)
    (rows,) = call(
        first_x_kernel, "first_x", (vel,) + tuple((o, VMEM) for o in (dist, part, behind, ahead)),
        ((wide, half, VMEM),), flops=6_000_000,
    )
    gathered = lax.all_to_all(rows, "vel", split_axis=0, concat_axis=0, tiled=True)
    facts = (vel, space, (kinetic_count, SMEM))
    held = tuple((o, VMEM) for o in (map_a, map_b, map_c) + consts + (kinetic_cells, relax_rate))
    f, up_x, down_x, up_y, down_y = call(
        first_collide_kernel, "first_collide", facts + ((gathered, VMEM),) + held,
        ((wide, jnp.float32, VMEM),) + ((halo, half, VMEM),) * 4,
        scratch=(hidden,), flops=2_500_000_000, limit=C_VMEM,
    )
    y_below = lax.ppermute(up_y, both, y_up)
    y_above = lax.ppermute(down_y, both, y_down)
    x_below = lax.ppermute(up_x, both, x_up)
    x_above = lax.ppermute(down_x, both, x_down)
    (part,) = call(
        second_z_kernel, "second_z", ((f, VMEM),), ((wide, jnp.float32, VMEM),), flops=6_000_000
    )
    (moved,) = call(
        second_xy_kernel, "second_xy",
        tuple((o, VMEM) for o in (f, part, x_below, x_above, y_below, y_above)),
        ((wide, jnp.float32, VMEM),), flops=12_000_000,
    )
    (result,) = call(
        second_collide_kernel, "second_collide", facts + ((moved, VMEM),) + held,
        ((wide, half, VMEM),), scratch=(hidden,), flops=2_500_000_000, limit=C_VMEM,
    )
    pieces = lax.all_to_all(result, "vel", split_axis=0, concat_axis=0, tiled=True)
    (out,) = call(
        place_kernel, "place", ((pieces, VMEM),), (((CX,) + layers, jnp.float32, HBM),),
        scratch=(VMEM((CX,) + layers, jnp.float32), DMA((4,))),
    )
    return out


def solution(mesh):
    return jax.shard_map(
        body,
        mesh=mesh,
        in_specs=(
            P("space", None, None, "vel"),
            P("space", None, None),
            P(None, "space"),
            P(),
            P(),
            P(),
            P(),
        ),
        out_specs=P("space", None, None, "vel"),
        check_vma=False,
    )
```

```python
import jax
import jax.numpy as jnp
import numpy as np
from jax import lax
from jax.experimental import pallas as pl
from jax.experimental.pallas import tpu as pltpu
from jax.sharding import PartitionSpec as P

GX = 16
GY = 16
GZ = 8
NV = GX * GY * GZ
RANK = 768
COURANT = 0.1
SPACING = 0.5
COLLIDE = 0.5

CX = 16
NY = 16
NZ = 16
LAYER = NY * NZ
WIDTH = 128
GROUPS = NV // WIDTH
OFFSET = 3.0 / 16.0
BX = 4
BY = 4
LINE = BX * NZ


def tables():
    k = np.arange(NV)
    vx = ((k // (GY * GZ)) - 0.5 * (GX - 1)) * SPACING
    vy = ((k // GZ % GY) - 0.5 * (GY - 1)) * SPACING
    vz = ((k % GZ) - 0.5 * (GZ - 1)) * SPACING
    s = vx * vx + vy * vy + vz * vz
    w = np.exp(-0.5 * s)
    w = w / w.sum()
    sx, sy, sz = (w * vx * vx).sum(), (w * vy * vy).sum(), (w * vz * vz).sum()
    m2, m4 = (w * s).sum(), (w * s * s).sum()
    basis = np.stack([np.ones(NV), vx, vy, vz, s - OFFSET])
    q = np.zeros((5, 5))
    scale = 1.0 / (m4 - m2 * m2)
    thermal = np.zeros(5)
    thermal[0] = (OFFSET - m2) * scale
    thermal[4] = scale
    q[:, 4] = thermal
    q[:, 0] = (OFFSET - m2) * thermal
    q[0, 0] += 1.0
    q[1, 1], q[2, 2], q[3, 3] = 1.0 / sx, 1.0 / sy, 1.0 / sz
    project = np.zeros((NV, 128))
    project[:, :5] = basis.T
    mix = np.zeros((128, 128))
    expand = np.zeros((128, NV))
    for part in range(3):
        mix[:5, 8 * part : 8 * part + 5] = q
        expand[8 * part : 8 * part + 5] = basis
    return (
        project.astype(jnp.bfloat16),
        mix.astype(np.float32),
        expand.astype(jnp.bfloat16),
        w.reshape(1, NV).astype(np.float32),
    )


def minmod_half(a, b):
    return 0.5 * (jnp.maximum(jnp.minimum(a, b), 0.0) + jnp.minimum(jnp.maximum(a, b), 0.0))


C_VMEM = 12 << 20
HBM = pltpu.HBM
VMEM = pltpu.VMEM
SMEM = pltpu.SMEM
DMA = pltpu.SemaphoreType.DMA


def call(kernel, name, operands, outs, scratch=(), flops=0, limit=8 << 20):
    shapes = [jax.ShapeDtypeStruct(shape, dtype) for shape, dtype, _ in outs]
    arrays = [o for o, _ in operands]
    moved = sum(o.size * o.dtype.itemsize for o in arrays + shapes)
    return pl.pallas_call(
        kernel,
        out_shape=tuple(shapes),
        in_specs=[pl.BlockSpec(memory_space=space) for _, space in operands],
        out_specs=tuple(pl.BlockSpec(memory_space=space) for _, _, space in outs),
        scratch_shapes=list(scratch),
        compiler_params=pltpu.CompilerParams(vmem_limit_bytes=limit),
        cost_estimate=pl.CostEstimate(flops=flops, bytes_accessed=moved, transcendentals=0),
        name=name,
    )(*arrays)


def speeds_yz():
    lane = lax.broadcasted_iota(jnp.int32, (NZ, WIDTH), 1)
    along_y = (lane >> 3).astype(jnp.float32) - 0.5 * (GY - 1)
    along_z = (lane & (GZ - 1)).astype(jnp.float32) - 0.5 * (GZ - 1)
    return along_y * (SPACING * COURANT), along_z * (SPACING * COURANT)


def flux_change_z(f, uz, z_up):
    dz = pltpu.roll(f, NZ - 1, 0) - f
    slope = minmod_half(pltpu.roll(dz, 1, 0), dz)
    down = pltpu.roll(f - slope, NZ - 1, 0)
    flux = jnp.where(z_up, f + slope, down)
    return uz * (flux - pltpu.roll(flux, 1, 0))


def edges(before, here, after):
    slope = minmod_half(here - before, after - here)
    return here + slope, here - slope


def upwind_face(before, here, after):
    return here + minmod_half(here - before, after - here)


def first_halo_kernel(vel_ref, space_ref, dist_ref, behind_ref, ahead_ref):
    forward = vel_ref[0] >= GROUPS // 2
    start = jnp.where(forward, CX - 2, 0)
    for i in range(2):
        behind_ref[i] = dist_ref[start + i].astype(jnp.bfloat16)
    ahead_ref[0] = dist_ref[jnp.where(forward, 0, CX - 1)].astype(jnp.bfloat16)


def quarters(rank):
    high, core = rank // 8, rank % 2
    return 2 * high + (core + high) % 2, rank // 2 % 4


def kinetic_cells_of(step, vel_ref, space_ref, count_ref, cells_ref):
    x_quarter, y_quarter = quarters(vel_ref[0])
    count = count_ref[step, space_ref[0]]
    shape = (LAYER, WIDTH)
    slot = lax.broadcasted_iota(jnp.int32, shape, 0)
    cell = (
        (BX * x_quarter + (slot >> 6)) * LAYER + BY * NZ * y_quarter + (slot & (LINE - 1))
    )
    lane = lax.broadcasted_iota(jnp.int32, (1, WIDTH), 1)
    found = jnp.zeros(shape, jnp.float32)
    for i in range(CX * LAYER // WIDTH):
        part = cells_ref[step : step + 1, WIDTH * i : WIDTH * (i + 1)]
        part = jnp.where(lane + WIDTH * i < count, part, -1)
        found = jnp.where(cell == part, 1.0, found)
    return jnp.broadcast_to(jnp.max(found, axis=1, keepdims=True), shape)


def rates_of(vel_ref, rate_ref):
    x_quarter, y_quarter = quarters(vel_ref[0])
    diagonal = lax.broadcasted_iota(jnp.int32, (NZ, NZ), 0) == lax.broadcasted_iota(
        jnp.int32, (NZ, NZ), 1
    )
    columns = []
    for x in range(BX):
        for y in range(BY):
            line = rate_ref[BX * x_quarter + x, pl.ds(BY * y_quarter + y, 1), :]
            column = jnp.sum(jnp.where(diagonal, line, 0.0), axis=1, keepdims=True)
            columns.append(jnp.broadcast_to(column, (NZ, WIDTH)))
    return jnp.concatenate(columns, axis=0)


def first_yz_kernel(f_ref, part_ref):
    uy, uz = speeds_yz()
    y_up = uy > 0.0
    z_up = uz > 0.0

    def layer(x, carry):
        def at(y):
            return f_ref[x, y % NY]

        up, _ = edges(at(-2), at(-1), at(0))
        next_up, next_down = edges(at(-1), at(0), at(1))
        flux_before = jnp.where(y_up, up, next_down)
        for y in range(NY):
            up = next_up
            next_up, next_down = edges(at(y), at(y + 1), at(y + 2))
            flux = jnp.where(y_up, up, next_down)
            here = at(y)
            part_ref[x, y] = here - uy * (flux - flux_before) - flux_change_z(here, uz, z_up)
            flux_before = flux
        return carry

    lax.fori_loop(0, CX, layer, 0)


def first_x_kernel(vel_ref, f_ref, part_ref, behind_ref, ahead_ref, rows_ref):
    rank = vel_ref[0]
    forward = rank >= GROUPS // 2
    ux = jnp.abs(rank.astype(jnp.float32) - 0.5 * (GX - 1)) * (SPACING * COURANT)
    layers = [jnp.where(forward, k, CX - 1 - k) for k in range(CX)]
    starts = [(x % BX) * LINE for x in layers[:BX]]
    owners = []
    for k in range(4):
        quarter = jnp.where(forward, k, 3 - k)
        high = quarter // 2
        owners.append(high * (GROUPS // 2) + (quarter + high) % 2)

    def line(quarter, y):
        inner = y * NZ
        y = quarter * BY + y

        def at(k):
            if k == -2:
                return behind_ref[jnp.where(forward, 0, 1), y].astype(jnp.float32)
            if k == -1:
                return behind_ref[jnp.where(forward, 1, 0), y].astype(jnp.float32)
            if k == CX:
                return ahead_ref[0, y].astype(jnp.float32)
            return f_ref[layers[k], y]

        face_before = upwind_face(at(-2), at(-1), at(0))
        for k in range(CX):
            face = upwind_face(at(k - 1), at(k), at(k + 1))
            result = part_ref[layers[k], y] - ux * (face - face_before)
            face_before = face
            start = pl.multiple_of(starts[k % BX] + inner, NZ)
            target = owners[k // BX] + quarter * 2
            rows_ref[target, pl.ds(start, NZ), :] = result.astype(jnp.bfloat16)

    def lines(quarter, carry):
        def one(y, inside):
            line(quarter, y)
            return inside

        lax.fori_loop(0, BY, one, 0)
        return carry

    lax.fori_loop(0, NY // BY, lines, 0)


def collide(rows, a_ref, b_ref, c_ref, project_ref, mix_ref, expand_ref, w_ref, hidden_ref):
    moments = jnp.dot(rows, project_ref[...], preferred_element_type=jnp.float32)
    coeffs = jnp.dot(
        moments, mix_ref[...], precision=lax.Precision.HIGHEST, preferred_element_type=jnp.float32
    )
    lane = lax.broadcasted_iota(jnp.int32, coeffs.shape, 1)
    high = coeffs.astype(jnp.bfloat16).astype(jnp.float32)
    rest = coeffs - high
    middle = rest.astype(jnp.bfloat16).astype(jnp.float32)
    split = jnp.where(lane < 8, high, jnp.where(lane < 16, middle, rest - middle))
    split = split.astype(jnp.bfloat16)
    for n in range(RANK // 256):
        cols = slice(256 * n, 256 * (n + 1))
        first = jnp.dot(rows, a_ref[:, cols], preferred_element_type=jnp.float32)
        second = jnp.dot(rows, b_ref[:, cols], preferred_element_type=jnp.float32)
        hidden_ref[:, cols] = (first * second).astype(jnp.bfloat16)
    hidden = hidden_ref[...]
    for n in range(NV // 256):
        cols = slice(256 * n, 256 * (n + 1))
        collision = jnp.dot(hidden, c_ref[:, cols], preferred_element_type=jnp.float32)
        collision = collision.astype(jnp.bfloat16).astype(jnp.float32)
        poly = jnp.dot(split, expand_ref[:, cols], preferred_element_type=jnp.float32)
        equilibrium = poly * w_ref[:, cols]
        for half in range(2):
            part = slice(WIDTH * half, WIDTH * (half + 1))
            yield 2 * n + half, collision[:, part], equilibrium[:, part]


def first_collide_kernel(
    vel_ref, space_ref, count_ref, rows_ref, cells_ref, rate_ref, a_ref, b_ref, c_ref,
    project_ref, mix_ref, expand_ref, w_ref,
    f_ref, rates_ref, x_up_ref, x_down_ref, y_up_ref, y_down_ref, hidden_ref,
):
    rows = jnp.concatenate([rows_ref[g] for g in range(GROUPS)], axis=1)
    kinetic = kinetic_cells_of(0, vel_ref, space_ref, count_ref, cells_ref) > 0.0
    rate = rates_of(vel_ref, rate_ref)
    rates_ref[...] = rate
    half = GROUPS // 2
    low_lane = lax.broadcasted_iota(jnp.int32, (NZ, WIDTH), 1) < WIDTH // 2
    for g, collision, equilibrium in collide(
        rows, a_ref, b_ref, c_ref, project_ref, mix_ref, expand_ref, w_ref, hidden_ref
    ):
        moved = rows_ref[g].astype(jnp.float32)
        change = jnp.where(kinetic, COLLIDE * collision, rate * (equilibrium - moved))
        result = moved + change
        f_ref[g] = result
        sent = result.astype(jnp.bfloat16)
        x_up_ref[g] = sent[3 * LINE : 4 * LINE]
        x_down_ref[g] = sent[0:LINE]
        if g >= half:
            x_up_ref[g + half] = sent[2 * LINE : 3 * LINE]
        else:
            x_down_ref[g + GROUPS] = sent[LINE : 2 * LINE]
        for x in range(BX):
            here = slice(NZ * x, NZ * (x + 1))
            y_down_ref[g, here] = sent[LINE * x : LINE * x + NZ]
            y_up_ref[g, here] = sent[LINE * x + 3 * NZ : LINE * x + 4 * NZ]
            if g >= half:
                low = g - half
                second = slice(LINE * x + NZ, LINE * x + 2 * NZ)
                third = slice(LINE * x + 2 * NZ, LINE * x + 3 * NZ)
                y_up_ref[GROUPS + low, here] = jnp.where(
                    low_lane, pltpu.roll(f_ref[low, third], WIDTH // 2, 1), result[third]
                ).astype(jnp.bfloat16)
                y_down_ref[GROUPS + low, here] = jnp.where(
                    low_lane, f_ref[low, second], pltpu.roll(result[second], WIDTH // 2, 1)
                ).astype(jnp.bfloat16)


def second_z_kernel(vel_ref, space_ref, count_ref, f_ref, cells_ref, part_ref, mask_ref):
    mask_ref[...] = kinetic_cells_of(1, vel_ref, space_ref, count_ref, cells_ref)
    _, uz = speeds_yz()
    z_up = uz > 0.0

    def group(g, carry):
        for c in range(BX * BY):
            here = slice(NZ * c, NZ * (c + 1))
            f = f_ref[g, here]
            part_ref[g, here] = f - flux_change_z(f, uz, z_up)
        return carry

    lax.fori_loop(0, GROUPS, group, 0)


def second_xy_kernel(
    f_ref, part_ref, y_below_ref, y_above_ref, x_below_ref, x_above_ref, moved_ref
):
    uy, _ = speeds_yz()
    y_up = uy > 0.0
    half = GROUPS // 2

    def wide(ref, g, i):
        return ref[g, NZ * i : NZ * (i + 1)].astype(jnp.float32)

    def group(pair, upward):
        g = pair + half if upward else pair
        extra = pair + GROUPS
        ux = (g.astype(jnp.float32) - 0.5 * (GX - 1)) * (SPACING * COURANT)
        ux = ux if upward else -ux
        for y in range(BY):
            behind, ahead = (x_below_ref, x_above_ref) if upward else (x_above_ref, x_below_ref)

            def at_x(k):
                if k == -2:
                    return wide(behind, extra, y)
                if k == -1:
                    return wide(behind, g, y)
                if k == BX:
                    return wide(ahead, g, y)
                x = k if upward else BX - 1 - k
                return f_ref[g, LINE * x + NZ * y : LINE * x + NZ * (y + 1)]

            face_before = upwind_face(at_x(-2), at_x(-1), at_x(0))
            for k in range(BX):
                x = k if upward else BX - 1 - k
                face = upwind_face(at_x(k - 1), at_x(k), at_x(k + 1))
                here = slice(LINE * x + NZ * y, LINE * x + NZ * (y + 1))
                moved_ref[g, here] = part_ref[g, here] - ux * (face - face_before)
                face_before = face
        for x in range(BX):

            def at_y(y):
                if y == -2:
                    below = wide(y_below_ref, extra, x)
                    return below if upward else pltpu.roll(below, WIDTH // 2, 1)
                if y == -1:
                    return wide(y_below_ref, g, x)
                if y == BY:
                    return wide(y_above_ref, g, x)
                if y == BY + 1:
                    above = wide(y_above_ref, extra, x)
                    return pltpu.roll(above, WIDTH // 2, 1) if upward else above
                return f_ref[g, LINE * x + NZ * y : LINE * x + NZ * (y + 1)]

            up, _ = edges(at_y(-2), at_y(-1), at_y(0))
            next_up, next_down = edges(at_y(-1), at_y(0), at_y(1))
            flux_before = jnp.where(y_up, up, next_down)
            for y in range(BY):
                up = next_up
                next_up, next_down = edges(at_y(y), at_y(y + 1), at_y(y + 2))
                flux = jnp.where(y_up, up, next_down)
                here = slice(LINE * x + NZ * y, LINE * x + NZ * (y + 1))
                moved_ref[g, here] = moved_ref[g, here] - uy * (flux - flux_before)
                flux_before = flux

    def downwards(pair, carry):
        group(pair, False)
        return carry

    def upwards(pair, carry):
        group(pair, True)
        return carry

    lax.fori_loop(0, half, downwards, 0)
    lax.fori_loop(0, half, upwards, 0)


def second_collide_kernel(
    moved_ref, mask_ref, rates_ref, a_ref, b_ref, c_ref, project_ref, mix_ref, expand_ref, w_ref,
    out_ref, hidden_ref,
):
    rows = jnp.concatenate([moved_ref[g].astype(jnp.bfloat16) for g in range(GROUPS)], axis=1)
    kinetic = mask_ref[...] > 0.0
    rate = rates_ref[...]
    for g, collision, equilibrium in collide(
        rows, a_ref, b_ref, c_ref, project_ref, mix_ref, expand_ref, w_ref, hidden_ref
    ):
        moved = moved_ref[g]
        change = jnp.where(kinetic, COLLIDE * collision, rate * (equilibrium - moved))
        out_ref[g] = (moved + change).astype(jnp.bfloat16)


def place_kernel(in_ref, out_hbm, out_ref, sems):
    stores = []
    for quarter in range(4):
        high = quarter // 2
        core = (quarter % 2) ^ high
        for x in range(BX):
            for y_quarter in range(4):
                for y in range(BY):
                    c = LINE * x + NZ * y
                    out_ref[BX * quarter + x, BY * y_quarter + y] = in_ref[
                        high * (GROUPS // 2) + y_quarter * 2 + core, c : c + NZ
                    ].astype(jnp.float32)
        part = slice(BX * quarter, BX * (quarter + 1))
        stores.append(pltpu.make_async_copy(out_ref.at[part], out_hbm.at[part], sems.at[quarter]))
        stores[-1].start()
    for store in stores:
        store.wait()


def device_of(space, high, x, core):
    return (space * 2 + high) * 8 + x * 2 + core


def steps_of(slabs):
    upwind, downwind, x_up, y_up = [], [], [], []
    for space in range(slabs):
        for high in range(2):
            for x in range(4):
                for core in range(2):
                    me = device_of(space, high, x, core)
                    after = device_of((space + 1) % slabs, high, x, core)
                    before = device_of((space - 1) % slabs, high, x, core)
                    upwind.append((me, after if high else before))
                    downwind.append((me, before if high else after))
                    quarter = 2 * high + (core ^ high)
                    next_slab = (space + (quarter == 3)) % slabs
                    quarter = (quarter + 1) % 4
                    x_up.append(
                        (me, device_of(next_slab, quarter // 2, x, (quarter % 2) ^ (quarter // 2)))
                    )
                    y_up.append((me, device_of(space, high, (x + 1) % 4, core)))
    back = lambda pairs: [(target, source) for source, target in pairs]
    return upwind, downwind, x_up, back(x_up), y_up, back(y_up)


def body(dist, relax_rate, kinetic_cells, kinetic_count, map_a, map_b, map_c):
    vel = (lax.axis_index("vel").astype(jnp.int32).reshape(1), SMEM)
    space = (lax.axis_index("space").astype(jnp.int32).reshape(1), SMEM)
    both = ("space", "vel")
    upwind, downwind, x_up, x_down, y_up, y_down = steps_of(lax.axis_size("space"))
    project, mix, expand, w = tables()
    consts = (jnp.asarray(project), jnp.asarray(mix), jnp.asarray(expand), jnp.asarray(w))
    layers = (NY, NZ, WIDTH)
    behind, ahead = call(
        first_halo_kernel, "first_halo", (vel, space, (dist, VMEM)),
        (((2,) + layers, jnp.bfloat16, VMEM), ((1,) + layers, jnp.bfloat16, VMEM)),
    )
    behind = lax.ppermute(behind, both, upwind)
    ahead = lax.ppermute(ahead, both, downwind)

    state = ((CX,) + layers, jnp.float32, VMEM)
    wide = (GROUPS, LAYER, WIDTH)
    halo = (GROUPS + GROUPS // 2, LINE, WIDTH)
    half = jnp.bfloat16
    hidden = VMEM((LAYER, RANK), half)

    (part,) = call(first_yz_kernel, "first_yz", ((dist, VMEM),), (state,), flops=12_000_000)
    (rows,) = call(
        first_x_kernel, "first_x", (vel,) + tuple((o, VMEM) for o in (dist, part, behind, ahead)),
        ((wide, half, VMEM),), flops=6_000_000,
    )
    gathered = lax.all_to_all(rows, "vel", split_axis=0, concat_axis=0, tiled=True)
    facts = (vel, space, (kinetic_count, SMEM))
    lanes = ((LAYER, WIDTH), jnp.float32, VMEM)
    held = tuple((o, VMEM) for o in (map_a, map_b, map_c) + consts)
    f, rates, up_x, down_x, up_y, down_y = call(
        first_collide_kernel, "first_collide",
        facts + ((gathered, VMEM), (kinetic_cells, VMEM), (relax_rate, VMEM)) + held,
        ((wide, jnp.float32, VMEM), lanes) + ((halo, half, VMEM),) * 4,
        scratch=(hidden,), flops=2_500_000_000, limit=C_VMEM,
    )
    y_below = lax.ppermute(up_y, both, y_up)
    y_above = lax.ppermute(down_y, both, y_down)
    x_below = lax.ppermute(up_x, both, x_up)
    x_above = lax.ppermute(down_x, both, x_down)
    part, mask = call(
        second_z_kernel, "second_z", facts + ((f, VMEM), (kinetic_cells, VMEM)),
        ((wide, jnp.float32, VMEM), lanes), flops=6_000_000,
    )
    (moved,) = call(
        second_xy_kernel, "second_xy",
        tuple((o, VMEM) for o in (f, part, y_below, y_above, x_below, x_above)),
        ((wide, jnp.float32, VMEM),), flops=12_000_000,
    )
    (result,) = call(
        second_collide_kernel, "second_collide", ((moved, VMEM), (mask, VMEM), (rates, VMEM)) + held,
        ((wide, half, VMEM),), scratch=(hidden,), flops=2_500_000_000, limit=C_VMEM,
    )
    pieces = lax.all_to_all(result, "vel", split_axis=0, concat_axis=0, tiled=True)
    (out,) = call(
        place_kernel, "place", ((pieces, VMEM),), (((CX,) + layers, jnp.float32, HBM),),
        scratch=(VMEM((CX,) + layers, jnp.float32), DMA((4,))),
    )
    return out


def solution(mesh):
    return jax.shard_map(
        body,
        mesh=mesh,
        in_specs=(
            P("space", None, None, "vel"),
            P("space", None, None),
            P(None, "space"),
            P(),
            P(),
            P(),
            P(),
        ),
        out_specs=P("space", None, None, "vel"),
        check_vma=False,
    )
```

```python
import jax
import jax.numpy as jnp
import numpy as np
from jax import lax
from jax.experimental import pallas as pl
from jax.experimental.pallas import tpu as pltpu
from jax.sharding import PartitionSpec as P

GX = 16
GY = 16
GZ = 8
NV = GX * GY * GZ
RANK = 768
COURANT = 0.1
SPACING = 0.5
COLLIDE = 0.5

CX = 16
NY = 16
NZ = 16
LAYER = NY * NZ
WIDTH = 128
GROUPS = NV // WIDTH
OFFSET = 3.0 / 16.0
BX = 4
BY = 4
LINE = BX * NZ


def tables():
    k = np.arange(NV)
    vx = ((k // (GY * GZ)) - 0.5 * (GX - 1)) * SPACING
    vy = ((k // GZ % GY) - 0.5 * (GY - 1)) * SPACING
    vz = ((k % GZ) - 0.5 * (GZ - 1)) * SPACING
    s = vx * vx + vy * vy + vz * vz
    w = np.exp(-0.5 * s)
    w = w / w.sum()
    sx, sy, sz = (w * vx * vx).sum(), (w * vy * vy).sum(), (w * vz * vz).sum()
    m2, m4 = (w * s).sum(), (w * s * s).sum()
    basis = np.stack([np.ones(NV), vx, vy, vz, s - OFFSET])
    q = np.zeros((5, 5))
    scale = 1.0 / (m4 - m2 * m2)
    thermal = np.zeros(5)
    thermal[0] = (OFFSET - m2) * scale
    thermal[4] = scale
    q[:, 4] = thermal
    q[:, 0] = (OFFSET - m2) * thermal
    q[0, 0] += 1.0
    q[1, 1], q[2, 2], q[3, 3] = 1.0 / sx, 1.0 / sy, 1.0 / sz
    project = np.zeros((NV, 128))
    project[:, :5] = basis.T
    mix = np.zeros((128, 128))
    expand = np.zeros((128, NV))
    for part in range(3):
        mix[:5, 8 * part : 8 * part + 5] = q
        expand[8 * part : 8 * part + 5] = basis
    return (
        project.astype(jnp.bfloat16),
        mix.astype(np.float32),
        expand.astype(jnp.bfloat16),
        w.reshape(1, NV).astype(np.float32),
    )


def minmod_half(a, b):
    return 0.5 * (jnp.maximum(jnp.minimum(a, b), 0.0) + jnp.minimum(jnp.maximum(a, b), 0.0))


C_VMEM = 12 << 20
HBM = pltpu.HBM
VMEM = pltpu.VMEM
SMEM = pltpu.SMEM
DMA = pltpu.SemaphoreType.DMA


def call(kernel, name, operands, outs, scratch=(), flops=0, limit=8 << 20):
    shapes = [jax.ShapeDtypeStruct(shape, dtype) for shape, dtype, _ in outs]
    arrays = [o for o, _ in operands]
    moved = sum(o.size * o.dtype.itemsize for o in arrays + shapes)
    return pl.pallas_call(
        kernel,
        out_shape=tuple(shapes),
        in_specs=[pl.BlockSpec(memory_space=space) for _, space in operands],
        out_specs=tuple(pl.BlockSpec(memory_space=space) for _, _, space in outs),
        scratch_shapes=list(scratch),
        compiler_params=pltpu.CompilerParams(vmem_limit_bytes=limit),
        cost_estimate=pl.CostEstimate(flops=flops, bytes_accessed=moved, transcendentals=0),
        name=name,
    )(*arrays)


def speeds_yz():
    lane = lax.broadcasted_iota(jnp.int32, (NZ, WIDTH), 1)
    along_y = (lane >> 3).astype(jnp.float32) - 0.5 * (GY - 1)
    along_z = (lane & (GZ - 1)).astype(jnp.float32) - 0.5 * (GZ - 1)
    return along_y * (SPACING * COURANT), along_z * (SPACING * COURANT)


def flux_change_z(f, uz, z_up):
    dz = pltpu.roll(f, NZ - 1, 0) - f
    slope = minmod_half(pltpu.roll(dz, 1, 0), dz)
    down = pltpu.roll(f - slope, NZ - 1, 0)
    flux = jnp.where(z_up, f + slope, down)
    return uz * (flux - pltpu.roll(flux, 1, 0))


def edges(before, here, after):
    slope = minmod_half(here - before, after - here)
    return here + slope, here - slope


def upwind_face(before, here, after):
    return here + minmod_half(here - before, after - here)


def first_halo_kernel(vel_ref, space_ref, dist_ref, behind_ref, ahead_ref):
    forward = vel_ref[0] >= GROUPS // 2
    start = jnp.where(forward, CX - 2, 0)
    for i in range(2):
        behind_ref[i] = dist_ref[start + i].astype(jnp.bfloat16)
    ahead_ref[0] = dist_ref[jnp.where(forward, 0, CX - 1)].astype(jnp.bfloat16)


def quarters(rank, space):
    high, core = (rank // 8 + space) % 2, rank % 2
    return 2 * high + (core + high) % 2, rank // 2 % 4


def kinetic_cells_of(step, vel_ref, space_ref, count_ref, cells_ref):
    x_quarter, y_quarter = quarters(vel_ref[0], space_ref[0])
    count = count_ref[step, space_ref[0]]
    shape = (LAYER, WIDTH)
    slot = lax.broadcasted_iota(jnp.int32, shape, 0)
    cell = (
        (BX * x_quarter + (slot >> 6)) * LAYER + BY * NZ * y_quarter + (slot & (LINE - 1))
    )
    lane = lax.broadcasted_iota(jnp.int32, (1, WIDTH), 1)
    found = jnp.zeros(shape, jnp.float32)
    for i in range(CX * LAYER // WIDTH):
        part = cells_ref[step : step + 1, WIDTH * i : WIDTH * (i + 1)]
        part = jnp.where(lane + WIDTH * i < count, part, -1)
        found = jnp.where(cell == part, 1.0, found)
    return jnp.broadcast_to(jnp.max(found, axis=1, keepdims=True), shape)


def rates_of(vel_ref, space_ref, rate_ref):
    x_quarter, y_quarter = quarters(vel_ref[0], space_ref[0])
    diagonal = lax.broadcasted_iota(jnp.int32, (NZ, NZ), 0) == lax.broadcasted_iota(
        jnp.int32, (NZ, NZ), 1
    )
    columns = []
    for x in range(BX):
        for y in range(BY):
            line = rate_ref[BX * x_quarter + x, pl.ds(BY * y_quarter + y, 1), :]
            column = jnp.sum(jnp.where(diagonal, line, 0.0), axis=1, keepdims=True)
            columns.append(jnp.broadcast_to(column, (NZ, WIDTH)))
    return jnp.concatenate(columns, axis=0)


def first_yz_kernel(f_ref, part_ref):
    uy, uz = speeds_yz()
    y_up = uy > 0.0
    z_up = uz > 0.0

    def layer(x, carry):
        def at(y):
            return f_ref[x, y % NY]

        up, _ = edges(at(-2), at(-1), at(0))
        next_up, next_down = edges(at(-1), at(0), at(1))
        flux_before = jnp.where(y_up, up, next_down)
        for y in range(NY):
            up = next_up
            next_up, next_down = edges(at(y), at(y + 1), at(y + 2))
            flux = jnp.where(y_up, up, next_down)
            here = at(y)
            part_ref[x, y] = here - uy * (flux - flux_before) - flux_change_z(here, uz, z_up)
            flux_before = flux
        return carry

    lax.fori_loop(0, CX, layer, 0)


def first_x_kernel(vel_ref, space_ref, f_ref, part_ref, behind_ref, ahead_ref, rows_ref):
    rank = vel_ref[0]
    forward = rank >= GROUPS // 2
    ux = jnp.abs(rank.astype(jnp.float32) - 0.5 * (GX - 1)) * (SPACING * COURANT)
    layers = [jnp.where(forward, k, CX - 1 - k) for k in range(CX)]
    starts = [(x % BX) * LINE for x in layers[:BX]]
    owners = []
    for k in range(4):
        quarter = jnp.where(forward, k, 3 - k)
        high = quarter // 2
        owners.append((high + space_ref[0]) % 2 * (GROUPS // 2) + (quarter + high) % 2)

    def line(quarter, y):
        inner = y * NZ
        y = quarter * BY + y

        def at(k):
            if k == -2:
                return behind_ref[jnp.where(forward, 0, 1), y].astype(jnp.float32)
            if k == -1:
                return behind_ref[jnp.where(forward, 1, 0), y].astype(jnp.float32)
            if k == CX:
                return ahead_ref[0, y].astype(jnp.float32)
            return f_ref[layers[k], y]

        face_before = upwind_face(at(-2), at(-1), at(0))
        for k in range(CX):
            face = upwind_face(at(k - 1), at(k), at(k + 1))
            result = part_ref[layers[k], y] - ux * (face - face_before)
            face_before = face
            start = pl.multiple_of(starts[k % BX] + inner, NZ)
            target = owners[k // BX] + quarter * 2
            rows_ref[target, pl.ds(start, NZ), :] = result.astype(jnp.bfloat16)

    def lines(quarter, carry):
        def one(y, inside):
            line(quarter, y)
            return inside

        lax.fori_loop(0, BY, one, 0)
        return carry

    lax.fori_loop(0, NY // BY, lines, 0)


def collide(rows, a_ref, b_ref, c_ref, project_ref, mix_ref, expand_ref, w_ref, hidden_ref):
    moments = jnp.dot(rows, project_ref[...], preferred_element_type=jnp.float32)
    coeffs = jnp.dot(
        moments, mix_ref[...], precision=lax.Precision.HIGHEST, preferred_element_type=jnp.float32
    )
    lane = lax.broadcasted_iota(jnp.int32, coeffs.shape, 1)
    high = coeffs.astype(jnp.bfloat16).astype(jnp.float32)
    rest = coeffs - high
    middle = rest.astype(jnp.bfloat16).astype(jnp.float32)
    split = jnp.where(lane < 8, high, jnp.where(lane < 16, middle, rest - middle))
    split = split.astype(jnp.bfloat16)
    for n in range(RANK // 256):
        cols = slice(256 * n, 256 * (n + 1))
        first = jnp.dot(rows, a_ref[:, cols], preferred_element_type=jnp.float32)
        second = jnp.dot(rows, b_ref[:, cols], preferred_element_type=jnp.float32)
        hidden_ref[:, cols] = (first * second).astype(jnp.bfloat16)
    hidden = hidden_ref[...]
    for n in range(NV // 256):
        cols = slice(256 * n, 256 * (n + 1))
        collision = jnp.dot(hidden, c_ref[:, cols], preferred_element_type=jnp.float32)
        collision = collision.astype(jnp.bfloat16).astype(jnp.float32)
        poly = jnp.dot(split, expand_ref[:, cols], preferred_element_type=jnp.float32)
        equilibrium = poly * w_ref[:, cols]
        for half in range(2):
            part = slice(WIDTH * half, WIDTH * (half + 1))
            yield 2 * n + half, collision[:, part], equilibrium[:, part]


def first_collide_kernel(
    vel_ref, space_ref, count_ref, rows_ref, cells_ref, rate_ref, a_ref, b_ref, c_ref,
    project_ref, mix_ref, expand_ref, w_ref,
    f_ref, rates_ref, x_up_ref, x_down_ref, y_up_ref, y_down_ref, hidden_ref,
):
    rows = jnp.concatenate([rows_ref[g] for g in range(GROUPS)], axis=1)
    kinetic = kinetic_cells_of(0, vel_ref, space_ref, count_ref, cells_ref) > 0.0
    rate = rates_of(vel_ref, space_ref, rate_ref)
    rates_ref[...] = rate
    half = GROUPS // 2
    low_lane = lax.broadcasted_iota(jnp.int32, (NZ, WIDTH), 1) < WIDTH // 2
    for g, collision, equilibrium in collide(
        rows, a_ref, b_ref, c_ref, project_ref, mix_ref, expand_ref, w_ref, hidden_ref
    ):
        moved = rows_ref[g].astype(jnp.float32)
        change = jnp.where(kinetic, COLLIDE * collision, rate * (equilibrium - moved))
        result = moved + change
        f_ref[g] = result
        sent = result.astype(jnp.bfloat16)
        x_up_ref[g] = sent[3 * LINE : 4 * LINE]
        x_down_ref[g] = sent[0:LINE]
        if g >= half:
            x_up_ref[g + half] = sent[2 * LINE : 3 * LINE]
        else:
            x_down_ref[g + GROUPS] = sent[LINE : 2 * LINE]
        for x in range(BX):
            here = slice(NZ * x, NZ * (x + 1))
            y_down_ref[g, here] = sent[LINE * x : LINE * x + NZ]
            y_up_ref[g, here] = sent[LINE * x + 3 * NZ : LINE * x + 4 * NZ]
            if g >= half:
                low = g - half
                second = slice(LINE * x + NZ, LINE * x + 2 * NZ)
                third = slice(LINE * x + 2 * NZ, LINE * x + 3 * NZ)
                y_up_ref[GROUPS + low, here] = jnp.where(
                    low_lane, pltpu.roll(f_ref[low, third], WIDTH // 2, 1), result[third]
                ).astype(jnp.bfloat16)
                y_down_ref[GROUPS + low, here] = jnp.where(
                    low_lane, f_ref[low, second], pltpu.roll(result[second], WIDTH // 2, 1)
                ).astype(jnp.bfloat16)


def second_z_kernel(vel_ref, space_ref, count_ref, f_ref, cells_ref, part_ref, mask_ref):
    mask_ref[...] = kinetic_cells_of(1, vel_ref, space_ref, count_ref, cells_ref)
    _, uz = speeds_yz()
    z_up = uz > 0.0

    def group(g, carry):
        for c in range(BX * BY):
            here = slice(NZ * c, NZ * (c + 1))
            f = f_ref[g, here]
            part_ref[g, here] = f - flux_change_z(f, uz, z_up)
        return carry

    lax.fori_loop(0, GROUPS, group, 0)


def second_xy_kernel(
    f_ref, part_ref, y_below_ref, y_above_ref, x_below_ref, x_above_ref, moved_ref
):
    uy, _ = speeds_yz()
    y_up = uy > 0.0
    half = GROUPS // 2

    def wide(ref, g, i):
        return ref[g, NZ * i : NZ * (i + 1)].astype(jnp.float32)

    def group(pair, upward):
        g = pair + half if upward else pair
        extra = pair + GROUPS
        ux = (g.astype(jnp.float32) - 0.5 * (GX - 1)) * (SPACING * COURANT)
        ux = ux if upward else -ux
        for y in range(BY):
            behind, ahead = (x_below_ref, x_above_ref) if upward else (x_above_ref, x_below_ref)

            def at_x(k):
                if k == -2:
                    return wide(behind, extra, y)
                if k == -1:
                    return wide(behind, g, y)
                if k == BX:
                    return wide(ahead, g, y)
                x = k if upward else BX - 1 - k
                return f_ref[g, LINE * x + NZ * y : LINE * x + NZ * (y + 1)]

            face_before = upwind_face(at_x(-2), at_x(-1), at_x(0))
            for k in range(BX):
                x = k if upward else BX - 1 - k
                face = upwind_face(at_x(k - 1), at_x(k), at_x(k + 1))
                here = slice(LINE * x + NZ * y, LINE * x + NZ * (y + 1))
                moved_ref[g, here] = part_ref[g, here] - ux * (face - face_before)
                face_before = face
        for x in range(BX):

            def at_y(y):
                if y == -2:
                    below = wide(y_below_ref, extra, x)
                    return below if upward else pltpu.roll(below, WIDTH // 2, 1)
                if y == -1:
                    return wide(y_below_ref, g, x)
                if y == BY:
                    return wide(y_above_ref, g, x)
                if y == BY + 1:
                    above = wide(y_above_ref, extra, x)
                    return pltpu.roll(above, WIDTH // 2, 1) if upward else above
                return f_ref[g, LINE * x + NZ * y : LINE * x + NZ * (y + 1)]

            up, _ = edges(at_y(-2), at_y(-1), at_y(0))
            next_up, next_down = edges(at_y(-1), at_y(0), at_y(1))
            flux_before = jnp.where(y_up, up, next_down)
            for y in range(BY):
                up = next_up
                next_up, next_down = edges(at_y(y), at_y(y + 1), at_y(y + 2))
                flux = jnp.where(y_up, up, next_down)
                here = slice(LINE * x + NZ * y, LINE * x + NZ * (y + 1))
                moved_ref[g, here] = moved_ref[g, here] - uy * (flux - flux_before)
                flux_before = flux

    def downwards(pair, carry):
        group(pair, False)
        return carry

    def upwards(pair, carry):
        group(pair, True)
        return carry

    lax.fori_loop(0, half, downwards, 0)
    lax.fori_loop(0, half, upwards, 0)


def second_collide_kernel(
    moved_ref, mask_ref, rates_ref, a_ref, b_ref, c_ref, project_ref, mix_ref, expand_ref, w_ref,
    out_ref, hidden_ref,
):
    rows = jnp.concatenate([moved_ref[g].astype(jnp.bfloat16) for g in range(GROUPS)], axis=1)
    kinetic = mask_ref[...] > 0.0
    rate = rates_ref[...]
    for g, collision, equilibrium in collide(
        rows, a_ref, b_ref, c_ref, project_ref, mix_ref, expand_ref, w_ref, hidden_ref
    ):
        moved = moved_ref[g]
        change = jnp.where(kinetic, COLLIDE * collision, rate * (equilibrium - moved))
        out_ref[g] = (moved + change).astype(jnp.bfloat16)


def place_kernel(space_ref, in_ref, out_hbm, out_ref, sems):
    stores = []
    for quarter in range(4):
        high = quarter // 2
        core = (quarter % 2) ^ high
        first = (high + space_ref[0]) % 2 * (GROUPS // 2) + core
        for x in range(BX):
            for y_quarter in range(4):
                for y in range(BY):
                    c = LINE * x + NZ * y
                    out_ref[BX * quarter + x, BY * y_quarter + y] = in_ref[
                        first + y_quarter * 2, c : c + NZ
                    ].astype(jnp.float32)
        part = slice(BX * quarter, BX * (quarter + 1))
        stores.append(pltpu.make_async_copy(out_ref.at[part], out_hbm.at[part], sems.at[quarter]))
        stores[-1].start()
    for store in stores:
        store.wait()


def device_of(space, high, x, core):
    return (space * 2 + high) * 8 + x * 2 + core


def holder_of(space, quarter, x):
    high = quarter // 2
    return device_of(space, (high + space) % 2, x, (quarter + high) % 2)


def steps_of(slabs):
    upwind, downwind, x_up, y_up = [], [], [], []
    for space in range(slabs):
        for high in range(2):
            for x in range(4):
                for core in range(2):
                    me = device_of(space, high, x, core)
                    after = device_of((space + 1) % slabs, high, x, core)
                    before = device_of((space - 1) % slabs, high, x, core)
                    upwind.append((me, after if high else before))
                    downwind.append((me, before if high else after))
                    turned = (high + space) % 2
                    quarter = 2 * turned + (core + turned) % 2
                    next_slab = (space + (quarter == 3)) % slabs
                    x_up.append((me, holder_of(next_slab, (quarter + 1) % 4, x)))
                    y_up.append((me, device_of(space, high, (x + 1) % 4, core)))
    back = lambda pairs: [(target, source) for source, target in pairs]
    return upwind, downwind, x_up, back(x_up), y_up, back(y_up)


def body(dist, relax_rate, kinetic_cells, kinetic_count, map_a, map_b, map_c):
    vel = (lax.axis_index("vel").astype(jnp.int32).reshape(1), SMEM)
    space = (lax.axis_index("space").astype(jnp.int32).reshape(1), SMEM)
    both = ("space", "vel")
    upwind, downwind, x_up, x_down, y_up, y_down = steps_of(lax.axis_size("space"))
    project, mix, expand, w = tables()
    consts = (jnp.asarray(project), jnp.asarray(mix), jnp.asarray(expand), jnp.asarray(w))
    layers = (NY, NZ, WIDTH)
    behind, ahead = call(
        first_halo_kernel, "first_halo", (vel, space, (dist, VMEM)),
        (((2,) + layers, jnp.bfloat16, VMEM), ((1,) + layers, jnp.bfloat16, VMEM)),
    )
    behind = lax.ppermute(behind, both, upwind)
    ahead = lax.ppermute(ahead, both, downwind)

    state = ((CX,) + layers, jnp.float32, VMEM)
    wide = (GROUPS, LAYER, WIDTH)
    halo = (GROUPS + GROUPS // 2, LINE, WIDTH)
    half = jnp.bfloat16
    hidden = VMEM((LAYER, RANK), half)

    (part,) = call(first_yz_kernel, "first_yz", ((dist, VMEM),), (state,), flops=12_000_000)
    (rows,) = call(
        first_x_kernel, "first_x", (vel, space) + tuple((o, VMEM) for o in (dist, part, behind, ahead)),
        ((wide, half, VMEM),), flops=6_000_000,
    )
    gathered = lax.all_to_all(rows, "vel", split_axis=0, concat_axis=0, tiled=True)
    facts = (vel, space, (kinetic_count, SMEM))
    lanes = ((LAYER, WIDTH), jnp.float32, VMEM)
    held = tuple((o, VMEM) for o in (map_a, map_b, map_c) + consts)
    f, rates, up_x, down_x, up_y, down_y = call(
        first_collide_kernel, "first_collide",
        facts + ((gathered, VMEM), (kinetic_cells, VMEM), (relax_rate, VMEM)) + held,
        ((wide, jnp.float32, VMEM), lanes) + ((halo, half, VMEM),) * 4,
        scratch=(hidden,), flops=2_500_000_000, limit=C_VMEM,
    )
    y_below = lax.ppermute(up_y, both, y_up)
    y_above = lax.ppermute(down_y, both, y_down)
    x_below = lax.ppermute(up_x, both, x_up)
    x_above = lax.ppermute(down_x, both, x_down)
    part, mask = call(
        second_z_kernel, "second_z", facts + ((f, VMEM), (kinetic_cells, VMEM)),
        ((wide, jnp.float32, VMEM), lanes), flops=6_000_000,
    )
    (moved,) = call(
        second_xy_kernel, "second_xy",
        tuple((o, VMEM) for o in (f, part, y_below, y_above, x_below, x_above)),
        ((wide, jnp.float32, VMEM),), flops=12_000_000,
    )
    (result,) = call(
        second_collide_kernel, "second_collide", ((moved, VMEM), (mask, VMEM), (rates, VMEM)) + held,
        ((wide, half, VMEM),), scratch=(hidden,), flops=2_500_000_000, limit=C_VMEM,
    )
    pieces = lax.all_to_all(result, "vel", split_axis=0, concat_axis=0, tiled=True)
    (out,) = call(
        place_kernel, "place", (space, (pieces, VMEM)), (((CX,) + layers, jnp.float32, HBM),),
        scratch=(VMEM((CX,) + layers, jnp.float32), DMA((4,))),
    )
    return out


def solution(mesh):
    return jax.shard_map(
        body,
        mesh=mesh,
        in_specs=(
            P("space", None, None, "vel"),
            P("space", None, None),
            P(None, "space"),
            P(),
            P(),
            P(),
            P(),
        ),
        out_specs=P("space", None, None, "vel"),
        check_vma=False,
    )
```

```python
import jax
import jax.numpy as jnp
import numpy as np
from jax import lax
from jax.experimental import pallas as pl
from jax.experimental.pallas import tpu as pltpu
from jax.sharding import PartitionSpec as P

GX = 16
GY = 16
GZ = 8
NV = GX * GY * GZ
RANK = 768
COURANT = 0.1
SPACING = 0.5
COLLIDE = 0.5

CX = 16
NY = 16
NZ = 16
LAYER = NY * NZ
WIDTH = 128
GROUPS = NV // WIDTH
OFFSET = 3.0 / 16.0
BX = 4
BY = 4
LINE = BX * NZ


def tables():
    k = np.arange(NV)
    vx = ((k // (GY * GZ)) - 0.5 * (GX - 1)) * SPACING
    vy = ((k // GZ % GY) - 0.5 * (GY - 1)) * SPACING
    vz = ((k % GZ) - 0.5 * (GZ - 1)) * SPACING
    s = vx * vx + vy * vy + vz * vz
    w = np.exp(-0.5 * s)
    w = w / w.sum()
    sx, sy, sz = (w * vx * vx).sum(), (w * vy * vy).sum(), (w * vz * vz).sum()
    m2, m4 = (w * s).sum(), (w * s * s).sum()
    basis = np.stack([np.ones(NV), vx, vy, vz, s - OFFSET])
    q = np.zeros((5, 5))
    scale = 1.0 / (m4 - m2 * m2)
    thermal = np.zeros(5)
    thermal[0] = (OFFSET - m2) * scale
    thermal[4] = scale
    q[:, 4] = thermal
    q[:, 0] = (OFFSET - m2) * thermal
    q[0, 0] += 1.0
    q[1, 1], q[2, 2], q[3, 3] = 1.0 / sx, 1.0 / sy, 1.0 / sz
    project = np.zeros((NV, 128))
    project[:, :5] = basis.T
    mix = np.zeros((128, 128))
    expand = np.zeros((128, NV))
    for part in range(3):
        mix[:5, 8 * part : 8 * part + 5] = q
        expand[8 * part : 8 * part + 5] = basis
    return (
        project.astype(jnp.bfloat16),
        mix.astype(np.float32),
        expand.astype(jnp.bfloat16),
        w.reshape(1, NV).astype(np.float32),
    )


def minmod_half(a, b):
    return 0.5 * (jnp.maximum(jnp.minimum(a, b), 0.0) + jnp.minimum(jnp.maximum(a, b), 0.0))


C_VMEM = 12 << 20
HBM = pltpu.HBM
VMEM = pltpu.VMEM
SMEM = pltpu.SMEM
DMA = pltpu.SemaphoreType.DMA


def call(kernel, name, operands, outs, scratch=(), flops=0, limit=8 << 20):
    shapes = [jax.ShapeDtypeStruct(shape, dtype) for shape, dtype, _ in outs]
    arrays = [o for o, _ in operands]
    moved = sum(o.size * o.dtype.itemsize for o in arrays + shapes)
    return pl.pallas_call(
        kernel,
        out_shape=tuple(shapes),
        in_specs=[pl.BlockSpec(memory_space=space) for _, space in operands],
        out_specs=tuple(pl.BlockSpec(memory_space=space) for _, _, space in outs),
        scratch_shapes=list(scratch),
        compiler_params=pltpu.CompilerParams(vmem_limit_bytes=limit),
        cost_estimate=pl.CostEstimate(flops=flops, bytes_accessed=moved, transcendentals=0),
        name=name,
    )(*arrays)


def speeds_yz():
    lane = lax.broadcasted_iota(jnp.int32, (NZ, WIDTH), 1)
    along_y = (lane >> 3).astype(jnp.float32) - 0.5 * (GY - 1)
    along_z = (lane & (GZ - 1)).astype(jnp.float32) - 0.5 * (GZ - 1)
    return along_y * (SPACING * COURANT), along_z * (SPACING * COURANT)


def flux_change_z(f, uz, z_up):
    dz = pltpu.roll(f, NZ - 1, 0) - f
    slope = minmod_half(pltpu.roll(dz, 1, 0), dz)
    down = pltpu.roll(f - slope, NZ - 1, 0)
    flux = jnp.where(z_up, f + slope, down)
    return uz * (flux - pltpu.roll(flux, 1, 0))


def edges(before, here, after):
    slope = minmod_half(here - before, after - here)
    return here + slope, here - slope


def upwind_face(before, here, after):
    return here + minmod_half(here - before, after - here)


def first_halo_kernel(vel_ref, space_ref, dist_ref, behind_ref, ahead_ref):
    forward = vel_ref[0] >= GROUPS // 2
    start = jnp.where(forward, CX - 2, 0)
    for i in range(2):
        behind_ref[i] = dist_ref[start + i].astype(jnp.bfloat16)
    ahead_ref[0] = dist_ref[jnp.where(forward, 0, CX - 1)].astype(jnp.bfloat16)


def quarters(rank, space):
    high, core = (rank // 8 + space) % 2, rank % 2
    return 2 * high + (core + high) % 2, rank // 2 % 4


def kinetic_cells_of(step, vel_ref, space_ref, count_ref, cells_ref):
    x_quarter, y_quarter = quarters(vel_ref[0], space_ref[0])
    count = count_ref[step, space_ref[0]]
    shape = (LAYER, WIDTH)
    slot = lax.broadcasted_iota(jnp.int32, shape, 0)
    cell = (
        (BX * x_quarter + (slot >> 6)) * LAYER + BY * NZ * y_quarter + (slot & (LINE - 1))
    )
    lane = lax.broadcasted_iota(jnp.int32, (1, WIDTH), 1)
    found = jnp.zeros(shape, jnp.float32)
    for i in range(CX * LAYER // WIDTH):
        part = cells_ref[step : step + 1, WIDTH * i : WIDTH * (i + 1)]
        part = jnp.where(lane + WIDTH * i < count, part, -1)
        found = jnp.where(cell == part, 1.0, found)
    return jnp.broadcast_to(jnp.max(found, axis=1, keepdims=True), shape)


def rates_of(vel_ref, space_ref, rate_ref):
    x_quarter, y_quarter = quarters(vel_ref[0], space_ref[0])
    diagonal = lax.broadcasted_iota(jnp.int32, (NZ, NZ), 0) == lax.broadcasted_iota(
        jnp.int32, (NZ, NZ), 1
    )
    columns = []
    for x in range(BX):
        for y in range(BY):
            line = rate_ref[BX * x_quarter + x, pl.ds(BY * y_quarter + y, 1), :]
            column = jnp.sum(jnp.where(diagonal, line, 0.0), axis=1, keepdims=True)
            columns.append(jnp.broadcast_to(column, (NZ, WIDTH)))
    return jnp.concatenate(columns, axis=0)


def first_yz_kernel(f_ref, part_ref):
    uy, uz = speeds_yz()
    y_up = uy > 0.0
    z_up = uz > 0.0

    def layer(x, carry):
        def at(y):
            return f_ref[x, y % NY]

        up, _ = edges(at(-2), at(-1), at(0))
        next_up, next_down = edges(at(-1), at(0), at(1))
        flux_before = jnp.where(y_up, up, next_down)
        for y in range(NY):
            up = next_up
            next_up, next_down = edges(at(y), at(y + 1), at(y + 2))
            flux = jnp.where(y_up, up, next_down)
            here = at(y)
            part_ref[x, y] = here - uy * (flux - flux_before) - flux_change_z(here, uz, z_up)
            flux_before = flux
        return carry

    lax.fori_loop(0, CX, layer, 0)


def first_x_kernel(vel_ref, space_ref, f_ref, part_ref, behind_ref, ahead_ref, rows_ref):
    rank = vel_ref[0]
    forward = rank >= GROUPS // 2
    ux = jnp.abs(rank.astype(jnp.float32) - 0.5 * (GX - 1)) * (SPACING * COURANT)
    layers = [jnp.where(forward, k, CX - 1 - k) for k in range(CX)]
    starts = [(x % BX) * LINE for x in layers[:BX]]
    owners = []
    for k in range(4):
        quarter = jnp.where(forward, k, 3 - k)
        high = quarter // 2
        owners.append((high + space_ref[0]) % 2 * (GROUPS // 2) + (quarter + high) % 2)

    def line(quarter, y):
        inner = y * NZ
        y = quarter * BY + y

        def at(k):
            if k == -2:
                return behind_ref[jnp.where(forward, 0, 1), y].astype(jnp.float32)
            if k == -1:
                return behind_ref[jnp.where(forward, 1, 0), y].astype(jnp.float32)
            if k == CX:
                return ahead_ref[0, y].astype(jnp.float32)
            return f_ref[layers[k], y]

        face_before = upwind_face(at(-2), at(-1), at(0))
        for k in range(CX):
            face = upwind_face(at(k - 1), at(k), at(k + 1))
            result = part_ref[layers[k], y] - ux * (face - face_before)
            face_before = face
            start = pl.multiple_of(starts[k % BX] + inner, NZ)
            target = owners[k // BX] + quarter * 2
            rows_ref[target, pl.ds(start, NZ), :] = result.astype(jnp.bfloat16)

    def lines(quarter, carry):
        def one(y, inside):
            line(quarter, y)
            return inside

        lax.fori_loop(0, BY, one, 0)
        return carry

    lax.fori_loop(0, NY // BY, lines, 0)


def collide(rows, a_ref, b_ref, c_ref, project_ref, mix_ref, expand_ref, w_ref, hidden_ref):
    moments = jnp.dot(rows, project_ref[...], preferred_element_type=jnp.float32)
    coeffs = jnp.dot(
        moments, mix_ref[...], precision=lax.Precision.HIGHEST, preferred_element_type=jnp.float32
    )
    lane = lax.broadcasted_iota(jnp.int32, coeffs.shape, 1)
    high = coeffs.astype(jnp.bfloat16).astype(jnp.float32)
    rest = coeffs - high
    middle = rest.astype(jnp.bfloat16).astype(jnp.float32)
    split = jnp.where(lane < 8, high, jnp.where(lane < 16, middle, rest - middle))
    split = split.astype(jnp.bfloat16)
    for n in range(RANK // 256):
        cols = slice(256 * n, 256 * (n + 1))
        first = jnp.dot(rows, a_ref[:, cols], preferred_element_type=jnp.float32)
        second = jnp.dot(rows, b_ref[:, cols], preferred_element_type=jnp.float32)
        hidden_ref[:, cols] = (first * second).astype(jnp.bfloat16)
    hidden = hidden_ref[...]
    for n in range(NV // 256):
        cols = slice(256 * n, 256 * (n + 1))
        collision = jnp.dot(hidden, c_ref[:, cols], preferred_element_type=jnp.float32)
        collision = collision.astype(jnp.bfloat16).astype(jnp.float32)
        poly = jnp.dot(split, expand_ref[:, cols], preferred_element_type=jnp.float32)
        equilibrium = poly * w_ref[:, cols]
        for half in range(2):
            part = slice(WIDTH * half, WIDTH * (half + 1))
            yield 2 * n + half, collision[:, part], equilibrium[:, part]


def first_collide_kernel(
    vel_ref, space_ref, count_ref, rows_ref, cells_ref, rate_ref, a_ref, b_ref, c_ref,
    project_ref, mix_ref, expand_ref, w_ref,
    f_ref, rates_ref, x_up_ref, x_down_ref, y_up_ref, y_down_ref, hidden_ref,
):
    rows = jnp.concatenate([rows_ref[g] for g in range(GROUPS)], axis=1)
    kinetic = kinetic_cells_of(0, vel_ref, space_ref, count_ref, cells_ref) > 0.0
    rate = rates_of(vel_ref, space_ref, rate_ref)
    rates_ref[...] = rate
    half = GROUPS // 2
    low_lane = lax.broadcasted_iota(jnp.int32, (NZ, WIDTH), 1) < WIDTH // 2
    for g, collision, equilibrium in collide(
        rows, a_ref, b_ref, c_ref, project_ref, mix_ref, expand_ref, w_ref, hidden_ref
    ):
        moved = rows_ref[g].astype(jnp.float32)
        change = jnp.where(kinetic, COLLIDE * collision, rate * (equilibrium - moved))
        result = moved + change
        f_ref[g] = result
        sent = result.astype(jnp.bfloat16)
        x_up_ref[g] = sent[3 * LINE : 4 * LINE]
        x_down_ref[g] = sent[0:LINE]
        if g >= half:
            x_up_ref[g + half] = sent[2 * LINE : 3 * LINE]
        else:
            x_down_ref[g + GROUPS] = sent[LINE : 2 * LINE]
        for x in range(BX):
            here = slice(NZ * x, NZ * (x + 1))
            y_down_ref[g, here] = sent[LINE * x : LINE * x + NZ]
            y_up_ref[g, here] = sent[LINE * x + 3 * NZ : LINE * x + 4 * NZ]
            if g >= half:
                low = g - half
                second = slice(LINE * x + NZ, LINE * x + 2 * NZ)
                third = slice(LINE * x + 2 * NZ, LINE * x + 3 * NZ)
                y_up_ref[GROUPS + low, here] = jnp.where(
                    low_lane, pltpu.roll(f_ref[low, third], WIDTH // 2, 1), result[third]
                ).astype(jnp.bfloat16)
                y_down_ref[GROUPS + low, here] = jnp.where(
                    low_lane, f_ref[low, second], pltpu.roll(result[second], WIDTH // 2, 1)
                ).astype(jnp.bfloat16)


def second_z_kernel(vel_ref, space_ref, count_ref, f_ref, cells_ref, part_ref, mask_ref):
    mask_ref[...] = kinetic_cells_of(1, vel_ref, space_ref, count_ref, cells_ref)
    _, uz = speeds_yz()
    z_up = uz > 0.0

    def group(g, carry):
        for c in range(BX * BY):
            here = slice(NZ * c, NZ * (c + 1))
            f = f_ref[g, here]
            part_ref[g, here] = f - flux_change_z(f, uz, z_up)
        return carry

    lax.fori_loop(0, GROUPS, group, 0)


def second_xy_kernel(
    f_ref, part_ref, x_below_ref, y_below_ref, x_above_ref, y_above_ref, moved_ref
):
    uy, _ = speeds_yz()
    y_up = uy > 0.0
    half = GROUPS // 2

    def wide(ref, g, i):
        return ref[g, NZ * i : NZ * (i + 1)].astype(jnp.float32)

    def group(pair, upward):
        g = pair + half if upward else pair
        extra = pair + GROUPS
        ux = (g.astype(jnp.float32) - 0.5 * (GX - 1)) * (SPACING * COURANT)
        ux = ux if upward else -ux
        for y in range(BY):
            behind, ahead = (x_below_ref, x_above_ref) if upward else (x_above_ref, x_below_ref)

            def at_x(k):
                if k == -2:
                    return wide(behind, extra, y)
                if k == -1:
                    return wide(behind, g, y)
                if k == BX:
                    return wide(ahead, g, y)
                x = k if upward else BX - 1 - k
                return f_ref[g, LINE * x + NZ * y : LINE * x + NZ * (y + 1)]

            face_before = upwind_face(at_x(-2), at_x(-1), at_x(0))
            for k in range(BX):
                x = k if upward else BX - 1 - k
                face = upwind_face(at_x(k - 1), at_x(k), at_x(k + 1))
                here = slice(LINE * x + NZ * y, LINE * x + NZ * (y + 1))
                moved_ref[g, here] = part_ref[g, here] - ux * (face - face_before)
                face_before = face
        for x in range(BX):

            def at_y(y):
                if y == -2:
                    below = wide(y_below_ref, extra, x)
                    return below if upward else pltpu.roll(below, WIDTH // 2, 1)
                if y == -1:
                    return wide(y_below_ref, g, x)
                if y == BY:
                    return wide(y_above_ref, g, x)
                if y == BY + 1:
                    above = wide(y_above_ref, extra, x)
                    return pltpu.roll(above, WIDTH // 2, 1) if upward else above
                return f_ref[g, LINE * x + NZ * y : LINE * x + NZ * (y + 1)]

            up, _ = edges(at_y(-2), at_y(-1), at_y(0))
            next_up, next_down = edges(at_y(-1), at_y(0), at_y(1))
            flux_before = jnp.where(y_up, up, next_down)
            for y in range(BY):
                up = next_up
                next_up, next_down = edges(at_y(y), at_y(y + 1), at_y(y + 2))
                flux = jnp.where(y_up, up, next_down)
                here = slice(LINE * x + NZ * y, LINE * x + NZ * (y + 1))
                moved_ref[g, here] = moved_ref[g, here] - uy * (flux - flux_before)
                flux_before = flux

    def downwards(pair, carry):
        group(pair, False)
        return carry

    def upwards(pair, carry):
        group(pair, True)
        return carry

    lax.fori_loop(0, half, downwards, 0)
    lax.fori_loop(0, half, upwards, 0)


def second_collide_kernel(
    moved_ref, mask_ref, rates_ref, a_ref, b_ref, c_ref, project_ref, mix_ref, expand_ref, w_ref,
    out_ref, hidden_ref,
):
    rows = jnp.concatenate([moved_ref[g].astype(jnp.bfloat16) for g in range(GROUPS)], axis=1)
    kinetic = mask_ref[...] > 0.0
    rate = rates_ref[...]
    for g, collision, equilibrium in collide(
        rows, a_ref, b_ref, c_ref, project_ref, mix_ref, expand_ref, w_ref, hidden_ref
    ):
        moved = moved_ref[g]
        change = jnp.where(kinetic, COLLIDE * collision, rate * (equilibrium - moved))
        out_ref[g] = (moved + change).astype(jnp.bfloat16)


def place_kernel(space_ref, in_ref, out_hbm, out_ref, sems):
    stores = []
    for quarter in range(4):
        high = quarter // 2
        core = (quarter % 2) ^ high
        first = (high + space_ref[0]) % 2 * (GROUPS // 2) + core
        for x in range(BX):
            for y_quarter in range(4):
                for y in range(BY):
                    c = LINE * x + NZ * y
                    out_ref[BX * quarter + x, BY * y_quarter + y] = in_ref[
                        first + y_quarter * 2, c : c + NZ
                    ].astype(jnp.float32)
        part = slice(BX * quarter, BX * (quarter + 1))
        stores.append(pltpu.make_async_copy(out_ref.at[part], out_hbm.at[part], sems.at[quarter]))
        stores[-1].start()
    for store in stores:
        store.wait()


def device_of(space, high, x, core):
    return (space * 2 + high) * 8 + x * 2 + core


def holder_of(space, quarter, x):
    high = quarter // 2
    return device_of(space, (high + space) % 2, x, (quarter + high) % 2)


def steps_of(slabs):
    upwind, downwind, x_up, y_up = [], [], [], []
    for space in range(slabs):
        for high in range(2):
            for x in range(4):
                for core in range(2):
                    me = device_of(space, high, x, core)
                    after = device_of((space + 1) % slabs, high, x, core)
                    before = device_of((space - 1) % slabs, high, x, core)
                    upwind.append((me, after if high else before))
                    downwind.append((me, before if high else after))
                    turned = (high + space) % 2
                    quarter = 2 * turned + (core + turned) % 2
                    next_slab = (space + (quarter == 3)) % slabs
                    x_up.append((me, holder_of(next_slab, (quarter + 1) % 4, x)))
                    y_up.append((me, device_of(space, high, (x + 1) % 4, core)))
    back = lambda pairs: [(target, source) for source, target in pairs]
    return upwind, downwind, x_up, back(x_up), y_up, back(y_up)


def body(dist, relax_rate, kinetic_cells, kinetic_count, map_a, map_b, map_c):
    vel = (lax.axis_index("vel").astype(jnp.int32).reshape(1), SMEM)
    space = (lax.axis_index("space").astype(jnp.int32).reshape(1), SMEM)
    both = ("space", "vel")
    upwind, downwind, x_up, x_down, y_up, y_down = steps_of(lax.axis_size("space"))
    project, mix, expand, w = tables()
    consts = (jnp.asarray(project), jnp.asarray(mix), jnp.asarray(expand), jnp.asarray(w))
    layers = (NY, NZ, WIDTH)
    behind, ahead = call(
        first_halo_kernel, "first_halo", (vel, space, (dist, VMEM)),
        (((2,) + layers, jnp.bfloat16, VMEM), ((1,) + layers, jnp.bfloat16, VMEM)),
    )
    behind = lax.ppermute(behind, both, upwind)
    ahead = lax.ppermute(ahead, both, downwind)

    state = ((CX,) + layers, jnp.float32, VMEM)
    wide = (GROUPS, LAYER, WIDTH)
    halo = (GROUPS + GROUPS // 2, LINE, WIDTH)
    half = jnp.bfloat16
    hidden = VMEM((LAYER, RANK), half)

    (part,) = call(first_yz_kernel, "first_yz", ((dist, VMEM),), (state,), flops=12_000_000)
    (rows,) = call(
        first_x_kernel, "first_x", (vel, space) + tuple((o, VMEM) for o in (dist, part, behind, ahead)),
        ((wide, half, VMEM),), flops=6_000_000,
    )
    gathered = lax.all_to_all(rows, "vel", split_axis=0, concat_axis=0, tiled=True)
    facts = (vel, space, (kinetic_count, SMEM))
    lanes = ((LAYER, WIDTH), jnp.float32, VMEM)
    held = tuple((o, VMEM) for o in (map_a, map_b, map_c) + consts)
    f, rates, up_x, down_x, up_y, down_y = call(
        first_collide_kernel, "first_collide",
        facts + ((gathered, VMEM), (kinetic_cells, VMEM), (relax_rate, VMEM)) + held,
        ((wide, jnp.float32, VMEM), lanes) + ((halo, half, VMEM),) * 4,
        scratch=(hidden,), flops=2_500_000_000, limit=C_VMEM,
    )
    y_below = lax.ppermute(up_y, both, y_up)
    y_above = lax.ppermute(down_y, both, y_down)
    x_below = lax.ppermute(up_x, both, x_up)
    x_above = lax.ppermute(down_x, both, x_down)
    part, mask = call(
        second_z_kernel, "second_z", facts + ((f, VMEM), (kinetic_cells, VMEM)),
        ((wide, jnp.float32, VMEM), lanes), flops=6_000_000,
    )
    (moved,) = call(
        second_xy_kernel, "second_xy",
        tuple((o, VMEM) for o in (f, part, x_below, y_below, x_above, y_above)),
        ((wide, jnp.float32, VMEM),), flops=12_000_000,
    )
    (result,) = call(
        second_collide_kernel, "second_collide", ((moved, VMEM), (mask, VMEM), (rates, VMEM)) + held,
        ((wide, half, VMEM),), scratch=(hidden,), flops=2_500_000_000, limit=C_VMEM,
    )
    pieces = lax.all_to_all(result, "vel", split_axis=0, concat_axis=0, tiled=True)
    (out,) = call(
        place_kernel, "place", (space, (pieces, VMEM)), (((CX,) + layers, jnp.float32, HBM),),
        scratch=(VMEM((CX,) + layers, jnp.float32), DMA((4,))),
    )
    return out


def solution(mesh):
    return jax.shard_map(
        body,
        mesh=mesh,
        in_specs=(
            P("space", None, None, "vel"),
            P("space", None, None),
            P(None, "space"),
            P(),
            P(),
            P(),
            P(),
        ),
        out_specs=P("space", None, None, "vel"),
        check_vma=False,
    )
```

```python
import jax
import jax.numpy as jnp
import numpy as np
from jax import lax
from jax.experimental import pallas as pl
from jax.experimental.pallas import tpu as pltpu
from jax.sharding import PartitionSpec as P

GX = 16
GY = 16
GZ = 8
NV = GX * GY * GZ
RANK = 768
COURANT = 0.1
SPACING = 0.5
COLLIDE = 0.5

CX = 16
NY = 16
NZ = 16
LAYER = NY * NZ
WIDTH = 128
GROUPS = NV // WIDTH
OFFSET = 3.0 / 16.0
BX = 4
BY = 4
LINE = BX * NZ


def tables():
    k = np.arange(NV)
    vx = ((k // (GY * GZ)) - 0.5 * (GX - 1)) * SPACING
    vy = ((k // GZ % GY) - 0.5 * (GY - 1)) * SPACING
    vz = ((k % GZ) - 0.5 * (GZ - 1)) * SPACING
    s = vx * vx + vy * vy + vz * vz
    w = np.exp(-0.5 * s)
    w = w / w.sum()
    sx, sy, sz = (w * vx * vx).sum(), (w * vy * vy).sum(), (w * vz * vz).sum()
    m2, m4 = (w * s).sum(), (w * s * s).sum()
    basis = np.stack([np.ones(NV), vx, vy, vz, s - OFFSET])
    q = np.zeros((5, 5))
    scale = 1.0 / (m4 - m2 * m2)
    thermal = np.zeros(5)
    thermal[0] = (OFFSET - m2) * scale
    thermal[4] = scale
    q[:, 4] = thermal
    q[:, 0] = (OFFSET - m2) * thermal
    q[0, 0] += 1.0
    q[1, 1], q[2, 2], q[3, 3] = 1.0 / sx, 1.0 / sy, 1.0 / sz
    project = np.zeros((NV, 128))
    project[:, :5] = basis.T
    mix = np.zeros((128, 128))
    expand = np.zeros((128, NV))
    for part in range(3):
        mix[:5, 8 * part : 8 * part + 5] = q
        expand[8 * part : 8 * part + 5] = basis
    return (
        project.astype(jnp.bfloat16),
        mix.astype(np.float32),
        expand.astype(jnp.bfloat16),
        w.reshape(1, NV).astype(np.float32),
    )


def minmod_half(a, b):
    return 0.5 * (jnp.maximum(jnp.minimum(a, b), 0.0) + jnp.minimum(jnp.maximum(a, b), 0.0))


C_VMEM = 12 << 20
HBM = pltpu.HBM
VMEM = pltpu.VMEM
SMEM = pltpu.SMEM
DMA = pltpu.SemaphoreType.DMA


def call(kernel, name, operands, outs, scratch=(), flops=0, limit=8 << 20):
    shapes = [jax.ShapeDtypeStruct(shape, dtype) for shape, dtype, _ in outs]
    arrays = [o for o, _ in operands]
    moved = sum(o.size * o.dtype.itemsize for o in arrays + shapes)
    return pl.pallas_call(
        kernel,
        out_shape=tuple(shapes),
        in_specs=[pl.BlockSpec(memory_space=space) for _, space in operands],
        out_specs=tuple(pl.BlockSpec(memory_space=space) for _, _, space in outs),
        scratch_shapes=list(scratch),
        compiler_params=pltpu.CompilerParams(vmem_limit_bytes=limit),
        cost_estimate=pl.CostEstimate(flops=flops, bytes_accessed=moved, transcendentals=0),
        name=name,
    )(*arrays)


def speeds_yz():
    lane = lax.broadcasted_iota(jnp.int32, (NZ, WIDTH), 1)
    along_y = (lane >> 3).astype(jnp.float32) - 0.5 * (GY - 1)
    along_z = (lane & (GZ - 1)).astype(jnp.float32) - 0.5 * (GZ - 1)
    return along_y * (SPACING * COURANT), along_z * (SPACING * COURANT)


def flux_change_z(f, uz, z_up):
    dz = pltpu.roll(f, NZ - 1, 0) - f
    slope = minmod_half(pltpu.roll(dz, 1, 0), dz)
    down = pltpu.roll(f - slope, NZ - 1, 0)
    flux = jnp.where(z_up, f + slope, down)
    return uz * (flux - pltpu.roll(flux, 1, 0))


def edges(before, here, after):
    slope = minmod_half(here - before, after - here)
    return here + slope, here - slope


def upwind_face(before, here, after):
    return here + minmod_half(here - before, after - here)


def first_halo_kernel(vel_ref, space_ref, dist_ref, behind_ref, ahead_ref):
    forward = vel_ref[0] >= GROUPS // 2
    start = jnp.where(forward, CX - 2, 0)
    for i in range(2):
        behind_ref[i] = dist_ref[start + i].astype(jnp.bfloat16)
    ahead_ref[0] = dist_ref[jnp.where(forward, 0, CX - 1)].astype(jnp.bfloat16)


def quarters(rank, space):
    high, core = (rank // 8 + space) % 2, rank % 2
    return 2 * high + (core + high) % 2, rank // 2 % 4


def kinetic_cells_of(step, vel_ref, space_ref, count_ref, cells_ref):
    x_quarter, y_quarter = quarters(vel_ref[0], space_ref[0])
    count = count_ref[step, space_ref[0]]
    shape = (LAYER, WIDTH)
    slot = lax.broadcasted_iota(jnp.int32, shape, 0)
    cell = (
        (BX * x_quarter + (slot >> 6)) * LAYER + BY * NZ * y_quarter + (slot & (LINE - 1))
    )
    lane = lax.broadcasted_iota(jnp.int32, (1, WIDTH), 1)
    found = jnp.zeros(shape, jnp.float32)
    for i in range(CX * LAYER // WIDTH):
        part = cells_ref[step : step + 1, WIDTH * i : WIDTH * (i + 1)]
        part = jnp.where(lane + WIDTH * i < count, part, -1)
        found = jnp.where(cell == part, 1.0, found)
    return jnp.broadcast_to(jnp.max(found, axis=1, keepdims=True), shape)


def rates_of(vel_ref, space_ref, rate_ref):
    x_quarter, y_quarter = quarters(vel_ref[0], space_ref[0])
    diagonal = lax.broadcasted_iota(jnp.int32, (NZ, NZ), 0) == lax.broadcasted_iota(
        jnp.int32, (NZ, NZ), 1
    )
    columns = []
    for x in range(BX):
        for y in range(BY):
            line = rate_ref[BX * x_quarter + x, pl.ds(BY * y_quarter + y, 1), :]
            column = jnp.sum(jnp.where(diagonal, line, 0.0), axis=1, keepdims=True)
            columns.append(jnp.broadcast_to(column, (NZ, WIDTH)))
    return jnp.concatenate(columns, axis=0)


def first_yz_kernel(f_ref, part_ref):
    uy, uz = speeds_yz()
    y_up = uy > 0.0
    z_up = uz > 0.0

    def layer(x, carry):
        def at(y):
            return f_ref[x, y % NY]

        up, _ = edges(at(-2), at(-1), at(0))
        next_up, next_down = edges(at(-1), at(0), at(1))
        flux_before = jnp.where(y_up, up, next_down)
        for y in range(NY):
            up = next_up
            next_up, next_down = edges(at(y), at(y + 1), at(y + 2))
            flux = jnp.where(y_up, up, next_down)
            here = at(y)
            part_ref[x, y] = here - uy * (flux - flux_before) - flux_change_z(here, uz, z_up)
            flux_before = flux
        return carry

    lax.fori_loop(0, CX, layer, 0)


def first_x_kernel(vel_ref, space_ref, f_ref, part_ref, behind_ref, ahead_ref, rows_ref):
    rank = vel_ref[0]
    forward = rank >= GROUPS // 2
    ux = jnp.abs(rank.astype(jnp.float32) - 0.5 * (GX - 1)) * (SPACING * COURANT)
    layers = [jnp.where(forward, k, CX - 1 - k) for k in range(CX)]
    starts = [(x % BX) * LINE for x in layers[:BX]]
    owners = []
    for k in range(4):
        quarter = jnp.where(forward, k, 3 - k)
        high = quarter // 2
        owners.append((high + space_ref[0]) % 2 * (GROUPS // 2) + (quarter + high) % 2)

    def line(quarter, y):
        inner = y * NZ
        y = quarter * BY + y

        def at(k):
            if k == -2:
                return behind_ref[jnp.where(forward, 0, 1), y].astype(jnp.float32)
            if k == -1:
                return behind_ref[jnp.where(forward, 1, 0), y].astype(jnp.float32)
            if k == CX:
                return ahead_ref[0, y].astype(jnp.float32)
            return f_ref[layers[k], y]

        face_before = upwind_face(at(-2), at(-1), at(0))
        for k in range(CX):
            face = upwind_face(at(k - 1), at(k), at(k + 1))
            result = part_ref[layers[k], y] - ux * (face - face_before)
            face_before = face
            start = pl.multiple_of(starts[k % BX] + inner, NZ)
            target = owners[k // BX] + quarter * 2
            rows_ref[target, pl.ds(start, NZ), :] = result.astype(jnp.bfloat16)

    def lines(quarter, carry):
        def one(y, inside):
            line(quarter, y)
            return inside

        lax.fori_loop(0, BY, one, 0)
        return carry

    lax.fori_loop(0, NY // BY, lines, 0)


def collide(rows, a_ref, b_ref, c_ref, project_ref, mix_ref, expand_ref, w_ref, hidden_ref):
    moments = jnp.dot(rows, project_ref[...], preferred_element_type=jnp.float32)
    coeffs = jnp.dot(
        moments, mix_ref[...], precision=lax.Precision.HIGHEST, preferred_element_type=jnp.float32
    )
    lane = lax.broadcasted_iota(jnp.int32, coeffs.shape, 1)
    high = coeffs.astype(jnp.bfloat16).astype(jnp.float32)
    rest = coeffs - high
    middle = rest.astype(jnp.bfloat16).astype(jnp.float32)
    split = jnp.where(lane < 8, high, jnp.where(lane < 16, middle, rest - middle))
    split = split.astype(jnp.bfloat16)
    for n in range(RANK // 256):
        cols = slice(256 * n, 256 * (n + 1))
        first = jnp.dot(rows, a_ref[:, cols], preferred_element_type=jnp.float32)
        second = jnp.dot(rows, b_ref[:, cols], preferred_element_type=jnp.float32)
        hidden_ref[:, cols] = (first * second).astype(jnp.bfloat16)
    hidden = hidden_ref[...]
    for n in range(NV // 256):
        cols = slice(256 * n, 256 * (n + 1))
        collision = jnp.dot(hidden, c_ref[:, cols], preferred_element_type=jnp.float32)
        collision = collision.astype(jnp.bfloat16).astype(jnp.float32)
        poly = jnp.dot(split, expand_ref[:, cols], preferred_element_type=jnp.float32)
        equilibrium = poly * w_ref[:, cols]
        for half in range(2):
            part = slice(WIDTH * half, WIDTH * (half + 1))
            yield 2 * n + half, collision[:, part], equilibrium[:, part]


def first_collide_kernel(
    vel_ref, space_ref, count_ref, rows_ref, cells_ref, rate_ref, a_ref, b_ref, c_ref,
    project_ref, mix_ref, expand_ref, w_ref,
    f_ref, rates_ref, x_even_ref, x_odd_ref, y_even_ref, y_odd_ref, hidden_ref,
):
    rows = jnp.concatenate([rows_ref[g] for g in range(GROUPS)], axis=1)
    kinetic = kinetic_cells_of(0, vel_ref, space_ref, count_ref, cells_ref) > 0.0
    rate = rates_of(vel_ref, space_ref, rate_ref)
    rates_ref[...] = rate
    half = GROUPS // 2
    x_quarter, y_quarter = quarters(vel_ref[0], space_ref[0])
    x_is_even, y_is_even = x_quarter % 2 == 0, y_quarter % 2 == 0

    def put(even_ref, odd_ref, is_even, where, up, down):
        even_ref[where] = jnp.where(is_even, up, down).astype(jnp.bfloat16)
        odd_ref[where] = jnp.where(is_even, down, up).astype(jnp.bfloat16)

    low_lane = lax.broadcasted_iota(jnp.int32, (NZ, WIDTH), 1) < WIDTH // 2
    for g, collision, equilibrium in collide(
        rows, a_ref, b_ref, c_ref, project_ref, mix_ref, expand_ref, w_ref, hidden_ref
    ):
        moved = rows_ref[g].astype(jnp.float32)
        change = jnp.where(kinetic, COLLIDE * collision, rate * (equilibrium - moved))
        result = moved + change
        f_ref[g] = result
        put(x_even_ref, x_odd_ref, x_is_even, g, result[3 * LINE :], result[:LINE])
        low = g - half
        if low >= 0:
            put(
                x_even_ref, x_odd_ref, x_is_even, GROUPS + low,
                result[2 * LINE : 3 * LINE], f_ref[low, LINE : 2 * LINE],
            )
        for x in range(BX):
            here = slice(NZ * x, NZ * (x + 1))
            first, second, third, fourth = (
                slice(LINE * x + NZ * y, LINE * x + NZ * (y + 1)) for y in range(BY)
            )
            put(y_even_ref, y_odd_ref, y_is_even, (g, here), result[fourth], result[first])
            if low >= 0:
                put(
                    y_even_ref, y_odd_ref, y_is_even, (GROUPS + low, here),
                    jnp.where(
                        low_lane, pltpu.roll(f_ref[low, third], WIDTH // 2, 1), result[third]
                    ),
                    jnp.where(
                        low_lane, f_ref[low, second], pltpu.roll(result[second], WIDTH // 2, 1)
                    ),
                )


def second_z_kernel(vel_ref, space_ref, count_ref, f_ref, cells_ref, part_ref, mask_ref):
    mask_ref[...] = kinetic_cells_of(1, vel_ref, space_ref, count_ref, cells_ref)
    _, uz = speeds_yz()
    z_up = uz > 0.0

    def group(g, carry):
        for c in range(BX * BY):
            here = slice(NZ * c, NZ * (c + 1))
            f = f_ref[g, here]
            part_ref[g, here] = f - flux_change_z(f, uz, z_up)
        return carry

    lax.fori_loop(0, GROUPS, group, 0)


def second_xy_kernel(
    vel_ref, space_ref, f_ref, part_ref, x_odd_ref, y_even_ref, y_odd_ref, x_even_ref, moved_ref
):
    uy, _ = speeds_yz()
    y_up = uy > 0.0
    half = GROUPS // 2

    x_quarter, y_quarter = quarters(vel_ref[0], space_ref[0])
    x_is_even, y_is_even = x_quarter % 2 == 0, y_quarter % 2 == 0

    def arrived(even_ref, odd_ref, is_even, g, i):
        even = even_ref[g, NZ * i : NZ * (i + 1)].astype(jnp.float32)
        odd = odd_ref[g, NZ * i : NZ * (i + 1)].astype(jnp.float32)
        return jnp.where(is_even, odd, even), jnp.where(is_even, even, odd)

    def group(pair, upward):
        g = pair + half if upward else pair
        extra = pair + GROUPS
        ux = (g.astype(jnp.float32) - 0.5 * (GX - 1)) * (SPACING * COURANT)
        ux = ux if upward else -ux
        for y in range(BY):
            here_x = (x_even_ref, x_odd_ref, x_is_even)
            behind, ahead = arrived(*here_x, g, y)[:: 1 if upward else -1]
            line = [arrived(*here_x, extra, y)[0 if upward else 1], behind]
            for k in range(BX):
                x = k if upward else BX - 1 - k
                line.append(f_ref[g, LINE * x + NZ * y : LINE * x + NZ * (y + 1)])
            line.append(ahead)

            def at_x(k):
                return line[k + 2]

            face_before = upwind_face(at_x(-2), at_x(-1), at_x(0))
            for k in range(BX):
                x = k if upward else BX - 1 - k
                face = upwind_face(at_x(k - 1), at_x(k), at_x(k + 1))
                here = slice(LINE * x + NZ * y, LINE * x + NZ * (y + 1))
                moved_ref[g, here] = part_ref[g, here] - ux * (face - face_before)
                face_before = face
        for x in range(BX):
            here_y = (y_even_ref, y_odd_ref, y_is_even)
            below, above = arrived(*here_y, g, x)
            below_2, above_2 = arrived(*here_y, extra, x)
            if upward:
                above_2 = pltpu.roll(above_2, WIDTH // 2, 1)
            else:
                below_2 = pltpu.roll(below_2, WIDTH // 2, 1)
            column = [below_2, below]
            for y in range(BY):
                column.append(f_ref[g, LINE * x + NZ * y : LINE * x + NZ * (y + 1)])
            column += [above, above_2]

            def at_y(y):
                return column[y + 2]

            up, _ = edges(at_y(-2), at_y(-1), at_y(0))
            next_up, next_down = edges(at_y(-1), at_y(0), at_y(1))
            flux_before = jnp.where(y_up, up, next_down)
            for y in range(BY):
                up = next_up
                next_up, next_down = edges(at_y(y), at_y(y + 1), at_y(y + 2))
                flux = jnp.where(y_up, up, next_down)
                here = slice(LINE * x + NZ * y, LINE * x + NZ * (y + 1))
                moved_ref[g, here] = moved_ref[g, here] - uy * (flux - flux_before)
                flux_before = flux

    def downwards(pair, carry):
        group(pair, False)
        return carry

    def upwards(pair, carry):
        group(pair, True)
        return carry

    lax.fori_loop(0, half, downwards, 0)
    lax.fori_loop(0, half, upwards, 0)


def second_collide_kernel(
    moved_ref, mask_ref, rates_ref, a_ref, b_ref, c_ref, project_ref, mix_ref, expand_ref, w_ref,
    out_ref, hidden_ref,
):
    rows = jnp.concatenate([moved_ref[g].astype(jnp.bfloat16) for g in range(GROUPS)], axis=1)
    kinetic = mask_ref[...] > 0.0
    rate = rates_ref[...]
    for g, collision, equilibrium in collide(
        rows, a_ref, b_ref, c_ref, project_ref, mix_ref, expand_ref, w_ref, hidden_ref
    ):
        moved = moved_ref[g]
        change = jnp.where(kinetic, COLLIDE * collision, rate * (equilibrium - moved))
        out_ref[g] = (moved + change).astype(jnp.bfloat16)


def place_kernel(space_ref, in_ref, out_hbm, out_ref, sems):
    stores = []
    for quarter in range(4):
        high = quarter // 2
        core = (quarter % 2) ^ high
        first = (high + space_ref[0]) % 2 * (GROUPS // 2) + core
        for x in range(BX):
            for y_quarter in range(4):
                for y in range(BY):
                    c = LINE * x + NZ * y
                    out_ref[BX * quarter + x, BY * y_quarter + y] = in_ref[
                        first + y_quarter * 2, c : c + NZ
                    ].astype(jnp.float32)
        part = slice(BX * quarter, BX * (quarter + 1))
        stores.append(pltpu.make_async_copy(out_ref.at[part], out_hbm.at[part], sems.at[quarter]))
        stores[-1].start()
    for store in stores:
        store.wait()


def device_of(space, high, x, core):
    return (space * 2 + high) * 8 + x * 2 + core


def holder_of(space, quarter, x):
    high = quarter // 2
    return device_of(space, (high + space) % 2, x, (quarter + high) % 2)


def steps_of(slabs):
    upwind, downwind = [], []
    x_even, x_odd, y_even, y_odd = [], [], [], []
    for space in range(slabs):
        before, after = (space - 1) % slabs, (space + 1) % slabs
        for quarter in range(4):
            next_x = holder_place(space, quarter + 1, slabs)
            last_x = holder_place(space, quarter - 1, slabs)
            for x in range(4):
                me = holder_of(space, quarter, x)
                rank = me % GROUPS
                forward = rank >= GROUPS // 2
                upwind.append((me, (after if forward else before) * GROUPS + rank))
                downwind.append((me, (before if forward else after) * GROUPS + rank))
                up, down = holder_of(*next_x, x), holder_of(*last_x, x)
                x_even.append((me, down if quarter % 2 else up))
                x_odd.append((me, up if quarter % 2 else down))
                up, down = (holder_of(space, quarter, (x + d) % 4) for d in (1, -1))
                y_even.append((me, down if x % 2 else up))
                y_odd.append((me, up if x % 2 else down))
    return upwind, downwind, x_even, x_odd, y_even, y_odd


def holder_place(space, quarter, slabs):
    return (space + quarter // 4) % slabs, quarter % 4


def body(dist, relax_rate, kinetic_cells, kinetic_count, map_a, map_b, map_c):
    vel = (lax.axis_index("vel").astype(jnp.int32).reshape(1), SMEM)
    space = (lax.axis_index("space").astype(jnp.int32).reshape(1), SMEM)
    both = ("space", "vel")
    upwind, downwind, *pairs = steps_of(lax.axis_size("space"))
    project, mix, expand, w = tables()
    consts = (jnp.asarray(project), jnp.asarray(mix), jnp.asarray(expand), jnp.asarray(w))
    layers = (NY, NZ, WIDTH)
    behind, ahead = call(
        first_halo_kernel, "first_halo", (vel, space, (dist, VMEM)),
        (((2,) + layers, jnp.bfloat16, VMEM), ((1,) + layers, jnp.bfloat16, VMEM)),
    )
    behind = lax.ppermute(behind, both, upwind)
    ahead = lax.ppermute(ahead, both, downwind)

    state = ((CX,) + layers, jnp.float32, VMEM)
    wide = (GROUPS, LAYER, WIDTH)
    halo = (GROUPS + GROUPS // 2, LINE, WIDTH)
    half = jnp.bfloat16
    hidden = VMEM((LAYER, RANK), half)

    (part,) = call(first_yz_kernel, "first_yz", ((dist, VMEM),), (state,), flops=12_000_000)
    (rows,) = call(
        first_x_kernel, "first_x", (vel, space) + tuple((o, VMEM) for o in (dist, part, behind, ahead)),
        ((wide, half, VMEM),), flops=6_000_000,
    )
    gathered = lax.all_to_all(rows, "vel", split_axis=0, concat_axis=0, tiled=True)
    facts = (vel, space, (kinetic_count, SMEM))
    lanes = ((LAYER, WIDTH), jnp.float32, VMEM)
    held = tuple((o, VMEM) for o in (map_a, map_b, map_c) + consts)
    f, rates, *halos = call(
        first_collide_kernel, "first_collide",
        facts + ((gathered, VMEM), (kinetic_cells, VMEM), (relax_rate, VMEM)) + held,
        ((wide, jnp.float32, VMEM), lanes) + ((halo, half, VMEM),) * 4,
        scratch=(hidden,), flops=2_500_000_000, limit=C_VMEM,
    )
    x_even, x_odd, y_even, y_odd = (
        lax.ppermute(o, both, p) for o, p in zip(halos, pairs, strict=True)
    )
    part, mask = call(
        second_z_kernel, "second_z", facts + ((f, VMEM), (kinetic_cells, VMEM)),
        ((wide, jnp.float32, VMEM), lanes), flops=6_000_000,
    )
    (moved,) = call(
        second_xy_kernel, "second_xy",
        (vel, space) + tuple((o, VMEM) for o in (f, part, x_odd, y_even, y_odd, x_even)),
        ((wide, jnp.float32, VMEM),), flops=12_000_000,
    )
    (result,) = call(
        second_collide_kernel, "second_collide", ((moved, VMEM), (mask, VMEM), (rates, VMEM)) + held,
        ((wide, half, VMEM),), scratch=(hidden,), flops=2_500_000_000, limit=C_VMEM,
    )
    pieces = lax.all_to_all(result, "vel", split_axis=0, concat_axis=0, tiled=True)
    (out,) = call(
        place_kernel, "place", (space, (pieces, VMEM)), (((CX,) + layers, jnp.float32, HBM),),
        scratch=(VMEM((CX,) + layers, jnp.float32), DMA((4,))),
    )
    return out


def solution(mesh):
    return jax.shard_map(
        body,
        mesh=mesh,
        in_specs=(
            P("space", None, None, "vel"),
            P("space", None, None),
            P(None, "space"),
            P(),
            P(),
            P(),
            P(),
        ),
        out_specs=P("space", None, None, "vel"),
        check_vma=False,
    )
```

```python
import jax
import jax.numpy as jnp
import numpy as np
from jax import lax
from jax.experimental import pallas as pl
from jax.experimental.pallas import tpu as pltpu
from jax.sharding import PartitionSpec as P

GX = 16
GY = 16
GZ = 8
NV = GX * GY * GZ
RANK = 768
COURANT = 0.1
SPACING = 0.5
COLLIDE = 0.5

CX = 16
NY = 16
NZ = 16
LAYER = NY * NZ
WIDTH = 128
GROUPS = NV // WIDTH
OFFSET = 3.0 / 16.0
BX = 4
BY = 4
LINE = BX * NZ


def tables():
    k = np.arange(NV)
    vx = ((k // (GY * GZ)) - 0.5 * (GX - 1)) * SPACING
    vy = ((k // GZ % GY) - 0.5 * (GY - 1)) * SPACING
    vz = ((k % GZ) - 0.5 * (GZ - 1)) * SPACING
    s = vx * vx + vy * vy + vz * vz
    w = np.exp(-0.5 * s)
    w = w / w.sum()
    sx, sy, sz = (w * vx * vx).sum(), (w * vy * vy).sum(), (w * vz * vz).sum()
    m2, m4 = (w * s).sum(), (w * s * s).sum()
    basis = np.stack([np.ones(NV), vx, vy, vz, s - OFFSET])
    q = np.zeros((5, 5))
    scale = 1.0 / (m4 - m2 * m2)
    thermal = np.zeros(5)
    thermal[0] = (OFFSET - m2) * scale
    thermal[4] = scale
    q[:, 4] = thermal
    q[:, 0] = (OFFSET - m2) * thermal
    q[0, 0] += 1.0
    q[1, 1], q[2, 2], q[3, 3] = 1.0 / sx, 1.0 / sy, 1.0 / sz
    project = np.zeros((NV, 128))
    project[:, :5] = basis.T
    mix = np.zeros((128, 128))
    expand = np.zeros((128, NV))
    for part in range(3):
        mix[:5, 8 * part : 8 * part + 5] = q
        expand[8 * part : 8 * part + 5] = basis
    return (
        project.astype(jnp.bfloat16),
        mix.astype(np.float32),
        expand.astype(jnp.bfloat16),
        w.reshape(1, NV).astype(np.float32),
    )


def minmod_half(a, b):
    return 0.5 * (jnp.maximum(jnp.minimum(a, b), 0.0) + jnp.minimum(jnp.maximum(a, b), 0.0))


C_VMEM = 12 << 20
HBM = pltpu.HBM
VMEM = pltpu.VMEM
SMEM = pltpu.SMEM
DMA = pltpu.SemaphoreType.DMA


def call(kernel, name, operands, outs, scratch=(), flops=0, limit=8 << 20):
    shapes = [jax.ShapeDtypeStruct(shape, dtype) for shape, dtype, _ in outs]
    arrays = [o for o, _ in operands]
    moved = sum(o.size * o.dtype.itemsize for o in arrays + shapes)
    return pl.pallas_call(
        kernel,
        out_shape=tuple(shapes),
        in_specs=[pl.BlockSpec(memory_space=space) for _, space in operands],
        out_specs=tuple(pl.BlockSpec(memory_space=space) for _, _, space in outs),
        scratch_shapes=list(scratch),
        compiler_params=pltpu.CompilerParams(vmem_limit_bytes=limit),
        cost_estimate=pl.CostEstimate(flops=flops, bytes_accessed=moved, transcendentals=0),
        name=name,
    )(*arrays)


def speeds_yz():
    lane = lax.broadcasted_iota(jnp.int32, (NZ, WIDTH), 1)
    along_y = (lane >> 3).astype(jnp.float32) - 0.5 * (GY - 1)
    along_z = (lane & (GZ - 1)).astype(jnp.float32) - 0.5 * (GZ - 1)
    return along_y * (SPACING * COURANT), along_z * (SPACING * COURANT)


def flux_change_z(f, uz, z_up):
    dz = pltpu.roll(f, NZ - 1, 0) - f
    slope = minmod_half(pltpu.roll(dz, 1, 0), dz)
    down = pltpu.roll(f - slope, NZ - 1, 0)
    flux = jnp.where(z_up, f + slope, down)
    return uz * (flux - pltpu.roll(flux, 1, 0))


def edges(before, here, after):
    slope = minmod_half(here - before, after - here)
    return here + slope, here - slope


def upwind_face(before, here, after):
    return here + minmod_half(here - before, after - here)


def first_halo_kernel(vel_ref, space_ref, dist_ref, behind_ref, ahead_ref):
    forward = vel_ref[0] >= GROUPS // 2
    start = jnp.where(forward, CX - 2, 0)
    for i in range(2):
        behind_ref[i] = dist_ref[start + i].astype(jnp.bfloat16)
    ahead_ref[0] = dist_ref[jnp.where(forward, 0, CX - 1)].astype(jnp.bfloat16)


def quarters(rank, space):
    high, core = (rank // 8 + space) % 2, rank % 2
    return 2 * high + (core + high) % 2, rank // 2 % 4


def kinetic_cells_of(step, vel_ref, space_ref, count_ref, cells_ref):
    x_quarter, y_quarter = quarters(vel_ref[0], space_ref[0])
    count = count_ref[step, space_ref[0]]
    shape = (LAYER, WIDTH)
    slot = lax.broadcasted_iota(jnp.int32, shape, 0)
    cell = (
        (BX * x_quarter + (slot >> 6)) * LAYER + BY * NZ * y_quarter + (slot & (LINE - 1))
    )
    lane = lax.broadcasted_iota(jnp.int32, (1, WIDTH), 1)
    found = jnp.zeros(shape, jnp.float32)
    for i in range(CX * LAYER // WIDTH):
        part = cells_ref[step : step + 1, WIDTH * i : WIDTH * (i + 1)]
        part = jnp.where(lane + WIDTH * i < count, part, -1)
        found = jnp.where(cell == part, 1.0, found)
    return jnp.broadcast_to(jnp.max(found, axis=1, keepdims=True), shape)


def rates_of(vel_ref, space_ref, rate_ref):
    x_quarter, y_quarter = quarters(vel_ref[0], space_ref[0])
    diagonal = lax.broadcasted_iota(jnp.int32, (NZ, NZ), 0) == lax.broadcasted_iota(
        jnp.int32, (NZ, NZ), 1
    )
    columns = []
    for x in range(BX):
        for y in range(BY):
            line = rate_ref[BX * x_quarter + x, pl.ds(BY * y_quarter + y, 1), :]
            column = jnp.sum(jnp.where(diagonal, line, 0.0), axis=1, keepdims=True)
            columns.append(jnp.broadcast_to(column, (NZ, WIDTH)))
    return jnp.concatenate(columns, axis=0)


def first_yz_kernel(f_ref, part_ref):
    uy, uz = speeds_yz()
    y_up = uy > 0.0
    z_up = uz > 0.0

    def layer(x, carry):
        def at(y):
            return f_ref[x, y % NY]

        up, _ = edges(at(-2), at(-1), at(0))
        next_up, next_down = edges(at(-1), at(0), at(1))
        flux_before = jnp.where(y_up, up, next_down)
        for y in range(NY):
            up = next_up
            next_up, next_down = edges(at(y), at(y + 1), at(y + 2))
            flux = jnp.where(y_up, up, next_down)
            here = at(y)
            part_ref[x, y] = here - uy * (flux - flux_before) - flux_change_z(here, uz, z_up)
            flux_before = flux
        return carry

    lax.fori_loop(0, CX, layer, 0)


def first_x_kernel(vel_ref, space_ref, f_ref, part_ref, behind_ref, ahead_ref, rows_ref):
    rank = vel_ref[0]
    forward = rank >= GROUPS // 2
    ux = jnp.abs(rank.astype(jnp.float32) - 0.5 * (GX - 1)) * (SPACING * COURANT)
    layers = [jnp.where(forward, k, CX - 1 - k) for k in range(CX)]
    starts = [(x % BX) * LINE for x in layers[:BX]]
    owners = []
    for k in range(4):
        quarter = jnp.where(forward, k, 3 - k)
        high = quarter // 2
        owners.append((high + space_ref[0]) % 2 * (GROUPS // 2) + (quarter + high) % 2)

    def line(quarter, y):
        inner = y * NZ
        y = quarter * BY + y

        def at(k):
            if k == -2:
                return behind_ref[jnp.where(forward, 0, 1), y].astype(jnp.float32)
            if k == -1:
                return behind_ref[jnp.where(forward, 1, 0), y].astype(jnp.float32)
            if k == CX:
                return ahead_ref[0, y].astype(jnp.float32)
            return f_ref[layers[k], y]

        face_before = upwind_face(at(-2), at(-1), at(0))
        for k in range(CX):
            face = upwind_face(at(k - 1), at(k), at(k + 1))
            result = part_ref[layers[k], y] - ux * (face - face_before)
            face_before = face
            start = pl.multiple_of(starts[k % BX] + inner, NZ)
            target = owners[k // BX] + quarter * 2
            rows_ref[target, pl.ds(start, NZ), :] = result.astype(jnp.bfloat16)

    def lines(quarter, carry):
        def one(y, inside):
            line(quarter, y)
            return inside

        lax.fori_loop(0, BY, one, 0)
        return carry

    lax.fori_loop(0, NY // BY, lines, 0)


def collide(rows, a_ref, b_ref, c_ref, project_ref, mix_ref, expand_ref, w_ref, hidden_ref):
    moments = jnp.dot(rows, project_ref[...], preferred_element_type=jnp.float32)
    for n in range(RANK // 256):
        cols = slice(256 * n, 256 * (n + 1))
        first = jnp.dot(rows, a_ref[:, cols], preferred_element_type=jnp.float32)
        second = jnp.dot(rows, b_ref[:, cols], preferred_element_type=jnp.float32)
        hidden_ref[:, cols] = (first * second).astype(jnp.bfloat16)
    return outcome(moments, c_ref, mix_ref, expand_ref, w_ref, hidden_ref)


def outcome(moments, c_ref, mix_ref, expand_ref, w_ref, hidden_ref):
    coeffs = jnp.dot(
        moments, mix_ref[...], precision=lax.Precision.HIGHEST, preferred_element_type=jnp.float32
    )
    lane = lax.broadcasted_iota(jnp.int32, coeffs.shape, 1)
    high = coeffs.astype(jnp.bfloat16).astype(jnp.float32)
    rest = coeffs - high
    middle = rest.astype(jnp.bfloat16).astype(jnp.float32)
    split = jnp.where(lane < 8, high, jnp.where(lane < 16, middle, rest - middle))
    split = split.astype(jnp.bfloat16)
    hidden = hidden_ref[...]
    for n in range(NV // 256):
        cols = slice(256 * n, 256 * (n + 1))
        collision = jnp.dot(hidden, c_ref[:, cols], preferred_element_type=jnp.float32)
        collision = collision.astype(jnp.bfloat16).astype(jnp.float32)
        poly = jnp.dot(split, expand_ref[:, cols], preferred_element_type=jnp.float32)
        equilibrium = poly * w_ref[:, cols]
        for half in range(2):
            part = slice(WIDTH * half, WIDTH * (half + 1))
            yield 2 * n + half, collision[:, part], equilibrium[:, part]


def first_collide_kernel(
    vel_ref, space_ref, count_ref, rows_ref, cells_ref, rate_ref, a_ref, b_ref, c_ref,
    project_ref, mix_ref, expand_ref, w_ref,
    f_ref, rates_ref, x_even_ref, x_odd_ref, y_even_ref, y_odd_ref, hidden_ref,
):
    rows = jnp.concatenate([rows_ref[g] for g in range(GROUPS)], axis=1)
    kinetic = kinetic_cells_of(0, vel_ref, space_ref, count_ref, cells_ref) > 0.0
    rate = rates_of(vel_ref, space_ref, rate_ref)
    rates_ref[...] = rate
    half = GROUPS // 2
    x_quarter, y_quarter = quarters(vel_ref[0], space_ref[0])
    x_is_even, y_is_even = x_quarter % 2 == 0, y_quarter % 2 == 0

    def put(even_ref, odd_ref, is_even, where, up, down):
        even_ref[where] = jnp.where(is_even, up, down).astype(jnp.bfloat16)
        odd_ref[where] = jnp.where(is_even, down, up).astype(jnp.bfloat16)

    low_lane = lax.broadcasted_iota(jnp.int32, (NZ, WIDTH), 1) < WIDTH // 2
    for g, collision, equilibrium in collide(
        rows, a_ref, b_ref, c_ref, project_ref, mix_ref, expand_ref, w_ref, hidden_ref
    ):
        moved = rows_ref[g].astype(jnp.float32)
        change = jnp.where(kinetic, COLLIDE * collision, rate * (equilibrium - moved))
        result = moved + change
        f_ref[g] = result
        put(x_even_ref, x_odd_ref, x_is_even, g, result[3 * LINE :], result[:LINE])
        low = g - half
        if low >= 0:
            put(
                x_even_ref, x_odd_ref, x_is_even, GROUPS + low,
                result[2 * LINE : 3 * LINE], f_ref[low, LINE : 2 * LINE],
            )
        for x in range(BX):
            here = slice(NZ * x, NZ * (x + 1))
            first, second, third, fourth = (
                slice(LINE * x + NZ * y, LINE * x + NZ * (y + 1)) for y in range(BY)
            )
            put(y_even_ref, y_odd_ref, y_is_even, (g, here), result[fourth], result[first])
            if low >= 0:
                put(
                    y_even_ref, y_odd_ref, y_is_even, (GROUPS + low, here),
                    jnp.where(
                        low_lane, pltpu.roll(f_ref[low, third], WIDTH // 2, 1), result[third]
                    ),
                    jnp.where(
                        low_lane, f_ref[low, second], pltpu.roll(result[second], WIDTH // 2, 1)
                    ),
                )


def second_z_kernel(vel_ref, space_ref, count_ref, f_ref, cells_ref, part_ref, mask_ref):
    mask_ref[...] = kinetic_cells_of(1, vel_ref, space_ref, count_ref, cells_ref)
    _, uz = speeds_yz()
    z_up = uz > 0.0

    def group(g, carry):
        for c in range(BX * BY):
            here = slice(NZ * c, NZ * (c + 1))
            f = f_ref[g, here]
            part_ref[g, here] = f - flux_change_z(f, uz, z_up)
        return carry

    lax.fori_loop(0, GROUPS, group, 0)


def second_kernel(
    vel_ref, space_ref, f_ref, part_ref, x_odd_ref, y_even_ref, y_odd_ref, x_even_ref,
    mask_ref, rates_ref, a_ref, b_ref, c_ref, project_ref, mix_ref, expand_ref, w_ref,
    out_ref, hidden_ref, moved_ref, first_ref, second_ref,
):
    uy, _ = speeds_yz()
    y_up = uy > 0.0
    half = GROUPS // 2

    x_quarter, y_quarter = quarters(vel_ref[0], space_ref[0])
    x_is_even, y_is_even = x_quarter % 2 == 0, y_quarter % 2 == 0

    def arrived(even_ref, odd_ref, is_even, g, i):
        even = even_ref[g, NZ * i : NZ * (i + 1)].astype(jnp.float32)
        odd = odd_ref[g, NZ * i : NZ * (i + 1)].astype(jnp.float32)
        return jnp.where(is_even, odd, even), jnp.where(is_even, even, odd)

    def group(pair, upward):
        g = pair + half if upward else pair
        extra = pair + GROUPS
        ux = abs(g - 0.5 * (GX - 1)) * (SPACING * COURANT)
        for y in range(BY):
            here_x = (x_even_ref, x_odd_ref, x_is_even)
            behind, ahead = arrived(*here_x, g, y)[:: 1 if upward else -1]
            line = [arrived(*here_x, extra, y)[0 if upward else 1], behind]
            for k in range(BX):
                x = k if upward else BX - 1 - k
                line.append(f_ref[g, LINE * x + NZ * y : LINE * x + NZ * (y + 1)])
            line.append(ahead)

            def at_x(k):
                return line[k + 2]

            face_before = upwind_face(at_x(-2), at_x(-1), at_x(0))
            for k in range(BX):
                x = k if upward else BX - 1 - k
                face = upwind_face(at_x(k - 1), at_x(k), at_x(k + 1))
                here = slice(LINE * x + NZ * y, LINE * x + NZ * (y + 1))
                moved_ref[g, here] = part_ref[g, here] - ux * (face - face_before)
                face_before = face
        for x in range(BX):
            here_y = (y_even_ref, y_odd_ref, y_is_even)
            below, above = arrived(*here_y, g, x)
            below_2, above_2 = arrived(*here_y, extra, x)
            if upward:
                above_2 = pltpu.roll(above_2, WIDTH // 2, 1)
            else:
                below_2 = pltpu.roll(below_2, WIDTH // 2, 1)
            column = [below_2, below]
            for y in range(BY):
                column.append(f_ref[g, LINE * x + NZ * y : LINE * x + NZ * (y + 1)])
            column += [above, above_2]

            def at_y(y):
                return column[y + 2]

            up, _ = edges(at_y(-2), at_y(-1), at_y(0))
            next_up, next_down = edges(at_y(-1), at_y(0), at_y(1))
            flux_before = jnp.where(y_up, up, next_down)
            for y in range(BY):
                up = next_up
                next_up, next_down = edges(at_y(y), at_y(y + 1), at_y(y + 2))
                flux = jnp.where(y_up, up, next_down)
                here = slice(LINE * x + NZ * y, LINE * x + NZ * (y + 1))
                moved_ref[g, here] = moved_ref[g, here] - uy * (flux - flux_before)
                flux_before = flux

    moments = jnp.zeros((LAYER, WIDTH), jnp.float32)
    chunk = 1
    for pair in range(0, half, chunk):
        groups = []
        for upward in (False, True):
            for i in range(chunk):
                group(pair + i, upward)
                groups.append(pair + i + (half if upward else 0))
        rows = jnp.concatenate([moved_ref[g].astype(jnp.bfloat16) for g in groups], axis=1)
        spans = [
            slice(WIDTH * g, WIDTH * (g + chunk)) for g in (pair, pair + half)
        ]

        def times(ref, cols):
            right = jnp.concatenate([ref[span, cols] for span in spans], axis=0)
            return jnp.dot(rows, right, preferred_element_type=jnp.float32)

        moments += times(project_ref, slice(0, WIDTH))
        for n in range(RANK // 256):
            cols = slice(256 * n, 256 * (n + 1))
            first, second = times(a_ref, cols), times(b_ref, cols)
            if pair:
                first += first_ref[:, cols]
                second += second_ref[:, cols]
            if pair + chunk < half:
                first_ref[:, cols] = first
                second_ref[:, cols] = second
            else:
                hidden_ref[:, cols] = (first * second).astype(jnp.bfloat16)
    rate = rates_ref[...]
    kinetic = mask_ref[...] > 0.0
    for g, collision, equilibrium in outcome(
        moments, c_ref, mix_ref, expand_ref, w_ref, hidden_ref
    ):
        moved = moved_ref[g]
        change = jnp.where(kinetic, COLLIDE * collision, rate * (equilibrium - moved))
        out_ref[g] = (moved + change).astype(jnp.bfloat16)


def place_kernel(space_ref, in_ref, out_hbm, out_ref, sems):
    stores = []
    for quarter in range(4):
        high = quarter // 2
        core = (quarter % 2) ^ high
        first = (high + space_ref[0]) % 2 * (GROUPS // 2) + core
        for x in range(BX):
            for y_quarter in range(4):
                for y in range(BY):
                    c = LINE * x + NZ * y
                    out_ref[BX * quarter + x, BY * y_quarter + y] = in_ref[
                        first + y_quarter * 2, c : c + NZ
                    ].astype(jnp.float32)
        part = slice(BX * quarter, BX * (quarter + 1))
        stores.append(pltpu.make_async_copy(out_ref.at[part], out_hbm.at[part], sems.at[quarter]))
        stores[-1].start()
    for store in stores:
        store.wait()


def device_of(space, high, x, core):
    return (space * 2 + high) * 8 + x * 2 + core


def holder_of(space, quarter, x):
    high = quarter // 2
    return device_of(space, (high + space) % 2, x, (quarter + high) % 2)


def steps_of(slabs):
    upwind, downwind = [], []
    x_even, x_odd, y_even, y_odd = [], [], [], []
    for space in range(slabs):
        before, after = (space - 1) % slabs, (space + 1) % slabs
        for quarter in range(4):
            next_x = holder_place(space, quarter + 1, slabs)
            last_x = holder_place(space, quarter - 1, slabs)
            for x in range(4):
                me = holder_of(space, quarter, x)
                rank = me % GROUPS
                forward = rank >= GROUPS // 2
                upwind.append((me, (after if forward else before) * GROUPS + rank))
                downwind.append((me, (before if forward else after) * GROUPS + rank))
                up, down = holder_of(*next_x, x), holder_of(*last_x, x)
                x_even.append((me, down if quarter % 2 else up))
                x_odd.append((me, up if quarter % 2 else down))
                up, down = (holder_of(space, quarter, (x + d) % 4) for d in (1, -1))
                y_even.append((me, down if x % 2 else up))
                y_odd.append((me, up if x % 2 else down))
    return upwind, downwind, x_even, x_odd, y_even, y_odd


def holder_place(space, quarter, slabs):
    return (space + quarter // 4) % slabs, quarter % 4


def body(dist, relax_rate, kinetic_cells, kinetic_count, map_a, map_b, map_c):
    vel = (lax.axis_index("vel").astype(jnp.int32).reshape(1), SMEM)
    space = (lax.axis_index("space").astype(jnp.int32).reshape(1), SMEM)
    both = ("space", "vel")
    upwind, downwind, *pairs = steps_of(lax.axis_size("space"))
    project, mix, expand, w = tables()
    consts = (jnp.asarray(project), jnp.asarray(mix), jnp.asarray(expand), jnp.asarray(w))
    layers = (NY, NZ, WIDTH)
    behind, ahead = call(
        first_halo_kernel, "first_halo", (vel, space, (dist, VMEM)),
        (((2,) + layers, jnp.bfloat16, VMEM), ((1,) + layers, jnp.bfloat16, VMEM)),
    )
    behind = lax.ppermute(behind, both, upwind)
    ahead = lax.ppermute(ahead, both, downwind)

    state = ((CX,) + layers, jnp.float32, VMEM)
    wide = (GROUPS, LAYER, WIDTH)
    halo = (GROUPS + GROUPS // 2, LINE, WIDTH)
    half = jnp.bfloat16
    hidden = VMEM((LAYER, RANK), half)

    (part,) = call(first_yz_kernel, "first_yz", ((dist, VMEM),), (state,), flops=12_000_000)
    (rows,) = call(
        first_x_kernel, "first_x", (vel, space) + tuple((o, VMEM) for o in (dist, part, behind, ahead)),
        ((wide, half, VMEM),), flops=6_000_000,
    )
    gathered = lax.all_to_all(rows, "vel", split_axis=0, concat_axis=0, tiled=True)
    facts = (vel, space, (kinetic_count, SMEM))
    lanes = ((LAYER, WIDTH), jnp.float32, VMEM)
    held = tuple((o, VMEM) for o in (map_a, map_b, map_c) + consts)
    f, rates, *halos = call(
        first_collide_kernel, "first_collide",
        facts + ((gathered, VMEM), (kinetic_cells, VMEM), (relax_rate, VMEM)) + held,
        ((wide, jnp.float32, VMEM), lanes) + ((halo, half, VMEM),) * 4,
        scratch=(hidden,), flops=2_500_000_000, limit=C_VMEM,
    )
    x_even, x_odd, y_even, y_odd = (
        lax.ppermute(o, both, p) for o, p in zip(halos, pairs, strict=True)
    )
    part, mask = call(
        second_z_kernel, "second_z", facts + ((f, VMEM), (kinetic_cells, VMEM)),
        ((wide, jnp.float32, VMEM), lanes), flops=6_000_000,
    )
    sums = VMEM((LAYER, RANK), jnp.float32)
    (result,) = call(
        second_kernel, "second_xy_collide",
        (vel, space)
        + tuple((o, VMEM) for o in (f, part, x_odd, y_even, y_odd, x_even, mask, rates)) + held,
        ((wide, half, VMEM),), scratch=(hidden, VMEM(wide, jnp.float32), sums, sums),
        flops=2_500_000_000, limit=C_VMEM,
    )
    pieces = lax.all_to_all(result, "vel", split_axis=0, concat_axis=0, tiled=True)
    (out,) = call(
        place_kernel, "place", (space, (pieces, VMEM)), (((CX,) + layers, jnp.float32, HBM),),
        scratch=(VMEM((CX,) + layers, jnp.float32), DMA((4,))),
    )
    return out


def solution(mesh):
    return jax.shard_map(
        body,
        mesh=mesh,
        in_specs=(
            P("space", None, None, "vel"),
            P("space", None, None),
            P(None, "space"),
            P(),
            P(),
            P(),
            P(),
        ),
        out_specs=P("space", None, None, "vel"),
        check_vma=False,
    )
```

```python
import jax
import jax.numpy as jnp
import numpy as np
from jax import lax
from jax.experimental import pallas as pl
from jax.experimental.pallas import tpu as pltpu
from jax.sharding import PartitionSpec as P

GX = 16
GY = 16
GZ = 8
NV = GX * GY * GZ
RANK = 768
COURANT = 0.1
SPACING = 0.5
COLLIDE = 0.5

CX = 16
NY = 16
NZ = 16
LAYER = NY * NZ
WIDTH = 128
GROUPS = NV // WIDTH
OFFSET = 3.0 / 16.0
BX = 4
BY = 4
LINE = BX * NZ


def tables():
    k = np.arange(NV)
    vx = ((k // (GY * GZ)) - 0.5 * (GX - 1)) * SPACING
    vy = ((k // GZ % GY) - 0.5 * (GY - 1)) * SPACING
    vz = ((k % GZ) - 0.5 * (GZ - 1)) * SPACING
    s = vx * vx + vy * vy + vz * vz
    w = np.exp(-0.5 * s)
    w = w / w.sum()
    sx, sy, sz = (w * vx * vx).sum(), (w * vy * vy).sum(), (w * vz * vz).sum()
    m2, m4 = (w * s).sum(), (w * s * s).sum()
    basis = np.stack([np.ones(NV), vx, vy, vz, s - OFFSET])
    q = np.zeros((5, 5))
    scale = 1.0 / (m4 - m2 * m2)
    thermal = np.zeros(5)
    thermal[0] = (OFFSET - m2) * scale
    thermal[4] = scale
    q[:, 4] = thermal
    q[:, 0] = (OFFSET - m2) * thermal
    q[0, 0] += 1.0
    q[1, 1], q[2, 2], q[3, 3] = 1.0 / sx, 1.0 / sy, 1.0 / sz
    project = np.zeros((NV, 128))
    project[:, :5] = basis.T
    mix = np.zeros((128, 128))
    expand = np.zeros((128, NV))
    for part in range(3):
        mix[:5, 8 * part : 8 * part + 5] = q
        expand[8 * part : 8 * part + 5] = basis
    return (
        project.astype(jnp.bfloat16),
        mix.astype(np.float32),
        expand.astype(jnp.bfloat16),
        w.reshape(1, NV).astype(np.float32),
    )


def minmod_half(a, b):
    return 0.5 * (jnp.maximum(jnp.minimum(a, b), 0.0) + jnp.minimum(jnp.maximum(a, b), 0.0))


C_VMEM = 12 << 20
HBM = pltpu.HBM
VMEM = pltpu.VMEM
SMEM = pltpu.SMEM
DMA = pltpu.SemaphoreType.DMA


def call(kernel, name, operands, outs, scratch=(), flops=0, limit=8 << 20):
    shapes = [jax.ShapeDtypeStruct(shape, dtype) for shape, dtype, _ in outs]
    arrays = [o for o, _ in operands]
    moved = sum(o.size * o.dtype.itemsize for o in arrays + shapes)
    return pl.pallas_call(
        kernel,
        out_shape=tuple(shapes),
        in_specs=[pl.BlockSpec(memory_space=space) for _, space in operands],
        out_specs=tuple(pl.BlockSpec(memory_space=space) for _, _, space in outs),
        scratch_shapes=list(scratch),
        compiler_params=pltpu.CompilerParams(vmem_limit_bytes=limit),
        cost_estimate=pl.CostEstimate(flops=flops, bytes_accessed=moved, transcendentals=0),
        name=name,
    )(*arrays)


def speeds_yz():
    lane = lax.broadcasted_iota(jnp.int32, (NZ, WIDTH), 1)
    along_y = (lane >> 3).astype(jnp.float32) - 0.5 * (GY - 1)
    along_z = (lane & (GZ - 1)).astype(jnp.float32) - 0.5 * (GZ - 1)
    return along_y * (SPACING * COURANT), along_z * (SPACING * COURANT)


def flux_change_z(f, uz, z_up):
    dz = pltpu.roll(f, NZ - 1, 0) - f
    slope = minmod_half(pltpu.roll(dz, 1, 0), dz)
    down = pltpu.roll(f - slope, NZ - 1, 0)
    flux = jnp.where(z_up, f + slope, down)
    return uz * (flux - pltpu.roll(flux, 1, 0))


def edges(before, here, after):
    slope = minmod_half(here - before, after - here)
    return here + slope, here - slope


def upwind_face(before, here, after):
    return here + minmod_half(here - before, after - here)


def first_halo_kernel(vel_ref, space_ref, dist_ref, behind_ref, ahead_ref):
    forward = vel_ref[0] >= GROUPS // 2
    start = jnp.where(forward, CX - 2, 0)
    for i in range(2):
        behind_ref[i] = dist_ref[start + i].astype(jnp.bfloat16)
    ahead_ref[0] = dist_ref[jnp.where(forward, 0, CX - 1)].astype(jnp.bfloat16)


def quarters(rank, space):
    high, core = (rank // 8 + space) % 2, rank % 2
    return 2 * high + (core + high) % 2, rank // 2 % 4


def kinetic_cells_of(step, vel_ref, space_ref, count_ref, cells_ref):
    x_quarter, y_quarter = quarters(vel_ref[0], space_ref[0])
    count = count_ref[step, space_ref[0]]
    shape = (LAYER, WIDTH)
    slot = lax.broadcasted_iota(jnp.int32, shape, 0)
    cell = (
        (BX * x_quarter + (slot >> 6)) * LAYER + BY * NZ * y_quarter + (slot & (LINE - 1))
    )
    lane = lax.broadcasted_iota(jnp.int32, (1, WIDTH), 1)
    found = jnp.zeros(shape, jnp.float32)
    for i in range(CX * LAYER // WIDTH):
        part = cells_ref[step : step + 1, WIDTH * i : WIDTH * (i + 1)]
        part = jnp.where(lane + WIDTH * i < count, part, -1)
        found = jnp.where(cell == part, 1.0, found)
    return jnp.broadcast_to(jnp.max(found, axis=1, keepdims=True), shape)


def rates_of(vel_ref, space_ref, rate_ref):
    x_quarter, y_quarter = quarters(vel_ref[0], space_ref[0])
    diagonal = lax.broadcasted_iota(jnp.int32, (NZ, NZ), 0) == lax.broadcasted_iota(
        jnp.int32, (NZ, NZ), 1
    )
    columns = []
    for x in range(BX):
        for y in range(BY):
            line = rate_ref[BX * x_quarter + x, pl.ds(BY * y_quarter + y, 1), :]
            column = jnp.sum(jnp.where(diagonal, line, 0.0), axis=1, keepdims=True)
            columns.append(jnp.broadcast_to(column, (NZ, WIDTH)))
    return jnp.concatenate(columns, axis=0)


def first_yz_kernel(f_ref, part_ref):
    uy, uz = speeds_yz()
    y_up = uy > 0.0
    z_up = uz > 0.0

    def layer(x, carry):
        def at(y):
            return f_ref[x, y % NY]

        up, _ = edges(at(-2), at(-1), at(0))
        next_up, next_down = edges(at(-1), at(0), at(1))
        flux_before = jnp.where(y_up, up, next_down)
        for y in range(NY):
            up = next_up
            next_up, next_down = edges(at(y), at(y + 1), at(y + 2))
            flux = jnp.where(y_up, up, next_down)
            here = at(y)
            part_ref[x, y] = here - uy * (flux - flux_before) - flux_change_z(here, uz, z_up)
            flux_before = flux
        return carry

    lax.fori_loop(0, CX, layer, 0)


def first_x_kernel(vel_ref, space_ref, f_ref, part_ref, behind_ref, ahead_ref, rows_ref):
    rank = vel_ref[0]
    forward = rank >= GROUPS // 2
    ux = jnp.abs(rank.astype(jnp.float32) - 0.5 * (GX - 1)) * (SPACING * COURANT)
    layers = [jnp.where(forward, k, CX - 1 - k) for k in range(CX)]
    starts = [(x % BX) * LINE for x in layers[:BX]]
    owners = []
    for k in range(4):
        quarter = jnp.where(forward, k, 3 - k)
        high = quarter // 2
        owners.append((high + space_ref[0]) % 2 * (GROUPS // 2) + (quarter + high) % 2)

    def line(quarter, y):
        inner = y * NZ
        y = quarter * BY + y

        def at(k):
            if k == -2:
                return behind_ref[jnp.where(forward, 0, 1), y].astype(jnp.float32)
            if k == -1:
                return behind_ref[jnp.where(forward, 1, 0), y].astype(jnp.float32)
            if k == CX:
                return ahead_ref[0, y].astype(jnp.float32)
            return f_ref[layers[k], y]

        face_before = upwind_face(at(-2), at(-1), at(0))
        for k in range(CX):
            face = upwind_face(at(k - 1), at(k), at(k + 1))
            result = part_ref[layers[k], y] - ux * (face - face_before)
            face_before = face
            start = pl.multiple_of(starts[k % BX] + inner, NZ)
            target = owners[k // BX] + quarter * 2
            rows_ref[target, pl.ds(start, NZ), :] = result.astype(jnp.bfloat16)

    def lines(quarter, carry):
        def one(y, inside):
            line(quarter, y)
            return inside

        lax.fori_loop(0, BY, one, 0)
        return carry

    lax.fori_loop(0, NY // BY, lines, 0)


def collide(rows, a_ref, b_ref, c_ref, project_ref, mix_ref, expand_ref, w_ref, hidden_ref):
    moments = jnp.dot(rows, project_ref[...], preferred_element_type=jnp.float32)
    for n in range(RANK // 256):
        cols = slice(256 * n, 256 * (n + 1))
        first = jnp.dot(rows, a_ref[:, cols], preferred_element_type=jnp.float32)
        second = jnp.dot(rows, b_ref[:, cols], preferred_element_type=jnp.float32)
        hidden_ref[:, cols] = (first * second).astype(jnp.bfloat16)
    return outcome(moments, c_ref, mix_ref, expand_ref, w_ref, hidden_ref)


def outcome(moments, c_ref, mix_ref, expand_ref, w_ref, hidden_ref):
    coeffs = jnp.dot(
        moments, mix_ref[...], precision=lax.Precision.HIGHEST, preferred_element_type=jnp.float32
    )
    lane = lax.broadcasted_iota(jnp.int32, coeffs.shape, 1)
    high = coeffs.astype(jnp.bfloat16).astype(jnp.float32)
    rest = coeffs - high
    middle = rest.astype(jnp.bfloat16).astype(jnp.float32)
    split = jnp.where(lane < 8, high, jnp.where(lane < 16, middle, rest - middle))
    split = split.astype(jnp.bfloat16)
    hidden = hidden_ref[...]
    for n in range(NV // 256):
        cols = slice(256 * n, 256 * (n + 1))
        collision = jnp.dot(hidden, c_ref[:, cols], preferred_element_type=jnp.float32)
        collision = collision.astype(jnp.bfloat16).astype(jnp.float32)
        poly = jnp.dot(split, expand_ref[:, cols], preferred_element_type=jnp.float32)
        equilibrium = poly * w_ref[:, cols]
        for half in range(2):
            part = slice(WIDTH * half, WIDTH * (half + 1))
            yield 2 * n + half, collision[:, part], equilibrium[:, part]


def first_collide_kernel(
    vel_ref, space_ref, count_ref, rows_ref, cells_ref, rate_ref, a_ref, b_ref, c_ref,
    project_ref, mix_ref, expand_ref, w_ref,
    f_ref, rates_ref, x_even_ref, x_odd_ref, y_even_ref, y_odd_ref, hidden_ref,
):
    rows = jnp.concatenate([rows_ref[g] for g in range(GROUPS)], axis=1)
    kinetic = kinetic_cells_of(0, vel_ref, space_ref, count_ref, cells_ref) > 0.0
    rate = rates_of(vel_ref, space_ref, rate_ref)
    rates_ref[...] = rate
    half = GROUPS // 2
    x_quarter, y_quarter = quarters(vel_ref[0], space_ref[0])
    x_is_even, y_is_even = x_quarter % 2 == 0, y_quarter % 2 == 0

    def put(even_ref, odd_ref, is_even, where, up, down):
        even_ref[where] = jnp.where(is_even, up, down).astype(jnp.bfloat16)
        odd_ref[where] = jnp.where(is_even, down, up).astype(jnp.bfloat16)

    low_lane = lax.broadcasted_iota(jnp.int32, (NZ, WIDTH), 1) < WIDTH // 2
    for g, collision, equilibrium in collide(
        rows, a_ref, b_ref, c_ref, project_ref, mix_ref, expand_ref, w_ref, hidden_ref
    ):
        moved = rows_ref[g].astype(jnp.float32)
        change = jnp.where(kinetic, COLLIDE * collision, rate * (equilibrium - moved))
        result = moved + change
        f_ref[g] = result
        put(x_even_ref, x_odd_ref, x_is_even, g, result[3 * LINE :], result[:LINE])
        low = g - half
        if low >= 0:
            put(
                x_even_ref, x_odd_ref, x_is_even, GROUPS + low,
                result[2 * LINE : 3 * LINE], f_ref[low, LINE : 2 * LINE],
            )
        for x in range(BX):
            here = slice(NZ * x, NZ * (x + 1))
            first, second, third, fourth = (
                slice(LINE * x + NZ * y, LINE * x + NZ * (y + 1)) for y in range(BY)
            )
            put(y_even_ref, y_odd_ref, y_is_even, (g, here), result[fourth], result[first])
            if low >= 0:
                put(
                    y_even_ref, y_odd_ref, y_is_even, (GROUPS + low, here),
                    jnp.where(
                        low_lane, pltpu.roll(f_ref[low, third], WIDTH // 2, 1), result[third]
                    ),
                    jnp.where(
                        low_lane, f_ref[low, second], pltpu.roll(result[second], WIDTH // 2, 1)
                    ),
                )


def second_z_kernel(vel_ref, space_ref, count_ref, f_ref, cells_ref, part_ref, mask_ref):
    mask_ref[...] = kinetic_cells_of(1, vel_ref, space_ref, count_ref, cells_ref)
    _, uz = speeds_yz()
    z_up = uz > 0.0

    half = GROUPS // 2

    def group(g, upward):
        ux = jnp.abs(g.astype(jnp.float32) - 0.5 * (GX - 1)) * (SPACING * COURANT)
        for y in range(BY):
            places = []
            for k in range(BX):
                x = k if upward else BX - 1 - k
                places.append(slice(LINE * x + NZ * y, LINE * x + NZ * (y + 1)))
            line = [f_ref[g, here] for here in places]
            face_1 = ux * upwind_face(line[0], line[1], line[2])
            face_2 = ux * upwind_face(line[1], line[2], line[3])
            inner = [None, face_1, face_2 - face_1, -face_2]
            for here, f, change in zip(places, line, inner, strict=True):
                part = f - flux_change_z(f, uz, z_up)
                part_ref[g, here] = part if change is None else part - change

    def downwards(g, carry):
        group(g, False)
        return carry

    def upwards(g, carry):
        group(g, True)
        return carry

    lax.fori_loop(0, half, downwards, 0)
    lax.fori_loop(half, GROUPS, upwards, 0)


def second_kernel(
    vel_ref, space_ref, f_ref, part_ref, x_odd_ref, y_even_ref, y_odd_ref, x_even_ref,
    mask_ref, rates_ref, a_ref, b_ref, c_ref, project_ref, mix_ref, expand_ref, w_ref,
    out_ref, hidden_ref, moved_ref, first_ref, second_ref,
):
    uy, _ = speeds_yz()
    y_up = uy > 0.0
    half = GROUPS // 2

    x_quarter, y_quarter = quarters(vel_ref[0], space_ref[0])
    x_is_even, y_is_even = x_quarter % 2 == 0, y_quarter % 2 == 0

    def arrived(even_ref, odd_ref, is_even, g, i):
        even = even_ref[g, NZ * i : NZ * (i + 1)].astype(jnp.float32)
        odd = odd_ref[g, NZ * i : NZ * (i + 1)].astype(jnp.float32)
        return jnp.where(is_even, odd, even), jnp.where(is_even, even, odd)

    def group(pair, upward):
        g = pair + half if upward else pair
        extra = pair + GROUPS
        partial = {}
        ux = abs(g - 0.5 * (GX - 1)) * (SPACING * COURANT)
        for y in range(BY):
            here_x = (x_even_ref, x_odd_ref, x_is_even)
            behind, ahead = arrived(*here_x, g, y)[:: 1 if upward else -1]
            line = [arrived(*here_x, extra, y)[0 if upward else 1], behind]
            for k in range(BX):
                x = k if upward else BX - 1 - k
                line.append(f_ref[g, LINE * x + NZ * y : LINE * x + NZ * (y + 1)])
            line.append(ahead)

            def at_x(k):
                return line[k + 2]

            face_0 = upwind_face(at_x(-1), at_x(0), at_x(1))
            outer = [
                face_0 - upwind_face(at_x(-2), at_x(-1), at_x(0)), -face_0, None,
                upwind_face(at_x(2), at_x(3), at_x(4)),
            ]
            for k in range(BX):
                x = k if upward else BX - 1 - k
                here = slice(LINE * x + NZ * y, LINE * x + NZ * (y + 1))
                part = part_ref[g, here]
                partial[x, y] = part if outer[k] is None else part - ux * outer[k]
        for x in range(BX):
            here_y = (y_even_ref, y_odd_ref, y_is_even)
            below, above = arrived(*here_y, g, x)
            below_2, above_2 = arrived(*here_y, extra, x)
            if upward:
                above_2 = pltpu.roll(above_2, WIDTH // 2, 1)
            else:
                below_2 = pltpu.roll(below_2, WIDTH // 2, 1)
            column = [below_2, below]
            for y in range(BY):
                column.append(f_ref[g, LINE * x + NZ * y : LINE * x + NZ * (y + 1)])
            column += [above, above_2]

            def at_y(y):
                return column[y + 2]

            up, _ = edges(at_y(-2), at_y(-1), at_y(0))
            next_up, next_down = edges(at_y(-1), at_y(0), at_y(1))
            flux_before = jnp.where(y_up, up, next_down)
            for y in range(BY):
                up = next_up
                next_up, next_down = edges(at_y(y), at_y(y + 1), at_y(y + 2))
                flux = jnp.where(y_up, up, next_down)
                here = slice(LINE * x + NZ * y, LINE * x + NZ * (y + 1))
                moved_ref[g, here] = partial[x, y] - uy * (flux - flux_before)
                flux_before = flux

    moments = jnp.zeros((LAYER, WIDTH), jnp.float32)
    chunk = 1
    for pair in range(0, half, chunk):
        groups = []
        for upward in (False, True):
            for i in range(chunk):
                group(pair + i, upward)
                groups.append(pair + i + (half if upward else 0))
        rows = jnp.concatenate([moved_ref[g].astype(jnp.bfloat16) for g in groups], axis=1)
        spans = [
            slice(WIDTH * g, WIDTH * (g + chunk)) for g in (pair, pair + half)
        ]

        def times(ref, cols):
            right = jnp.concatenate([ref[span, cols] for span in spans], axis=0)
            return jnp.dot(rows, right, preferred_element_type=jnp.float32)

        moments += times(project_ref, slice(0, WIDTH))
        for n in range(RANK // 256):
            cols = slice(256 * n, 256 * (n + 1))
            first, second = times(a_ref, cols), times(b_ref, cols)
            if pair:
                first += first_ref[:, cols]
                second += second_ref[:, cols]
            if pair + chunk < half:
                first_ref[:, cols] = first
                second_ref[:, cols] = second
            else:
                hidden_ref[:, cols] = (first * second).astype(jnp.bfloat16)
    rate = rates_ref[...]
    kinetic = mask_ref[...] > 0.0
    for g, collision, equilibrium in outcome(
        moments, c_ref, mix_ref, expand_ref, w_ref, hidden_ref
    ):
        moved = moved_ref[g]
        change = jnp.where(kinetic, COLLIDE * collision, rate * (equilibrium - moved))
        out_ref[g] = (moved + change).astype(jnp.bfloat16)


def place_kernel(space_ref, in_ref, out_hbm, out_ref, sems):
    stores = []
    for quarter in range(4):
        high = quarter // 2
        core = (quarter % 2) ^ high
        first = (high + space_ref[0]) % 2 * (GROUPS // 2) + core
        for x in range(BX):
            for y_quarter in range(4):
                for y in range(BY):
                    c = LINE * x + NZ * y
                    out_ref[BX * quarter + x, BY * y_quarter + y] = in_ref[
                        first + y_quarter * 2, c : c + NZ
                    ].astype(jnp.float32)
        part = slice(BX * quarter, BX * (quarter + 1))
        stores.append(pltpu.make_async_copy(out_ref.at[part], out_hbm.at[part], sems.at[quarter]))
        stores[-1].start()
    for store in stores:
        store.wait()


def device_of(space, high, x, core):
    return (space * 2 + high) * 8 + x * 2 + core


def holder_of(space, quarter, x):
    high = quarter // 2
    return device_of(space, (high + space) % 2, x, (quarter + high) % 2)


def steps_of(slabs):
    upwind, downwind = [], []
    x_even, x_odd, y_even, y_odd = [], [], [], []
    for space in range(slabs):
        before, after = (space - 1) % slabs, (space + 1) % slabs
        for quarter in range(4):
            next_x = holder_place(space, quarter + 1, slabs)
            last_x = holder_place(space, quarter - 1, slabs)
            for x in range(4):
                me = holder_of(space, quarter, x)
                rank = me % GROUPS
                forward = rank >= GROUPS // 2
                upwind.append((me, (after if forward else before) * GROUPS + rank))
                downwind.append((me, (before if forward else after) * GROUPS + rank))
                up, down = holder_of(*next_x, x), holder_of(*last_x, x)
                x_even.append((me, down if quarter % 2 else up))
                x_odd.append((me, up if quarter % 2 else down))
                up, down = (holder_of(space, quarter, (x + d) % 4) for d in (1, -1))
                y_even.append((me, down if x % 2 else up))
                y_odd.append((me, up if x % 2 else down))
    return upwind, downwind, x_even, x_odd, y_even, y_odd


def holder_place(space, quarter, slabs):
    return (space + quarter // 4) % slabs, quarter % 4


def body(dist, relax_rate, kinetic_cells, kinetic_count, map_a, map_b, map_c):
    vel = (lax.axis_index("vel").astype(jnp.int32).reshape(1), SMEM)
    space = (lax.axis_index("space").astype(jnp.int32).reshape(1), SMEM)
    both = ("space", "vel")
    upwind, downwind, *pairs = steps_of(lax.axis_size("space"))
    project, mix, expand, w = tables()
    consts = (jnp.asarray(project), jnp.asarray(mix), jnp.asarray(expand), jnp.asarray(w))
    layers = (NY, NZ, WIDTH)
    behind, ahead = call(
        first_halo_kernel, "first_halo", (vel, space, (dist, VMEM)),
        (((2,) + layers, jnp.bfloat16, VMEM), ((1,) + layers, jnp.bfloat16, VMEM)),
    )
    behind = lax.ppermute(behind, both, upwind)
    ahead = lax.ppermute(ahead, both, downwind)

    state = ((CX,) + layers, jnp.float32, VMEM)
    wide = (GROUPS, LAYER, WIDTH)
    halo = (GROUPS + GROUPS // 2, LINE, WIDTH)
    half = jnp.bfloat16
    hidden = VMEM((LAYER, RANK), half)

    (part,) = call(first_yz_kernel, "first_yz", ((dist, VMEM),), (state,), flops=12_000_000)
    (rows,) = call(
        first_x_kernel, "first_x", (vel, space) + tuple((o, VMEM) for o in (dist, part, behind, ahead)),
        ((wide, half, VMEM),), flops=6_000_000,
    )
    gathered = lax.all_to_all(rows, "vel", split_axis=0, concat_axis=0, tiled=True)
    facts = (vel, space, (kinetic_count, SMEM))
    lanes = ((LAYER, WIDTH), jnp.float32, VMEM)
    held = tuple((o, VMEM) for o in (map_a, map_b, map_c) + consts)
    f, rates, *halos = call(
        first_collide_kernel, "first_collide",
        facts + ((gathered, VMEM), (kinetic_cells, VMEM), (relax_rate, VMEM)) + held,
        ((wide, jnp.float32, VMEM), lanes) + ((halo, half, VMEM),) * 4,
        scratch=(hidden,), flops=2_500_000_000, limit=C_VMEM,
    )
    x_even, x_odd, y_even, y_odd = (
        lax.ppermute(o, both, p) for o, p in zip(halos, pairs, strict=True)
    )
    part, mask = call(
        second_z_kernel, "second_z", facts + ((f, VMEM), (kinetic_cells, VMEM)),
        ((wide, jnp.float32, VMEM), lanes), flops=6_000_000,
    )
    sums = VMEM((LAYER, RANK), jnp.float32)
    (result,) = call(
        second_kernel, "second_xy_collide",
        (vel, space)
        + tuple((o, VMEM) for o in (f, part, x_odd, y_even, y_odd, x_even, mask, rates)) + held,
        ((wide, half, VMEM),), scratch=(hidden, VMEM(wide, jnp.float32), sums, sums),
        flops=2_500_000_000, limit=C_VMEM,
    )
    pieces = lax.all_to_all(result, "vel", split_axis=0, concat_axis=0, tiled=True)
    (out,) = call(
        place_kernel, "place", (space, (pieces, VMEM)), (((CX,) + layers, jnp.float32, HBM),),
        scratch=(VMEM((CX,) + layers, jnp.float32), DMA((4,))),
    )
    return out


def solution(mesh):
    return jax.shard_map(
        body,
        mesh=mesh,
        in_specs=(
            P("space", None, None, "vel"),
            P("space", None, None),
            P(None, "space"),
            P(),
            P(),
            P(),
            P(),
        ),
        out_specs=P("space", None, None, "vel"),
        check_vma=False,
    )
```

```python
import jax
import jax.numpy as jnp
import numpy as np
from jax import lax
from jax.experimental import pallas as pl
from jax.experimental.pallas import tpu as pltpu
from jax.sharding import PartitionSpec as P

GX = 16
GY = 16
GZ = 8
NV = GX * GY * GZ
RANK = 768
COURANT = 0.1
SPACING = 0.5
COLLIDE = 0.5

CX = 16
NY = 16
NZ = 16
LAYER = NY * NZ
WIDTH = 128
GROUPS = NV // WIDTH
OFFSET = 3.0 / 16.0
BX = 4
BY = 4
LINE = BX * NZ


def tables():
    k = np.arange(NV)
    vx = ((k // (GY * GZ)) - 0.5 * (GX - 1)) * SPACING
    vy = ((k // GZ % GY) - 0.5 * (GY - 1)) * SPACING
    vz = ((k % GZ) - 0.5 * (GZ - 1)) * SPACING
    s = vx * vx + vy * vy + vz * vz
    w = np.exp(-0.5 * s)
    w = w / w.sum()
    sx, sy, sz = (w * vx * vx).sum(), (w * vy * vy).sum(), (w * vz * vz).sum()
    m2, m4 = (w * s).sum(), (w * s * s).sum()
    basis = np.stack([np.ones(NV), vx, vy, vz, s - OFFSET])
    q = np.zeros((5, 5))
    scale = 1.0 / (m4 - m2 * m2)
    thermal = np.zeros(5)
    thermal[0] = (OFFSET - m2) * scale
    thermal[4] = scale
    q[:, 4] = thermal
    q[:, 0] = (OFFSET - m2) * thermal
    q[0, 0] += 1.0
    q[1, 1], q[2, 2], q[3, 3] = 1.0 / sx, 1.0 / sy, 1.0 / sz
    project = np.zeros((NV, 128))
    project[:, :5] = basis.T
    mix = np.zeros((128, 128))
    expand = np.zeros((128, NV))
    for part in range(3):
        mix[:5, 8 * part : 8 * part + 5] = q
        expand[8 * part : 8 * part + 5] = basis
    return (
        project.astype(jnp.bfloat16),
        mix.astype(np.float32),
        expand.astype(jnp.bfloat16),
        w.reshape(1, NV).astype(np.float32),
    )


def minmod_half(a, b):
    return 0.5 * (jnp.maximum(jnp.minimum(a, b), 0.0) + jnp.minimum(jnp.maximum(a, b), 0.0))


C_VMEM = 12 << 20
HBM = pltpu.HBM
VMEM = pltpu.VMEM
SMEM = pltpu.SMEM
DMA = pltpu.SemaphoreType.DMA


def call(kernel, name, operands, outs, scratch=(), flops=0, limit=8 << 20):
    shapes = [jax.ShapeDtypeStruct(shape, dtype) for shape, dtype, _ in outs]
    arrays = [o for o, _ in operands]
    moved = sum(o.size * o.dtype.itemsize for o in arrays + shapes)
    return pl.pallas_call(
        kernel,
        out_shape=tuple(shapes),
        in_specs=[pl.BlockSpec(memory_space=space) for _, space in operands],
        out_specs=tuple(pl.BlockSpec(memory_space=space) for _, _, space in outs),
        scratch_shapes=list(scratch),
        compiler_params=pltpu.CompilerParams(vmem_limit_bytes=limit),
        cost_estimate=pl.CostEstimate(flops=flops, bytes_accessed=moved, transcendentals=0),
        name=name,
    )(*arrays)


def speeds_yz():
    lane = lax.broadcasted_iota(jnp.int32, (NZ, WIDTH), 1)
    along_y = (lane >> 3).astype(jnp.float32) - 0.5 * (GY - 1)
    along_z = (lane & (GZ - 1)).astype(jnp.float32) - 0.5 * (GZ - 1)
    return along_y * (SPACING * COURANT), along_z * (SPACING * COURANT)


def flux_change_z(f, uz, z_up):
    dz = pltpu.roll(f, NZ - 1, 0) - f
    slope = minmod_half(pltpu.roll(dz, 1, 0), dz)
    down = pltpu.roll(f - slope, NZ - 1, 0)
    flux = jnp.where(z_up, f + slope, down)
    return uz * (flux - pltpu.roll(flux, 1, 0))


def edges(before, here, after):
    slope = minmod_half(here - before, after - here)
    return here + slope, here - slope


def upwind_face(before, here, after):
    return here + minmod_half(here - before, after - here)


def first_halo_kernel(vel_ref, space_ref, dist_ref, behind_ref, ahead_ref):
    forward = vel_ref[0] >= GROUPS // 2
    start = jnp.where(forward, CX - 2, 0)
    for i in range(2):
        behind_ref[i] = dist_ref[start + i].astype(jnp.bfloat16)
    ahead_ref[0] = dist_ref[jnp.where(forward, 0, CX - 1)].astype(jnp.bfloat16)


def quarters(rank, space):
    high, core = (rank // 8 + space) % 2, rank % 2
    return 2 * high + (core + high) % 2, rank // 2 % 4


def kinetic_cells_of(step, vel_ref, space_ref, count_ref, cells_ref):
    x_quarter, y_quarter = quarters(vel_ref[0], space_ref[0])
    count = count_ref[step, space_ref[0]]
    shape = (LAYER, WIDTH)
    slot = lax.broadcasted_iota(jnp.int32, shape, 0)
    cell = (
        (BX * x_quarter + (slot >> 6)) * LAYER + BY * NZ * y_quarter + (slot & (LINE - 1))
    )
    lane = lax.broadcasted_iota(jnp.int32, (1, WIDTH), 1)
    found = jnp.zeros(shape, jnp.float32)
    for i in range(CX * LAYER // WIDTH):
        part = cells_ref[step : step + 1, WIDTH * i : WIDTH * (i + 1)]
        part = jnp.where(lane + WIDTH * i < count, part, -1)
        found = jnp.where(cell == part, 1.0, found)
    return jnp.broadcast_to(jnp.max(found, axis=1, keepdims=True), shape)


def rates_of(vel_ref, space_ref, rate_ref):
    x_quarter, y_quarter = quarters(vel_ref[0], space_ref[0])
    diagonal = lax.broadcasted_iota(jnp.int32, (NZ, NZ), 0) == lax.broadcasted_iota(
        jnp.int32, (NZ, NZ), 1
    )
    columns = []
    for x in range(BX):
        for y in range(BY):
            line = rate_ref[BX * x_quarter + x, pl.ds(BY * y_quarter + y, 1), :]
            column = jnp.sum(jnp.where(diagonal, line, 0.0), axis=1, keepdims=True)
            columns.append(jnp.broadcast_to(column, (NZ, WIDTH)))
    return jnp.concatenate(columns, axis=0)


def first_yz_kernel(f_ref, part_ref):
    uy, uz = speeds_yz()
    y_up = uy > 0.0
    z_up = uz > 0.0

    def layer(x, carry):
        def at(y):
            return f_ref[x, y % NY]

        up, _ = edges(at(-2), at(-1), at(0))
        next_up, next_down = edges(at(-1), at(0), at(1))
        flux_before = jnp.where(y_up, up, next_down)
        for y in range(NY):
            up = next_up
            next_up, next_down = edges(at(y), at(y + 1), at(y + 2))
            flux = jnp.where(y_up, up, next_down)
            here = at(y)
            part_ref[x, y] = here - uy * (flux - flux_before) - flux_change_z(here, uz, z_up)
            flux_before = flux
        return carry

    lax.fori_loop(0, CX, layer, 0)


def first_x_kernel(vel_ref, space_ref, f_ref, part_ref, behind_ref, ahead_ref, rows_ref):
    rank = vel_ref[0]
    forward = rank >= GROUPS // 2
    ux = jnp.abs(rank.astype(jnp.float32) - 0.5 * (GX - 1)) * (SPACING * COURANT)
    layers = [jnp.where(forward, k, CX - 1 - k) for k in range(CX)]
    starts = [(x % BX) * LINE for x in layers[:BX]]
    owners = []
    for k in range(4):
        quarter = jnp.where(forward, k, 3 - k)
        high = quarter // 2
        owners.append((high + space_ref[0]) % 2 * (GROUPS // 2) + (quarter + high) % 2)

    def line(quarter, y):
        inner = y * NZ
        y = quarter * BY + y

        def at(k):
            if k == -2:
                return behind_ref[jnp.where(forward, 0, 1), y].astype(jnp.float32)
            if k == -1:
                return behind_ref[jnp.where(forward, 1, 0), y].astype(jnp.float32)
            if k == CX:
                return ahead_ref[0, y].astype(jnp.float32)
            return f_ref[layers[k], y]

        face_before = upwind_face(at(-2), at(-1), at(0))
        for k in range(CX):
            face = upwind_face(at(k - 1), at(k), at(k + 1))
            result = part_ref[layers[k], y] - ux * (face - face_before)
            face_before = face
            start = pl.multiple_of(starts[k % BX] + inner, NZ)
            target = owners[k // BX] + quarter * 2
            rows_ref[target, pl.ds(start, NZ), :] = result.astype(jnp.bfloat16)

    def lines(quarter, carry):
        def one(y, inside):
            line(quarter, y)
            return inside

        lax.fori_loop(0, BY, one, 0)
        return carry

    lax.fori_loop(0, NY // BY, lines, 0)


def collide(rows, a_ref, b_ref, c_ref, project_ref, mix_ref, expand_ref, w_ref, hidden_ref):
    moments = jnp.dot(rows, project_ref[...], preferred_element_type=jnp.float32)
    for n in range(RANK // 256):
        cols = slice(256 * n, 256 * (n + 1))
        first = jnp.dot(rows, a_ref[:, cols], preferred_element_type=jnp.float32)
        second = jnp.dot(rows, b_ref[:, cols], preferred_element_type=jnp.float32)
        hidden_ref[:, cols] = (first * second).astype(jnp.bfloat16)
    return outcome(moments, c_ref, mix_ref, expand_ref, w_ref, hidden_ref)


def outcome(moments, c_ref, mix_ref, expand_ref, w_ref, hidden_ref):
    coeffs = jnp.dot(
        moments, mix_ref[...], precision=lax.Precision.HIGHEST, preferred_element_type=jnp.float32
    )
    lane = lax.broadcasted_iota(jnp.int32, coeffs.shape, 1)
    high = coeffs.astype(jnp.bfloat16).astype(jnp.float32)
    rest = coeffs - high
    middle = rest.astype(jnp.bfloat16).astype(jnp.float32)
    split = jnp.where(lane < 8, high, jnp.where(lane < 16, middle, rest - middle))
    split = split.astype(jnp.bfloat16)
    hidden = hidden_ref[...]
    for n in range(NV // 256):
        cols = slice(256 * n, 256 * (n + 1))
        collision = jnp.dot(hidden, c_ref[:, cols], preferred_element_type=jnp.float32)
        collision = collision.astype(jnp.bfloat16).astype(jnp.float32)
        poly = jnp.dot(split, expand_ref[:, cols], preferred_element_type=jnp.float32)
        equilibrium = poly * w_ref[:, cols]
        for half in range(2):
            part = slice(WIDTH * half, WIDTH * (half + 1))
            yield 2 * n + half, collision[:, part], equilibrium[:, part]


def first_collide_kernel(
    vel_ref, space_ref, count_ref, rows_ref, cells_ref, rate_ref, a_ref, b_ref, c_ref,
    project_ref, mix_ref, expand_ref, w_ref,
    f_ref, rates_ref, x_even_ref, x_odd_ref, y_even_ref, y_odd_ref, hidden_ref,
):
    rows = jnp.concatenate([rows_ref[g] for g in range(GROUPS)], axis=1)
    terms = collide(
        rows, a_ref, b_ref, c_ref, project_ref, mix_ref, expand_ref, w_ref, hidden_ref
    )
    kinetic = kinetic_cells_of(0, vel_ref, space_ref, count_ref, cells_ref) > 0.0
    rate = rates_of(vel_ref, space_ref, rate_ref)
    rates_ref[...] = rate
    half = GROUPS // 2
    x_quarter, y_quarter = quarters(vel_ref[0], space_ref[0])
    x_is_even, y_is_even = x_quarter % 2 == 0, y_quarter % 2 == 0

    def put(even_ref, odd_ref, is_even, where, up, down):
        even_ref[where] = jnp.where(is_even, up, down).astype(jnp.bfloat16)
        odd_ref[where] = jnp.where(is_even, down, up).astype(jnp.bfloat16)

    low_lane = lax.broadcasted_iota(jnp.int32, (NZ, WIDTH), 1) < WIDTH // 2
    for g, collision, equilibrium in terms:
        moved = rows_ref[g].astype(jnp.float32)
        change = jnp.where(kinetic, COLLIDE * collision, rate * (equilibrium - moved))
        result = moved + change
        f_ref[g] = result
        put(x_even_ref, x_odd_ref, x_is_even, g, result[3 * LINE :], result[:LINE])
        low = g - half
        if low >= 0:
            put(
                x_even_ref, x_odd_ref, x_is_even, GROUPS + low,
                result[2 * LINE : 3 * LINE], f_ref[low, LINE : 2 * LINE],
            )
        for x in range(BX):
            here = slice(NZ * x, NZ * (x + 1))
            first, second, third, fourth = (
                slice(LINE * x + NZ * y, LINE * x + NZ * (y + 1)) for y in range(BY)
            )
            put(y_even_ref, y_odd_ref, y_is_even, (g, here), result[fourth], result[first])
            if low >= 0:
                put(
                    y_even_ref, y_odd_ref, y_is_even, (GROUPS + low, here),
                    jnp.where(
                        low_lane, pltpu.roll(f_ref[low, third], WIDTH // 2, 1), result[third]
                    ),
                    jnp.where(
                        low_lane, f_ref[low, second], pltpu.roll(result[second], WIDTH // 2, 1)
                    ),
                )


def second_z_kernel(vel_ref, space_ref, count_ref, f_ref, cells_ref, part_ref, mask_ref):
    mask_ref[...] = kinetic_cells_of(1, vel_ref, space_ref, count_ref, cells_ref)
    _, uz = speeds_yz()
    z_up = uz > 0.0

    half = GROUPS // 2

    def group(g, upward):
        ux = jnp.abs(g.astype(jnp.float32) - 0.5 * (GX - 1)) * (SPACING * COURANT)
        for y in range(BY):
            places = []
            for k in range(BX):
                x = k if upward else BX - 1 - k
                places.append(slice(LINE * x + NZ * y, LINE * x + NZ * (y + 1)))
            line = [f_ref[g, here] for here in places]
            face_1 = ux * upwind_face(line[0], line[1], line[2])
            face_2 = ux * upwind_face(line[1], line[2], line[3])
            inner = [None, face_1, face_2 - face_1, -face_2]
            for here, f, change in zip(places, line, inner, strict=True):
                part = f - flux_change_z(f, uz, z_up)
                part_ref[g, here] = part if change is None else part - change

    def downwards(g, carry):
        group(g, False)
        return carry

    def upwards(g, carry):
        group(g, True)
        return carry

    lax.fori_loop(0, half, downwards, 0)
    lax.fori_loop(half, GROUPS, upwards, 0)


def second_kernel(
    vel_ref, space_ref, f_ref, part_ref, x_odd_ref, y_even_ref, y_odd_ref, x_even_ref,
    mask_ref, rates_ref, a_ref, b_ref, c_ref, project_ref, mix_ref, expand_ref, w_ref,
    out_ref, hidden_ref, moved_ref, first_ref, second_ref,
):
    uy, _ = speeds_yz()
    y_up = uy > 0.0
    half = GROUPS // 2

    x_quarter, y_quarter = quarters(vel_ref[0], space_ref[0])
    x_is_even, y_is_even = x_quarter % 2 == 0, y_quarter % 2 == 0

    def arrived(even_ref, odd_ref, is_even, g, i):
        even = even_ref[g, NZ * i : NZ * (i + 1)].astype(jnp.float32)
        odd = odd_ref[g, NZ * i : NZ * (i + 1)].astype(jnp.float32)
        return jnp.where(is_even, odd, even), jnp.where(is_even, even, odd)

    def group(pair, upward):
        g = pair + half if upward else pair
        extra = pair + GROUPS
        partial = {}
        ux = abs(g - 0.5 * (GX - 1)) * (SPACING * COURANT)
        for y in range(BY):
            here_x = (x_even_ref, x_odd_ref, x_is_even)
            behind, ahead = arrived(*here_x, g, y)[:: 1 if upward else -1]
            line = [arrived(*here_x, extra, y)[0 if upward else 1], behind]
            for k in range(BX):
                x = k if upward else BX - 1 - k
                line.append(f_ref[g, LINE * x + NZ * y : LINE * x + NZ * (y + 1)])
            line.append(ahead)

            def at_x(k):
                return line[k + 2]

            face_0 = upwind_face(at_x(-1), at_x(0), at_x(1))
            outer = [
                face_0 - upwind_face(at_x(-2), at_x(-1), at_x(0)), -face_0, None,
                upwind_face(at_x(2), at_x(3), at_x(4)),
            ]
            for k in range(BX):
                x = k if upward else BX - 1 - k
                here = slice(LINE * x + NZ * y, LINE * x + NZ * (y + 1))
                part = part_ref[g, here]
                partial[x, y] = part if outer[k] is None else part - ux * outer[k]
        for x in range(BX):
            here_y = (y_even_ref, y_odd_ref, y_is_even)
            below, above = arrived(*here_y, g, x)
            below_2, above_2 = arrived(*here_y, extra, x)
            if upward:
                above_2 = pltpu.roll(above_2, WIDTH // 2, 1)
            else:
                below_2 = pltpu.roll(below_2, WIDTH // 2, 1)
            column = [below_2, below]
            for y in range(BY):
                column.append(f_ref[g, LINE * x + NZ * y : LINE * x + NZ * (y + 1)])
            column += [above, above_2]

            def at_y(y):
                return column[y + 2]

            up, _ = edges(at_y(-2), at_y(-1), at_y(0))
            next_up, next_down = edges(at_y(-1), at_y(0), at_y(1))
            flux_before = jnp.where(y_up, up, next_down)
            for y in range(BY):
                up = next_up
                next_up, next_down = edges(at_y(y), at_y(y + 1), at_y(y + 2))
                flux = jnp.where(y_up, up, next_down)
                here = slice(LINE * x + NZ * y, LINE * x + NZ * (y + 1))
                moved_ref[g, here] = partial[x, y] - uy * (flux - flux_before)
                flux_before = flux

    moments = jnp.zeros((LAYER, WIDTH), jnp.float32)
    chunk = 1
    for pair in range(0, half, chunk):
        groups = []
        for upward in (False, True):
            for i in range(chunk):
                group(pair + i, upward)
                groups.append(pair + i + (half if upward else 0))
        rows = jnp.concatenate([moved_ref[g].astype(jnp.bfloat16) for g in groups], axis=1)
        spans = [
            slice(WIDTH * g, WIDTH * (g + chunk)) for g in (pair, pair + half)
        ]

        def times(ref, cols):
            right = jnp.concatenate([ref[span, cols] for span in spans], axis=0)
            return jnp.dot(rows, right, preferred_element_type=jnp.float32)

        moments += times(project_ref, slice(0, WIDTH))
        for n in range(RANK // 256):
            cols = slice(256 * n, 256 * (n + 1))
            first, second = times(a_ref, cols), times(b_ref, cols)
            if pair:
                first += first_ref[:, cols]
                second += second_ref[:, cols]
            if pair + chunk < half:
                first_ref[:, cols] = first
                second_ref[:, cols] = second
            else:
                hidden_ref[:, cols] = (first * second).astype(jnp.bfloat16)
    rate = rates_ref[...]
    kinetic = mask_ref[...] > 0.0
    for g, collision, equilibrium in outcome(
        moments, c_ref, mix_ref, expand_ref, w_ref, hidden_ref
    ):
        moved = moved_ref[g]
        change = jnp.where(kinetic, COLLIDE * collision, rate * (equilibrium - moved))
        out_ref[g] = (moved + change).astype(jnp.bfloat16)


def place_kernel(space_ref, in_ref, out_hbm, out_ref, sems):
    stores = []
    for quarter in range(4):
        high = quarter // 2
        core = (quarter % 2) ^ high
        first = (high + space_ref[0]) % 2 * (GROUPS // 2) + core
        for x in range(BX):
            for y_quarter in range(4):
                for y in range(BY):
                    c = LINE * x + NZ * y
                    out_ref[BX * quarter + x, BY * y_quarter + y] = in_ref[
                        first + y_quarter * 2, c : c + NZ
                    ].astype(jnp.float32)
        part = slice(BX * quarter, BX * (quarter + 1))
        stores.append(pltpu.make_async_copy(out_ref.at[part], out_hbm.at[part], sems.at[quarter]))
        stores[-1].start()
    for store in stores:
        store.wait()


def device_of(space, high, x, core):
    return (space * 2 + high) * 8 + x * 2 + core


def holder_of(space, quarter, x):
    high = quarter // 2
    return device_of(space, (high + space) % 2, x, (quarter + high) % 2)


def steps_of(slabs):
    upwind, downwind = [], []
    x_even, x_odd, y_even, y_odd = [], [], [], []
    for space in range(slabs):
        before, after = (space - 1) % slabs, (space + 1) % slabs
        for quarter in range(4):
            next_x = holder_place(space, quarter + 1, slabs)
            last_x = holder_place(space, quarter - 1, slabs)
            for x in range(4):
                me = holder_of(space, quarter, x)
                rank = me % GROUPS
                forward = rank >= GROUPS // 2
                upwind.append((me, (after if forward else before) * GROUPS + rank))
                downwind.append((me, (before if forward else after) * GROUPS + rank))
                up, down = holder_of(*next_x, x), holder_of(*last_x, x)
                x_even.append((me, down if quarter % 2 else up))
                x_odd.append((me, up if quarter % 2 else down))
                up, down = (holder_of(space, quarter, (x + d) % 4) for d in (1, -1))
                y_even.append((me, down if x % 2 else up))
                y_odd.append((me, up if x % 2 else down))
    return upwind, downwind, x_even, x_odd, y_even, y_odd


def holder_place(space, quarter, slabs):
    return (space + quarter // 4) % slabs, quarter % 4


def body(dist, relax_rate, kinetic_cells, kinetic_count, map_a, map_b, map_c):
    vel = (lax.axis_index("vel").astype(jnp.int32).reshape(1), SMEM)
    space = (lax.axis_index("space").astype(jnp.int32).reshape(1), SMEM)
    both = ("space", "vel")
    upwind, downwind, *pairs = steps_of(lax.axis_size("space"))
    project, mix, expand, w = tables()
    consts = (jnp.asarray(project), jnp.asarray(mix), jnp.asarray(expand), jnp.asarray(w))
    layers = (NY, NZ, WIDTH)
    behind, ahead = call(
        first_halo_kernel, "first_halo", (vel, space, (dist, VMEM)),
        (((2,) + layers, jnp.bfloat16, VMEM), ((1,) + layers, jnp.bfloat16, VMEM)),
    )
    behind = lax.ppermute(behind, both, upwind)
    ahead = lax.ppermute(ahead, both, downwind)

    state = ((CX,) + layers, jnp.float32, VMEM)
    wide = (GROUPS, LAYER, WIDTH)
    halo = (GROUPS + GROUPS // 2, LINE, WIDTH)
    half = jnp.bfloat16
    hidden = VMEM((LAYER, RANK), half)

    (part,) = call(first_yz_kernel, "first_yz", ((dist, VMEM),), (state,), flops=12_000_000)
    (rows,) = call(
        first_x_kernel, "first_x", (vel, space) + tuple((o, VMEM) for o in (dist, part, behind, ahead)),
        ((wide, half, VMEM),), flops=6_000_000,
    )
    gathered = lax.all_to_all(rows, "vel", split_axis=0, concat_axis=0, tiled=True)
    facts = (vel, space, (kinetic_count, SMEM))
    lanes = ((LAYER, WIDTH), jnp.float32, VMEM)
    held = tuple((o, VMEM) for o in (map_a, map_b, map_c) + consts)
    f, rates, *halos = call(
        first_collide_kernel, "first_collide",
        facts + ((gathered, VMEM), (kinetic_cells, VMEM), (relax_rate, VMEM)) + held,
        ((wide, jnp.float32, VMEM), lanes) + ((halo, half, VMEM),) * 4,
        scratch=(hidden,), flops=2_500_000_000, limit=C_VMEM,
    )
    x_even, x_odd, y_even, y_odd = (
        lax.ppermute(o, both, p) for o, p in zip(halos, pairs, strict=True)
    )
    part, mask = call(
        second_z_kernel, "second_z", facts + ((f, VMEM), (kinetic_cells, VMEM)),
        ((wide, jnp.float32, VMEM), lanes), flops=6_000_000,
    )
    sums = VMEM((LAYER, RANK), jnp.float32)
    (result,) = call(
        second_kernel, "second_xy_collide",
        (vel, space)
        + tuple((o, VMEM) for o in (f, part, x_odd, y_even, y_odd, x_even, mask, rates)) + held,
        ((wide, half, VMEM),), scratch=(hidden, VMEM(wide, jnp.float32), sums, sums),
        flops=2_500_000_000, limit=C_VMEM,
    )
    pieces = lax.all_to_all(result, "vel", split_axis=0, concat_axis=0, tiled=True)
    (out,) = call(
        place_kernel, "place", (space, (pieces, VMEM)), (((CX,) + layers, jnp.float32, HBM),),
        scratch=(VMEM((CX,) + layers, jnp.float32), DMA((4,))),
    )
    return out


def solution(mesh):
    return jax.shard_map(
        body,
        mesh=mesh,
        in_specs=(
            P("space", None, None, "vel"),
            P("space", None, None),
            P(None, "space"),
            P(),
            P(),
            P(),
            P(),
        ),
        out_specs=P("space", None, None, "vel"),
        check_vma=False,
    )
```
